32 devices in a mesh: dp: 8 (over z, x), tensor: 4 (over y, core).
Axes of the slice: x: 2, y: 2, z: 4, core: 2. Of those that a mesh axis runs over, the one named last changes fastest.
Arguments:
- queries: bfloat16 [512, 4, 64, 128], P('dp', None, 'tensor'), may hold values from -9 to 9
- draft_keys: bfloat16 [512, 4, 8, 128], P('dp', None, 'tensor'), may hold values from -6 to 6
- draft_values: bfloat16 [512, 4, 8, 128], P('dp', None, 'tensor'), may hold values from -6 to 6
- suffix_keys: bfloat16 [512, 32, 8, 128], P('dp', None, 'tensor'), may hold values from -6 to 6
- suffix_values: bfloat16 [512, 32, 8, 128], P('dp', None, 'tensor'), may hold values from -6 to 6
- suffix_len: int32 [512], P('dp'), may hold values from 1 to 32, as said below
- prefix_keys: bfloat16 [8, 4096, 8, 128], P('dp', None, 'tensor'), may hold values from -6 to 6
- prefix_values: bfloat16 [8, 4096, 8, 128], P('dp', None, 'tensor'), may hold values from -6 to 6
- row_prefix: int32 [512, 1], P('dp'), may hold values from 0 to 7; in each aligned block of 64 rows (0 to 63, 64 to 127, ...) at most 16 rows name the same one
- prefix_slot: int32 [8], replicated, may hold values from 0 to 7, each once
- out_weight: bfloat16 [8192, 4096], P('tensor'), may hold values from -0.09375 to 0.09375
Outputs:
- projected: bfloat16 [512, 4, 4096], P('dp', None, 'tensor')
The draws below stay inside these ranges and needn't reach their ends.
Inputs may be any that keep to these rules, and one draw needn't show every extreme that they name: `row_prefix`: the rows of one device name any one prefix at most 16 times, a bound that some block reaches. `prefix_slot`: A permutation. `suffix_len`: the rows of every device include one of length 32.
All inputs are finite; a program needn't handle non-finite values.
Results may differ from the reference program's by a relative error of at most 0.014.
Values may be sent and summed in bfloat16 or wider, within the bound.
No kernel may reach another device: no remote copies, remote signals or barrier semaphores. Data moves between devices by JAX's collectives and lax.ppermute only.
A program may use at most 128 MiB of HBM per device.

```python
import math
import jax
import jax.numpy as jnp
import numpy as np
from jax import lax

HQ = 64
KVH = 8
HD = 128
DOUT = 4096
DRAFT = 4
ROWS_DEV = 64
PREFIX_LEN = 4096
SUF = 32
ROWS = 512
NPREF = 8
CAP = 16
N_TENSOR = 4


def draw_queries(key, part):
    key = jax.random.fold_in(key, 1)
    key_one = jax.random.fold_in(key, 0)
    shape = (ROWS, DRAFT, HQ, HD)
    result = jnp.clip(jax.random.normal(key_one, shape), -6.0, 6.0)
    return result.astype(jnp.bfloat16)


def draw_prefix_keys(key, part):
    key = jax.random.fold_in(key, 2)
    shape = (NPREF, PREFIX_LEN, KVH, HD)
    result = jnp.clip(jax.random.normal(key, shape), -6.0, 6.0)
    return result.astype(jnp.bfloat16)


def draw_suffix_len(key, part):
    key = jax.random.fold_in(key, 3)
    key_one, key_two = jax.random.split(key)
    lengths = jax.random.randint(key_one, (NPREF, ROWS_DEV), 1, SUF + 1)
    picked = jax.random.randint(key_two, (NPREF, 1), 0, ROWS_DEV)
    lengths = jnp.where(jnp.arange(ROWS_DEV)[None, :] == picked, SUF, lengths)
    return lengths.reshape(ROWS).astype(jnp.int32)


def draw_draft_keys(key, part):
    key = jax.random.fold_in(key, 4)
    result = drawn_keys_from(key, (ROWS, DRAFT, KVH, HD))
    return result.astype(jnp.bfloat16)


def draw_suffix_keys(key, part):
    key = jax.random.fold_in(key, 5)
    result = drawn_keys_from(key, (ROWS, SUF, KVH, HD))
    return result.astype(jnp.bfloat16)


def drawn_keys_from(key, shape):
    result = jnp.clip(jax.random.normal(key, shape), -6.0, 6.0)
    return result


def with_spikes(drawn, stream_key, source, target, blocks, factor):
    owner, partner = [(jnp.arange(drawn.shape[axis_at]) // (drawn.shape[axis_at] // blocks)).reshape([-1 if axis == axis_at else 1 for axis in range(drawn.ndim)]) for axis_at in (source, target)]
    chosen = jax.random.permutation(stream_key, blocks)[partner]
    strong = (owner == chosen) | (owner == (partner + blocks // 2) % blocks)
    return jnp.where(strong, factor * drawn, drawn)


def steps_of(own_key, extent, shards, smallest, largest):
    level = 1.0
    for dim, blocks in shards:
        heights = jax.random.uniform(jax.random.fold_in(jax.random.fold_in(own_key, 6), dim), (blocks,), jnp.float32, smallest / len(shards), largest / len(shards))
        level = level * jnp.repeat(jnp.exp(heights), extent[dim] // blocks).reshape((-1,) + (1,) * (len(extent) - 1 - dim))
    return level


def routed_block(key, own, number, rows, number_of, top, bound, lean):
    order = jax.random.permutation(key, number_of)
    crowded, common = load_shares(number_of, rows * top, bound, lean, True), load_shares(number_of, rows * top, bound, lean, False)
    places = jnp.arange(number_of)

    def named(tallies, turn):
        used = int((tallies > 0).sum())
        fixed = max(1, used // 4)
        moved = fixed + (places - fixed + turn * (used - fixed)) % max(1, number_of - fixed)
        return jnp.zeros((number_of,), jnp.int32).at[order[jnp.where(places < fixed, places, moved)]].set(jnp.asarray(tallies, jnp.int32))

    tallies = jnp.where(number % 4 == 0, named(crowded, number // 4), named(common, number - number // 4 - 1))
    mixed = jax.random.permutation(jax.random.fold_in(own, 3), number_of)
    giver, receiver = mixed[0:number_of // 2 * 2:2], mixed[1:number_of // 2 * 2:2]
    margin = jnp.minimum(tallies[giver] - 1, bound - tallies[receiver]) // 2
    margin = jnp.where((giver == order[0]) | (receiver == order[0]) | (tallies[receiver] == 0), 0, jnp.maximum(margin, 0))
    moved = jax.random.randint(jax.random.fold_in(own, 4), (number_of // 2,), 0, 1 << 20) % (margin + 1)
    tallies = tallies.at[giver].add(-moved).at[receiver].add(moved)
    labels = jnp.searchsorted(jnp.cumsum(tallies), jnp.arange(rows * top), side="right").astype(jnp.int32)
    table = labels.reshape(top, rows).T
    table = table[jax.random.permutation(jax.random.fold_in(own, 1), rows)]
    turn = jax.random.randint(jax.random.fold_in(own, 2), (rows, 1), 0, top)
    return jnp.take_along_axis(table, (jnp.arange(top)[None, :] + turn) % top, axis=1)


def load_shares(amount, total, reach, lean, full):
    portions = [(1 << 20) // math.isqrt(grade ** lean) + 1 for grade in range(1, amount + 1)]
    largest = reach if full else min(reach, max(-(-total // amount), total * portions[0] // sum(portions)))
    least = 1 if total - largest >= amount - 1 else 0
    holding, rest = [largest] + [least] * (amount - 1), total - largest - least * (amount - 1)
    while rest > 0:
        candidates = [i for i in range(1, amount) if holding[i] < largest] or [i for i in range(1, amount) if holding[i] < reach]
        pool, budget = sum([portions[i] for i in candidates]), rest
        for i in candidates:
            addition = min(reach - holding[i], max(1, budget * portions[i] // pool), rest)
            holding[i] = holding[i] + addition
            rest = rest - addition
    return np.array(holding)


def gaussian(stream_key, shape, deviation, bound, shards=(), held_as=jnp.bfloat16):
    values = deviation * jax.random.normal(stream_key, shape, jnp.float32)
    if shards:
        values = values * steps_of(stream_key, shape, shards, -0.22, 0.18)
    return jnp.clip(values, -bound, bound).astype(held_as)


def gaussian_with(key, shape, spread, limit, cuts, heavy, kind=jnp.bfloat16):
    values = spread * jax.random.normal(key, shape, jnp.float32)
    if cuts:
        values = values * steps_of(key, shape, cuts, -0.22, 0.18)
    return jnp.clip(with_spikes(values, jax.random.fold_in(key, 3), *heavy), -limit, limit).astype(kind)


def setup_inputs(seed: int = 0) -> dict:
    seeds = jax.random.split(jax.random.key(seed), 12)
    queries = draw_queries(jax.random.fold_in(seeds[11], 71), 0)
    draft_keys = draw_draft_keys(jax.random.fold_in(seeds[11], 71), 0)
    draft_values = gaussian(seeds[2], (ROWS, DRAFT, KVH, HD), 1.0, 6.0, ((0, 8), (2, 4)))
    suffix_keys = draw_suffix_keys(jax.random.fold_in(seeds[11], 71), 0)
    suffix_values = gaussian(seeds[4], (ROWS, SUF, KVH, HD), 1.0, 6.0, ((0, 8), (2, 4)))
    suffix_len = draw_suffix_len(jax.random.fold_in(seeds[11], 71), 0)
    prefix_keys = draw_prefix_keys(jax.random.fold_in(seeds[11], 71), 0)
    prefix_values = gaussian(seeds[7], (NPREF, PREFIX_LEN, KVH, HD), 1.0, 6.0, ((0, 8), (2, 4)))
    row_prefix_keys = jax.random.split(jax.random.fold_in(seeds[8], 1), ROWS // ROWS_DEV)
    row_prefix_turns = jax.random.permutation(jax.random.fold_in(seeds[8], 3), ROWS // ROWS_DEV)
    row_prefix = jax.vmap(lambda own, number: routed_block(jax.random.fold_in(seeds[8], 2), own, number, ROWS_DEV, NPREF, 1, CAP, 2))(row_prefix_keys, row_prefix_turns).reshape((ROWS, 1))
    prefix_slot = jax.random.permutation(seeds[9], NPREF).astype(jnp.int32)
    out_weight = gaussian_with(seeds[10], (HQ * HD, DOUT), (HQ * HD) ** -0.5, 0.09375, ((0, 4),), (0, 1, 4, 2.0))
    return {"queries": queries, "draft_keys": draft_keys, "draft_values": draft_values, "suffix_keys": suffix_keys, "suffix_values": suffix_values, "suffix_len": suffix_len, "prefix_keys": prefix_keys, "prefix_values": prefix_values, "row_prefix": row_prefix, "prefix_slot": prefix_slot, "out_weight": out_weight}


def reference(queries, draft_keys, draft_values, suffix_keys, suffix_values, suffix_len, prefix_keys, prefix_values, row_prefix, prefix_slot, out_weight):
    group_size = HQ // KVH
    score_scale = HD ** -0.5
    holder = prefix_slot[row_prefix[:, 0]].astype(jnp.int32)
    key_count = PREFIX_LEN + SUF + DRAFT
    position = jnp.arange(key_count, dtype=jnp.int32)
    draft_pos = jnp.arange(DRAFT, dtype=jnp.int32)

    def one_row(row_items):
        query_row, draft_key, draft_value, suffix_key, suffix_value, length, holder_row = row_items
        prefix_key = lax.dynamic_index_in_dim(prefix_keys, holder_row, 0, keepdims=False)
        prefix_value = lax.dynamic_index_in_dim(prefix_values, holder_row, 0, keepdims=False)
        all_keys = jnp.concatenate([prefix_key, suffix_key, draft_key], 0).astype(jnp.float32)
        all_values = jnp.concatenate([prefix_value, suffix_value, draft_value], 0).astype(jnp.float32)
        in_prefix = position[None, :] < PREFIX_LEN
        in_suffix = (position[None, :] >= PREFIX_LEN) & (position[None, :] < PREFIX_LEN + length)
        in_draft = (position[None, :] >= PREFIX_LEN + SUF) & (position[None, :] - PREFIX_LEN - SUF <= draft_pos[:, None])
        visible = in_prefix | in_suffix | in_draft
        query_grid = query_row.reshape(DRAFT, KVH, group_size, HD).astype(jnp.float32)
        scores = jnp.einsum('tagd,jad->tagj', query_grid, all_keys) * score_scale
        visible_mask = visible[:, None, None, :]
        scores = jnp.where(visible_mask, scores, jnp.float32(-1e30))
        running_max = jnp.max(scores, axis=-1, keepdims=True)
        exponent = jnp.where(visible_mask, jnp.exp(scores - running_max), jnp.float32(0.0))
        denominator = jnp.sum(exponent, axis=-1)
        rounded = lax.optimization_barrier(exponent.astype(jnp.bfloat16)).astype(jnp.float32)
        result = jnp.einsum('tagj,jad->tagd', rounded, all_values) / denominator[..., None]
        return result.reshape(DRAFT, HQ * HD).astype(jnp.bfloat16)

    batch_rows = math.gcd(ROWS, 16)
    batches = ROWS // batch_rows

    def regroup(array):
        return array.reshape((batches, batch_rows) + array.shape[1:])

    attention = lax.map(jax.vmap(one_row), (regroup(queries), regroup(draft_keys), regroup(draft_values), regroup(suffix_keys), regroup(suffix_values), regroup(suffix_len), regroup(holder)))
    flat_rows = attention.reshape(ROWS * DRAFT, HQ * HD)
    group_width = HQ * HD // N_TENSOR
    summed = jnp.zeros((ROWS * DRAFT, DOUT), jnp.float32)
    for group_index in range(N_TENSOR):
        columns = flat_rows[:, group_index * group_width:(group_index + 1) * group_width]
        rows_w = out_weight[group_index * group_width:(group_index + 1) * group_width]
        partial_value = jnp.dot(columns, rows_w, preferred_element_type=jnp.float32)
        summed = summed + lax.optimization_barrier(partial_value.astype(jnp.bfloat16)).astype(jnp.float32)
    return summed.astype(jnp.bfloat16).reshape(ROWS, DRAFT, DOUT)
```

```python
import functools
import math

import jax
import jax.numpy as jnp
from jax import lax
from jax.experimental import pallas as pl
from jax.experimental.pallas import tpu as pltpu
from jax.sharding import PartitionSpec as P

BF = jnp.bfloat16
F32 = jnp.float32
EXTRA = 16
VMEM = 56 * 1024 * 1024
LIMIT = 1e30


def params():
    return pltpu.CompilerParams(vmem_limit_bytes=VMEM)


def route(row_prefix, prefix_slot, peers, capacity):
    rows = row_prefix.shape[0]
    prefixes = prefix_slot.shape[0]
    name = row_prefix[:, 0]
    row = jnp.arange(rows, dtype=jnp.int32)
    owner = jnp.sum(
        jnp.where(
            row_prefix == jnp.arange(prefixes, dtype=jnp.int32)[None, :], prefix_slot[None, :], 0
        ),
        axis=1,
    )
    same = (name[:, None] == name[None, :]) & (row[None, :] < row[:, None])
    rank = jnp.sum(same.astype(jnp.int32), axis=1)
    target = owner * capacity + rank
    slots = jnp.arange(peers * capacity, dtype=jnp.int32)
    slot_row = jnp.sum(jnp.where(target[None, :] == slots[:, None], row[None, :], 0), axis=1)
    key = rank * rows + row
    place = jnp.sum((key[None, :] < key[:, None]).astype(jnp.int32), axis=1)
    at = place[None, :] == row[:, None]
    order = jnp.sum(jnp.where(at, row[None, :], 0), axis=1)
    order_target = jnp.sum(jnp.where(at, target[None, :], 0), axis=1)
    return slot_row, place, order, order_target


def pack_kernel(peers, capacity, held, first, heads, slot_row, q_ref, *outs):
    draft, group = q_ref.shape[1], q_ref.shape[2] // heads
    per = draft * group

    def one_peer(peer, _):
        for k in range(held):
            row = slot_row[peer * capacity + first + k]
            x = q_ref[row].astype(F32)
            for a in range(heads):
                part = x[:, a * group : (a + 1) * group, :].reshape(per, x.shape[-1])
                outs[a][peer, k * per : (k + 1) * per, :] = part.astype(BF)
        return 0

    lax.fori_loop(0, peers, one_peer, 0)


def pack(queries, slot_row, peers, capacity, held, first, heads):
    draft, query_heads, dim = queries.shape[1:]
    per = draft * query_heads // heads
    shape = jax.ShapeDtypeStruct((peers, held * per, dim), BF)
    return pl.pallas_call(
        functools.partial(pack_kernel, peers, capacity, held, first, heads),
        out_shape=[shape] * heads,
        grid_spec=pltpu.PrefetchScalarGridSpec(
            num_scalar_prefetch=1,
            grid=(1,),
            in_specs=[pl.BlockSpec(queries.shape, lambda i, s: (0, 0, 0, 0))],
            out_specs=[pl.BlockSpec(shape.shape, lambda i, s: (0, 0, 0))] * heads,
        ),
        compiler_params=params(),
        cost_estimate=pl.CostEstimate(flops=0, bytes_accessed=4 << 20, transcendentals=0),
        name="pack_queries",
    )(slot_row, queries)


def attend_kernel(per, block, q_ref, k_ref, v_ref, o_ref, acc_ref):
    tile_peers, peer_rows, dim = q_ref.shape
    rows = tile_peers * peer_rows
    keys = k_ref.shape[1]
    scale = dim**-0.5 * math.log2(math.e)
    q = q_ref[...].reshape(rows, dim)
    ones = jnp.ones((block, dim), BF)

    def scores(j):
        part = k_ref[:, pl.ds(j * block, block)]
        return jnp.dot(q, part, preferred_element_type=F32)

    def values(j):
        return jnp.concatenate([v_ref[pl.ds(j * block, block), :], ones], axis=1)

    def finish(shift):
        total = acc_ref[...]
        den = total[:, dim:]
        out = (total[:, :dim] / den).astype(BF)
        o_ref[:, :peer_rows, :] = out.reshape(tile_peers, peer_rows, dim)
        log_sum = shift + jnp.log2(den)
        high = log_sum.astype(BF).astype(F32)
        rest = log_sum - high
        mid = rest.astype(BF).astype(F32)
        low = rest - mid
        lane = lax.broadcasted_iota(jnp.int32, (rows, dim), 1)
        row = lax.broadcasted_iota(jnp.int32, (rows, dim), 0)
        third = lane // per
        term = jnp.where(third == 0, high, jnp.where(third == 1, mid, low))
        term = jnp.where((lane % per == row % per) & (third < 3), term, 0.0)
        held = peer_rows // per
        slot = lax.broadcasted_iota(jnp.int32, (tile_peers * EXTRA, rows), 0)
        source = lax.broadcasted_iota(jnp.int32, (tile_peers * EXTRA, rows), 1) // per
        pick = (source // held == slot // EXTRA) & (source % held == slot % EXTRA)
        logs = jnp.dot(
            jnp.where(pick, 1.0, 0.0).astype(BF), term.astype(BF), preferred_element_type=F32
        )
        o_ref[:, peer_rows:, :] = logs.astype(BF).reshape(tile_peers, EXTRA, dim)

    count = keys // block
    now = scores(0)
    shift = jnp.max(now, axis=1, keepdims=True) * scale
    for j in range(count):
        later = scores(j + 1) if j + 1 < count else None
        weights = jnp.exp2(now * scale - shift).astype(BF)
        part = jnp.dot(weights, values(j), preferred_element_type=F32)
        if j == 0:
            acc_ref[...] = part
        else:
            acc_ref[...] += part
        now = later
    finish(shift)
    fits = jnp.max(acc_ref[:, dim:]) < LIMIT

    @pl.when(jnp.logical_not(fits))
    def _():
        acc_ref[...] = jnp.zeros_like(acc_ref)

        def step(j, top):
            part = scores(j) * scale
            new = jnp.maximum(top, jnp.max(part, axis=1, keepdims=True))
            weights = jnp.exp2(part - new).astype(BF)
            acc_ref[...] = acc_ref[...] * jnp.exp2(top - new) + jnp.dot(
                weights, values(j), preferred_element_type=F32
            )
            return new

        finish(lax.fori_loop(0, count, step, jnp.full((rows, 1), -1e30, F32)))


def attend(q, keys_t, values, per):
    peers, peer_rows, dim = q.shape
    count = values.shape[0]
    tile = max(1, min(peers, 512 // peer_rows))
    block = min(512, count)
    rows = peers * peer_rows
    return pl.pallas_call(
        functools.partial(attend_kernel, per, block),
        out_shape=jax.ShapeDtypeStruct((peers, peer_rows + EXTRA, dim), BF),
        grid=(peers // tile,),
        in_specs=[
            pl.BlockSpec((tile, peer_rows, dim), lambda i: (i, 0, 0)),
            pl.BlockSpec((dim, count), lambda i: (0, 0)),
            pl.BlockSpec((count, dim), lambda i: (0, 0)),
        ],
        out_specs=pl.BlockSpec((tile, peer_rows + EXTRA, dim), lambda i: (i, 0, 0)),
        scratch_shapes=[pltpu.VMEM((tile * peer_rows, 2 * dim), F32)],
        compiler_params=params(),
        cost_estimate=pl.CostEstimate(
            flops=8 * rows * count * dim, bytes_accessed=4 << 20, transcendentals=rows * count
        ),
        name="attend_prefix",
    )(q, keys_t, values)


def visibility(lengths, draft_count, suffix_count):
    position = jnp.arange(suffix_count + draft_count, dtype=jnp.int32)
    draft_pos = jnp.arange(draft_count, dtype=jnp.int32)
    earlier = position[None, None, :] < lengths[:, None, None]
    earlier = earlier & (position[None, None, :] < suffix_count)
    fresh = (position[None, :] >= suffix_count) & (
        position[None, :] - suffix_count <= draft_pos[:, None]
    )
    return earlier | fresh[None, :, :]


def local_attention(query_grid, key_rows, value_rows, visible):
    scale = query_grid.shape[-1] ** (-0.5)
    scores = (
        jnp.einsum("rtagd,rjad->rtagj", query_grid, key_rows, preferred_element_type=F32) * scale
    )
    visible_mask = visible[:, :, None, None, :]
    scores = jnp.where(visible_mask, scores, F32(-1e30))
    top = jnp.max(scores, axis=-1)
    exponent = jnp.where(visible_mask, jnp.exp(scores - top[..., None]), F32(0.0))
    denominator = jnp.sum(exponent, axis=-1)
    summed = jnp.einsum(
        "rtagj,rjad->rtagd", exponent.astype(BF), value_rows, preferred_element_type=F32
    )
    return summed / denominator[..., None], (top + jnp.log(denominator)) * F32(math.log2(math.e))


def join_kernel(
    capacity, held, halves, heads, per, group, base, order, target, own, *refs
):
    received = [refs[s * heads : (s + 1) * heads] for s in range(halves)]
    refs = refs[halves * heads :]
    local, local_log, weight, out, part, mine, logs, att = refs
    del own
    rows, dim = mine.shape[0] // per, mine.shape[1]
    peer_rows = held * per

    @pl.when(pl.program_id(0) == 0)
    def _():
        lane = lax.broadcasted_iota(jnp.int32, (per, dim), 1)
        row = lax.broadcasted_iota(jnp.int32, (per, dim), 0)
        diagonal = (lane % per == row) & (lane < 3 * per)
        slot_of = lax.broadcasted_iota(jnp.int32, (EXTRA, dim), 0)
        ones = jnp.ones((dim, dim), BF)
        for a in range(heads):

            def one(i, _):
                at = order[base + i]
                to = target[base + i]
                peer, slot = to // capacity, to % capacity
                half, slot = slot // held, slot % held
                start = pl.multiple_of(slot * per, per)
                block = received[0][a][peer, pl.ds(start, per), :].astype(F32)
                extra = received[0][a][peer, peer_rows:, :].astype(F32)
                if halves == 2:
                    other = received[1][a][peer, pl.ds(start, per), :].astype(F32)
                    other_extra = received[1][a][peer, peer_rows:, :].astype(F32)
                    block = jnp.where(half == 0, block, other)
                    extra = jnp.where(half == 0, extra, other_extra)
                here = pl.multiple_of(i * per, per)
                part[pl.ds(here, per), :] = block
                mine[pl.ds(here, per), :] = local[a, at]
                picked = jnp.sum(jnp.where(slot_of == slot, extra, 0.0), axis=0, keepdims=True)
                logs[0, pl.ds(here, per), :] = jnp.where(diagonal, picked, 0.0).astype(BF)
                own_log = local_log[a, at]
                logs[1, pl.ds(here, per), :] = jnp.where(diagonal, own_log, 0.0).astype(BF)
                return 0

            lax.fori_loop(0, rows, one, 0)
            first = jnp.dot(logs[0], ones, preferred_element_type=F32)
            second = jnp.dot(logs[1], ones, preferred_element_type=F32)
            top = jnp.maximum(first, second)
            first = jnp.exp2(first - top)
            second = jnp.exp2(second - top)
            part[...] = (part[...] * first + mine[...] * second) / (first + second)
            for g in range(group):
                head = part[pl.ds(g, rows * per // group, stride=group), :]
                column = (a * group + g) * dim
                att[:, column : column + dim] = head.astype(BF)

    out[...] = jnp.dot(att[...], weight[...], preferred_element_type=F32).astype(BF)


def join(received, local, local_log, order, target, own, weight, base, rows, capacity, held, group):
    halves, heads = len(received), len(received[0])
    flat = [array for half in received for array in half]
    _, slots, per, dim = local.shape
    depth, width = weight.shape
    draft = per // group
    block = 512
    share = width // block
    groups = lax.axis_size("tensor")
    each = width // groups // block

    def column(n, order, target, own):
        place = n // each
        chips = groups // 2
        core = jnp.where(place < chips, 1 - own[0] % 2, own[0] % 2)
        shard = 2 * (place % chips) + core
        return (0, shard * each + n % each)

    whole = lambda array: pl.BlockSpec(array.shape, lambda n, *_: (0,) * array.ndim)
    return pl.pallas_call(
        functools.partial(join_kernel, capacity, held, halves, heads, per, group, base),
        out_shape=jax.ShapeDtypeStruct((rows * draft, width), BF),
        grid_spec=pltpu.PrefetchScalarGridSpec(
            num_scalar_prefetch=3,
            grid=(share,),
            in_specs=[whole(array) for array in flat]
            + [whole(local), whole(local_log), pl.BlockSpec((depth, block), column)],
            out_specs=pl.BlockSpec((rows * draft, block), lambda n, *_: (0, n)),
            scratch_shapes=[
                pltpu.VMEM((rows * per, dim), F32),
                pltpu.VMEM((rows * per, dim), F32),
                pltpu.VMEM((2, rows * per, dim), BF),
                pltpu.VMEM((rows * draft, depth), BF),
            ],
        ),
        compiler_params=params(),
        cost_estimate=pl.CostEstimate(
            flops=2 * rows * draft * depth * width, bytes_accessed=24 << 20, transcendentals=0
        ),
        name="join_project",
    )(order, target, own, *flat, local, local_log, weight)


def scatter_sum(terms, own):
    size = lax.axis_size("tensor")
    chips = size // 2
    width = terms.shape[1] // size
    half = chips * width
    there = lax.ppermute(terms[:, :half], "tensor", [(i, i ^ 1) for i in range(size)])
    both = terms[:, half:].astype(F32) + there.astype(F32)
    shares = [both[:, c * width : (c + 1) * width] for c in range(chips)]
    chip = own // 2

    def share_of(index):
        picked = shares[0]
        for c in range(1, chips):
            picked = jnp.where(index == c, shares[c], picked)
        return picked

    total = share_of(chip)
    for d in range(1, chips):
        pairs = [(i, i ^ (2 * d)) for i in range(size)]
        got = lax.ppermute(share_of(chip ^ d).astype(BF), "tensor", pairs)
        total = total + got.astype(F32)
    return total.astype(BF)


def exchange(x):
    return lax.all_to_all(x, "dp", split_axis=0, concat_axis=0, tiled=True)


def body(
    queries,
    draft_keys,
    draft_values,
    suffix_keys,
    suffix_values,
    suffix_len,
    prefix_keys,
    prefix_values,
    row_prefix,
    prefix_slot,
    out_weight,
):
    row_count, draft, query_heads, dim = queries.shape
    heads = draft_keys.shape[2]
    group = query_heads // heads
    per = draft * group
    suffix_count = suffix_keys.shape[1]
    peers = lax.axis_size("dp")
    capacity = 2 * row_count // peers
    held = capacity // 2
    own = lax.axis_index("tensor").astype(jnp.int32)

    slot_row, place, order, target = route(row_prefix, prefix_slot, peers, capacity)
    sent = [
        [exchange(q) for q in pack(queries, slot_row, peers, capacity, held, s * held, heads)]
        for s in range(2)
    ]

    keys_t = [prefix_keys[0, :, a, :].T for a in range(heads)]
    values = [prefix_values[0, :, a, :] for a in range(heads)]

    query_grid = queries.reshape(row_count, draft, heads, group, dim)
    all_keys = jnp.concatenate([suffix_keys, draft_keys], axis=1)
    all_values = jnp.concatenate([suffix_values, draft_values], axis=1)
    visible = visibility(suffix_len, draft, suffix_count)
    local, local_log = local_attention(query_grid, all_keys, all_values, visible)
    local = local.transpose(2, 0, 1, 3, 4).reshape(heads, row_count, per, dim)
    log = local_log.transpose(2, 0, 1, 3).reshape(heads, row_count, 1, per)
    high = lax.reduce_precision(log, 8, 7)
    mid = lax.reduce_precision(log - high, 8, 7)
    low = log - high - mid
    terms = jnp.concatenate([high, mid, low], axis=-1)
    terms = jnp.pad(terms, ((0, 0), (0, 0), (0, 0), (0, dim - 3 * per)))

    back = [[exchange(attend(sent[s][a], keys_t[a], values[a], per)) for a in range(heads)] for s in range(2)]

    rows = row_count // 2
    outs = []
    for s in range(2):
        partial = join(
            back[: s + 1],
            local,
            terms,
            order,
            target,
            own.reshape(1),
            out_weight,
            s * rows,
            rows,
            capacity,
            held,
            group,
        )
        outs.append(scatter_sum(partial, own))
    ordered = jnp.concatenate(outs, axis=0).reshape(row_count, -1)
    pick = (place[:, None] == jnp.arange(row_count, dtype=jnp.int32)[None, :]).astype(BF)
    result = jnp.dot(pick, ordered, preferred_element_type=F32).astype(BF)
    return result.reshape(row_count, draft, -1)


def solution(mesh):
    placed = (
        P("dp", None, "tensor", None),
        P("dp", None, "tensor", None),
        P("dp", None, "tensor", None),
        P("dp", None, "tensor", None),
        P("dp", None, "tensor", None),
        P("dp"),
        P("dp", None, "tensor", None),
        P("dp", None, "tensor", None),
        P("dp", None),
        P(),
        P("tensor", None),
    )
    return jax.shard_map(
        body, mesh=mesh, in_specs=placed, out_specs=P("dp", None, "tensor"), check_vma=False
    )
```

```python
import functools
import math

import jax
import jax.numpy as jnp
from jax import lax
from jax.experimental import pallas as pl
from jax.experimental.pallas import tpu as pltpu
from jax.sharding import PartitionSpec as P

BF = jnp.bfloat16
F32 = jnp.float32
EXTRA = 16
VMEM = 56 * 1024 * 1024
LIMIT = 1e30


def params():
    return pltpu.CompilerParams(vmem_limit_bytes=VMEM)


def route(row_prefix, prefix_slot, me, peers, capacity):
    rows = row_prefix.shape[0]
    prefixes = prefix_slot.shape[0]
    name = row_prefix[:, 0]
    row = jnp.arange(rows, dtype=jnp.int32)
    owner = jnp.sum(
        jnp.where(
            row_prefix == jnp.arange(prefixes, dtype=jnp.int32)[None, :], prefix_slot[None, :], 0
        ),
        axis=1,
    )
    same = (name[:, None] == name[None, :]) & (row[None, :] < row[:, None])
    rank = jnp.sum(same.astype(jnp.int32), axis=1)
    target = (owner ^ me) * capacity + rank
    slots = jnp.arange(peers * capacity, dtype=jnp.int32)
    slot_row = jnp.sum(jnp.where(target[None, :] == slots[:, None], row[None, :], 0), axis=1)
    place = jnp.sum((target[None, :] < target[:, None]).astype(jnp.int32), axis=1)
    at = place[None, :] == row[:, None]
    order = jnp.sum(jnp.where(at, row[None, :], 0), axis=1)
    order_target = jnp.sum(jnp.where(at, target[None, :], 0), axis=1)
    return slot_row, place, order, order_target


def pack_kernel(shifts, capacity, slot_row, q_ref, *outs):
    per = q_ref.shape[1] * q_ref.shape[2]

    def one(k, _):
        for shift, out in zip(shifts, outs):
            out[k] = q_ref[slot_row[shift * capacity + k]]
        return 0

    lax.fori_loop(0, capacity, one, 0)


def pack(queries, slot_row, shifts, capacity):
    shape = jax.ShapeDtypeStruct((capacity,) + queries.shape[1:], BF)
    packed = pl.pallas_call(
        functools.partial(pack_kernel, shifts, capacity),
        out_shape=[shape] * len(shifts),
        grid_spec=pltpu.PrefetchScalarGridSpec(
            num_scalar_prefetch=1,
            grid=(1,),
            in_specs=[pl.BlockSpec(queries.shape, lambda i, s: (0, 0, 0, 0))],
            out_specs=[pl.BlockSpec(shape.shape, lambda i, s: (0, 0, 0, 0))] * len(shifts),
        ),
        compiler_params=params(),
        cost_estimate=pl.CostEstimate(flops=0, bytes_accessed=4 << 20, transcendentals=0),
        name="pack_queries",
    )(slot_row, queries)
    return [x.reshape(-1, x.shape[-1]) for x in packed]


def split_kernel(heads, k_ref, v_ref, kt_ref, vs_ref, wide):
    count = v_ref.shape[0] // heads
    for source, is_key in ((k_ref, True), (v_ref, False)):
        wide[...] = source[...].astype(F32)
        for a in range(heads):
            part = wide[pl.ds(a, count, stride=heads), :]
            if is_key:
                kt_ref[a] = part.T.astype(BF)
            else:
                vs_ref[a] = part.astype(BF)


def split_heads(keys, values):
    count, heads, dim = keys.shape
    steps = 4
    each = count // steps
    rows = pl.BlockSpec((each * heads, dim), lambda i: (i, 0))
    return pl.pallas_call(
        functools.partial(split_kernel, heads),
        out_shape=[
            jax.ShapeDtypeStruct((heads, dim, count), BF),
            jax.ShapeDtypeStruct((heads, count, dim), BF),
        ],
        grid=(steps,),
        in_specs=[rows, rows],
        out_specs=[
            pl.BlockSpec((heads, dim, each), lambda i: (0, 0, i)),
            pl.BlockSpec((heads, each, dim), lambda i: (0, i, 0)),
        ],
        scratch_shapes=[pltpu.VMEM((each * heads, dim), F32)],
        compiler_params=params(),
        cost_estimate=pl.CostEstimate(flops=0, bytes_accessed=8 << 20, transcendentals=0),
        name="split_heads",
    )(keys.reshape(count * heads, dim), values.reshape(count * heads, dim))


def attend_kernel(capacity, group, block, q_ref, k_ref, v_ref, o_ref, acc_ref):
    heads, dim, keys = k_ref.shape
    rows = q_ref.shape[0]
    per = rows // capacity
    each = rows // heads
    scale = dim**-0.5 * math.log2(math.e)
    ones = jnp.ones((block, dim), BF)
    grid = q_ref[...].astype(F32).reshape(rows // (heads * group), heads, group, dim)
    queries = [grid[:, a].reshape(each, dim).astype(BF) for a in range(heads)]

    def scores(a, j):
        part = k_ref[a, :, pl.ds(j * block, block)]
        return jnp.dot(queries[a], part, preferred_element_type=F32)

    def values(a, j):
        return jnp.concatenate([v_ref[a, pl.ds(j * block, block), :], ones], axis=1)

    def natural(parts):
        split = [x.reshape(each // group, 1, group, dim) for x in parts]
        return jnp.concatenate(split, axis=1).reshape(rows, dim)

    def finish(shifts):
        sums = [acc_ref[a, :, dim:] for a in range(heads)]
        out = [acc_ref[a, :, :dim] / sums[a] for a in range(heads)]
        o_ref[:rows, :] = natural(out).astype(BF)
        log_sum = natural([shifts[a] + jnp.log2(sums[a]) for a in range(heads)])
        high = log_sum.astype(BF).astype(F32)
        lane = lax.broadcasted_iota(jnp.int32, (rows, dim), 1)
        row = lax.broadcasted_iota(jnp.int32, (rows, dim), 0)
        term = jnp.where(lane < per, high, log_sum - high)
        term = jnp.where((lane % per == row % per) & (lane < 2 * per), term, 0.0)
        slot = lax.broadcasted_iota(jnp.int32, (EXTRA, rows), 0)
        source = lax.broadcasted_iota(jnp.int32, (EXTRA, rows), 1) // per
        pick = jnp.where(source == slot, 1.0, 0.0).astype(BF)
        logs = jnp.dot(pick, term.astype(BF), preferred_element_type=F32)
        o_ref[rows:, :] = logs.astype(BF)

    count = keys // block
    now = [scores(a, 0) for a in range(heads)]
    shifts = [jnp.max(x, axis=1, keepdims=True) * scale for x in now]
    for j in range(count):
        for a in range(heads):
            weights = jnp.exp2(now[a] * scale - shifts[a]).astype(BF)
            if j + 1 < count:
                now[a] = scores(a, j + 1)
            part = jnp.dot(weights, values(a, j), preferred_element_type=F32)
            if j == 0:
                acc_ref[a] = part
            else:
                acc_ref[a] += part
    finish(shifts)
    fits = jnp.max(acc_ref[:, :, dim:]) < LIMIT

    @pl.when(jnp.logical_not(fits))
    def _():
        acc_ref[...] = jnp.zeros_like(acc_ref)
        tops = []
        for a in range(heads):

            def step(j, top):
                part = scores(a, j) * scale
                new = jnp.maximum(top, jnp.max(part, axis=1, keepdims=True))
                weights = jnp.exp2(part - new).astype(BF)
                acc_ref[a] = acc_ref[a] * jnp.exp2(top - new) + jnp.dot(
                    weights, values(a, j), preferred_element_type=F32
                )
                return new

            tops.append(lax.fori_loop(0, count, step, jnp.full((each, 1), -1e30, F32)))
        finish(tops)


def attend(q, keys_t, values, capacity, group):
    rows, dim = q.shape
    heads, count, _ = values.shape
    block = min(512, count)
    return pl.pallas_call(
        functools.partial(attend_kernel, capacity, group, block),
        out_shape=jax.ShapeDtypeStruct((rows + EXTRA, dim), BF),
        scratch_shapes=[pltpu.VMEM((heads, rows // heads, 2 * dim), F32)],
        compiler_params=params(),
        cost_estimate=pl.CostEstimate(
            flops=8 * rows * count * dim, bytes_accessed=5 << 20, transcendentals=rows * count
        ),
        name="attend_prefix",
    )(q, keys_t, values)


def visibility(lengths, draft_count, suffix_count):
    position = jnp.arange(suffix_count + draft_count, dtype=jnp.int32)
    draft_pos = jnp.arange(draft_count, dtype=jnp.int32)
    earlier = position[None, None, :] < lengths[:, None, None]
    earlier = earlier & (position[None, None, :] < suffix_count)
    fresh = (position[None, :] >= suffix_count) & (
        position[None, :] - suffix_count <= draft_pos[:, None]
    )
    return earlier | fresh[None, :, :]


def local_attention(query_grid, key_rows, value_rows, visible):
    scale = query_grid.shape[-1] ** (-0.5)
    scores = (
        jnp.einsum("rtagd,rjad->rtagj", query_grid, key_rows, preferred_element_type=F32) * scale
    )
    visible_mask = visible[:, :, None, None, :]
    scores = jnp.where(visible_mask, scores, F32(-1e30))
    top = jnp.max(scores, axis=-1)
    exponent = jnp.where(visible_mask, jnp.exp(scores - top[..., None]), F32(0.0))
    denominator = jnp.sum(exponent, axis=-1)
    summed = jnp.einsum(
        "rtagj,rjad->rtagd", exponent.astype(BF), value_rows, preferred_element_type=F32
    )
    return summed / denominator[..., None], (top + jnp.log(denominator)) * F32(math.log2(math.e))


def join_kernel(capacity, count, base, order, target, own, *refs):
    del own
    received, refs = refs[:count], refs[count:]
    local, local_log, weight, out, blocks, block_logs, part, mine, logs, spread, att = refs
    rows, per, dim = part.shape
    held = capacity * per
    heads = att.shape[1] // dim
    draft = per // heads

    @pl.when(pl.program_id(0) == 0)
    def _():
        for s in range(count):
            values = received[s][...].astype(F32)
            blocks[s * capacity : (s + 1) * capacity] = values[:held].reshape(capacity, per, dim)
            block_logs[s * EXTRA : (s + 1) * EXTRA] = values[held:]

        def gather(i, _):
            at = order[base + i]
            slot = target[base + i]
            part[i] = blocks[slot]
            mine[i] = local[at]
            place = (slot // capacity) * EXTRA + slot % capacity
            logs[0, pl.ds(i, 1), :] = block_logs[pl.ds(place, 1), :]
            logs[1, pl.ds(i, 1), :] = local_log[pl.ds(at, 1), :]
            return 0

        lax.fori_loop(0, rows, gather, 0)
        lane = lax.broadcasted_iota(jnp.int32, (rows, dim), 1)
        first = logs[0] + pltpu.roll(logs[0], dim - per, axis=1)
        share = 1.0 / (1.0 + jnp.exp2(logs[1] - first))
        high = share.astype(BF).astype(F32)
        low = pltpu.roll(share - high, per, axis=1)
        logs[0] = jnp.where(lane < per, high, jnp.where(lane < 2 * per, low, 0.0))
        diagonal = lax.broadcasted_iota(jnp.int32, (per, dim), 1) % per
        diagonal = diagonal == lax.broadcasted_iota(jnp.int32, (per, dim), 0)

        def widen(i, _):
            row = logs[0, pl.ds(i, 1), :]
            spread[i] = jnp.where(diagonal, row, 0.0).astype(BF)
            return 0

        lax.fori_loop(0, rows, widen, 0)
        ones = jnp.ones((dim, dim), BF)
        shares = jnp.dot(
            spread[...].reshape(rows * per, dim), ones, preferred_element_type=F32
        ).reshape(rows, per, dim)
        mixed = mine[...] + shares * (part[...] - mine[...])
        part[...] = mixed
        flat = part.reshape(rows * per, dim)
        for h in range(heads):
            head = flat[pl.ds(h, rows * draft, stride=heads), :]
            att[:, h * dim : (h + 1) * dim] = head.astype(BF)

    out[...] = jnp.dot(att[...], weight[...], preferred_element_type=F32).astype(BF)


def join(received, local, local_log, order, target, own, weight, base, rows, capacity):
    count = len(received)
    per, dim = local.shape[1:]
    depth, width = weight.shape
    draft = per * dim // depth
    block = 512
    groups = lax.axis_size("tensor")
    each = width // groups // block

    def column(n, order, target, own):
        place = n // each
        chips = groups // 2
        core = jnp.where(place < chips, 1 - own[0] % 2, own[0] % 2)
        shard = 2 * (place % chips) + core
        return (0, shard * each + n % each)

    whole = lambda array: pl.BlockSpec(array.shape, lambda n, *_: (0,) * array.ndim)
    return pl.pallas_call(
        functools.partial(join_kernel, capacity, count, base),
        out_shape=jax.ShapeDtypeStruct((rows * draft, width), BF),
        grid_spec=pltpu.PrefetchScalarGridSpec(
            num_scalar_prefetch=3,
            grid=(width // block,),
            in_specs=[whole(array) for array in received]
            + [whole(local), whole(local_log), pl.BlockSpec((depth, block), column)],
            out_specs=pl.BlockSpec((rows * draft, block), lambda n, *_: (0, n)),
            scratch_shapes=[
                pltpu.VMEM((count * capacity, per, dim), F32),
                pltpu.VMEM((count * EXTRA, dim), F32),
                pltpu.VMEM((rows, per, dim), F32),
                pltpu.VMEM((rows, per, dim), F32),
                pltpu.VMEM((2, rows, dim), F32),
                pltpu.VMEM((rows, per, dim), BF),
                pltpu.VMEM((rows * draft, depth), BF),
            ],
        ),
        compiler_params=params(),
        cost_estimate=pl.CostEstimate(
            flops=2 * rows * draft * depth * width, bytes_accessed=24 << 20, transcendentals=0
        ),
        name="join_project",
    )(order, target, own, *received, local, local_log, weight)


def scatter_sum(terms, own):
    size = lax.axis_size("tensor")
    chips = size // 2
    width = terms.shape[1] // size
    half = chips * width
    there = lax.ppermute(terms[:, :half], "tensor", [(i, i ^ 1) for i in range(size)])
    both = terms[:, half:].astype(F32) + there.astype(F32)
    shares = [both[:, c * width : (c + 1) * width] for c in range(chips)]
    chip = own // 2

    def share_of(index):
        picked = shares[0]
        for c in range(1, chips):
            picked = jnp.where(index == c, shares[c], picked)
        return picked

    total = share_of(chip)
    for d in range(1, chips):
        pairs = [(i, i ^ (2 * d)) for i in range(size)]
        got = lax.ppermute(share_of(chip ^ d).astype(BF), "tensor", pairs)
        total = total + got.astype(F32)
    return total.astype(BF)


def hop(x, shift):
    size = lax.axis_size("dp")
    return lax.ppermute(x, "dp", [(i, i ^ shift) for i in range(size)])


def body(
    queries,
    draft_keys,
    draft_values,
    suffix_keys,
    suffix_values,
    suffix_len,
    prefix_keys,
    prefix_values,
    row_prefix,
    prefix_slot,
    out_weight,
):
    row_count, draft, query_heads, dim = queries.shape
    heads = draft_keys.shape[2]
    group = query_heads // heads
    per = draft * query_heads
    suffix_count = suffix_keys.shape[1]
    peers = lax.axis_size("dp")
    capacity = 2 * row_count // peers
    own = lax.axis_index("tensor").astype(jnp.int32)
    me = lax.axis_index("dp").astype(jnp.int32)

    slot_row, place, order, target = route(row_prefix, prefix_slot, me, peers, capacity)
    near, far = list(range(peers // 2)), list(range(peers // 2, peers))
    queried = dict(zip(far, pack(queries, slot_row, far, capacity)))
    queried.update(zip(near, pack(queries, slot_row, near, capacity)))
    arrived = {s: hop(queried[s], s) if s else queried[s] for s in far + near}

    keys_t, values = split_heads(prefix_keys[0], prefix_values[0])
    back = {}
    for s in near + far:
        result = attend(arrived[s], keys_t, values, capacity, group)
        back[s] = hop(result, s) if s else result

    query_grid = queries.reshape(row_count, draft, heads, group, dim)
    all_keys = jnp.concatenate([suffix_keys, draft_keys], axis=1)
    all_values = jnp.concatenate([suffix_values, draft_values], axis=1)
    visible = visibility(suffix_len, draft, suffix_count)
    local, local_log = local_attention(query_grid, all_keys, all_values, visible)
    local = local.reshape(row_count, per, dim)
    local_log = jnp.pad(local_log.reshape(row_count, per), ((0, 0), (0, dim - per)))

    rows = row_count // 2
    early = peers - rows // capacity
    outs = []
    for base, count in ((0, early), (rows, peers)):
        received = [back[s] for s in range(count)]
        partial = join(
            received, local, local_log, order, target, own.reshape(1), out_weight, base, rows, capacity
        )
        outs.append(scatter_sum(partial, own))
    ordered = jnp.concatenate(outs, axis=0).reshape(row_count, -1)
    pick = (place[:, None] == jnp.arange(row_count, dtype=jnp.int32)[None, :]).astype(BF)
    result = jnp.dot(pick, ordered, preferred_element_type=F32).astype(BF)
    return result.reshape(row_count, draft, -1)


def solution(mesh):
    placed = (
        P("dp", None, "tensor", None),
        P("dp", None, "tensor", None),
        P("dp", None, "tensor", None),
        P("dp", None, "tensor", None),
        P("dp", None, "tensor", None),
        P("dp"),
        P("dp", None, "tensor", None),
        P("dp", None, "tensor", None),
        P("dp", None),
        P(),
        P("tensor", None),
    )
    return jax.shard_map(
        body, mesh=mesh, in_specs=placed, out_specs=P("dp", None, "tensor"), check_vma=False
    )
```

```python
import functools
import math

import jax
import jax.numpy as jnp
from jax import lax
from jax.experimental import pallas as pl
from jax.experimental.pallas import tpu as pltpu
from jax.sharding import PartitionSpec as P

BF = jnp.bfloat16
F32 = jnp.float32
EXTRA = 16
VMEM = 56 * 1024 * 1024
LIMIT = 1e30


def params():
    return pltpu.CompilerParams(vmem_limit_bytes=VMEM)


def route(row_prefix, prefix_slot, me, peers, capacity):
    rows = row_prefix.shape[0]
    prefixes = prefix_slot.shape[0]
    name = row_prefix[:, 0]
    row = jnp.arange(rows, dtype=jnp.int32)
    owner = jnp.sum(
        jnp.where(
            row_prefix == jnp.arange(prefixes, dtype=jnp.int32)[None, :], prefix_slot[None, :], 0
        ),
        axis=1,
    )
    same = (name[:, None] == name[None, :]) & (row[None, :] < row[:, None])
    rank = jnp.sum(same.astype(jnp.int32), axis=1)
    target = (owner ^ me) * capacity + rank
    slots = jnp.arange(peers * capacity, dtype=jnp.int32)
    slot_row = jnp.sum(jnp.where(target[None, :] == slots[:, None], row[None, :], 0), axis=1)
    place = jnp.sum((target[None, :] < target[:, None]).astype(jnp.int32), axis=1)
    at = place[None, :] == row[:, None]
    order = jnp.sum(jnp.where(at, row[None, :], 0), axis=1)
    order_target = jnp.sum(jnp.where(at, target[None, :], 0), axis=1)
    return slot_row, place, order, order_target


def pack_kernel(shifts, capacity, slot_row, q_ref, *outs):
    per = q_ref.shape[1] * q_ref.shape[2]

    def one(k, _):
        for shift, out in zip(shifts, outs):
            out[k] = q_ref[slot_row[shift * capacity + k]]
        return 0

    lax.fori_loop(0, capacity, one, 0)


def pack(queries, slot_row, shifts, capacity):
    shape = jax.ShapeDtypeStruct((capacity,) + queries.shape[1:], BF)
    packed = pl.pallas_call(
        functools.partial(pack_kernel, shifts, capacity),
        out_shape=[shape] * len(shifts),
        grid_spec=pltpu.PrefetchScalarGridSpec(
            num_scalar_prefetch=1,
            grid=(1,),
            in_specs=[pl.BlockSpec(queries.shape, lambda i, s: (0, 0, 0, 0))],
            out_specs=[pl.BlockSpec(shape.shape, lambda i, s: (0, 0, 0, 0))] * len(shifts),
        ),
        compiler_params=params(),
        cost_estimate=pl.CostEstimate(flops=0, bytes_accessed=4 << 20, transcendentals=0),
        name="pack_queries",
    )(slot_row, queries)
    return [x.reshape(-1, x.shape[-1]) for x in packed]


def split_kernel(heads, k_ref, v_ref, kt_ref, vs_ref, wide):
    count = v_ref.shape[0] // heads
    for source, is_key in ((k_ref, True), (v_ref, False)):
        wide[...] = source[...].astype(F32)
        for a in range(heads):
            part = wide[pl.ds(a, count, stride=heads), :]
            if is_key:
                kt_ref[a] = part.T.astype(BF)
            else:
                vs_ref[a] = part.astype(BF)


def split_heads(keys, values):
    count, heads, dim = keys.shape
    steps = 4
    each = count // steps
    rows = pl.BlockSpec((each * heads, dim), lambda i: (i, 0))
    return pl.pallas_call(
        functools.partial(split_kernel, heads),
        out_shape=[
            jax.ShapeDtypeStruct((heads, dim, count), BF),
            jax.ShapeDtypeStruct((heads, count, dim), BF),
        ],
        grid=(steps,),
        in_specs=[rows, rows],
        out_specs=[
            pl.BlockSpec((heads, dim, each), lambda i: (0, 0, i)),
            pl.BlockSpec((heads, each, dim), lambda i: (0, i, 0)),
        ],
        scratch_shapes=[pltpu.VMEM((each * heads, dim), F32)],
        compiler_params=params(),
        cost_estimate=pl.CostEstimate(flops=0, bytes_accessed=8 << 20, transcendentals=0),
        name="split_heads",
    )(keys.reshape(count * heads, dim), values.reshape(count * heads, dim))


def attend_kernel(capacity, group, block, chunk, q_ref, k_ref, v_ref, o_ref, acc_ref, weight_ref):
    heads, dim, keys = k_ref.shape
    rows = q_ref.shape[0]
    per = rows // capacity
    each = rows // heads
    scale = dim**-0.5 * math.log2(math.e)
    ones = jnp.ones((block, dim), BF)
    grid = q_ref[...].astype(F32).reshape(rows // (heads * group), heads, group, dim)
    queries = [grid[:, a].reshape(each, dim).astype(BF) for a in range(heads)]

    def scores(a, j):
        part = k_ref[a, :, pl.ds(j * block, block)]
        return jnp.dot(queries[a], part, preferred_element_type=F32)

    def values(a, j):
        return jnp.concatenate([v_ref[a, pl.ds(j * block, block), :], ones], axis=1)

    def natural(parts):
        split = [x.reshape(each // group, 1, group, dim) for x in parts]
        return jnp.concatenate(split, axis=1).reshape(rows, dim)

    def finish(shifts):
        sums = [acc_ref[a, :, dim:] for a in range(heads)]
        out = [acc_ref[a, :, :dim] / sums[a] for a in range(heads)]
        o_ref[:rows, :] = natural(out).astype(BF)
        log_sum = natural([shifts[a] + jnp.log2(sums[a]) for a in range(heads)])
        high = log_sum.astype(BF).astype(F32)
        lane = lax.broadcasted_iota(jnp.int32, (rows, dim), 1)
        row = lax.broadcasted_iota(jnp.int32, (rows, dim), 0)
        term = jnp.where(lane < per, high, log_sum - high)
        term = jnp.where((lane % per == row % per) & (lane < 2 * per), term, 0.0)
        slot = lax.broadcasted_iota(jnp.int32, (EXTRA, rows), 0)
        source = lax.broadcasted_iota(jnp.int32, (EXTRA, rows), 1) // per
        pick = jnp.where(source == slot, 1.0, 0.0).astype(BF)
        logs = jnp.dot(pick, term.astype(BF), preferred_element_type=F32)
        o_ref[rows:, :] = logs.astype(BF)

    count = keys // block
    steps = block // chunk

    def accumulate(a, j):
        slot = (a * count + j) % 2
        part = jnp.dot(weight_ref[slot], values(a, j), preferred_element_type=F32)
        if j == 0:
            acc_ref[a] = part
        else:
            acc_ref[a] += part

    shifts = []
    before = None
    for a in range(heads):
        for j in range(count):
            slot = (a * count + j) % 2
            for c in range(steps):
                first = j * block + c * chunk
                part = jnp.dot(
                    queries[a], k_ref[a, :, first : first + chunk], preferred_element_type=F32
                )
                if first == 0:
                    shifts.append(jnp.max(part, axis=1, keepdims=True) * scale)
                weights = jnp.exp2(part * scale - shifts[a])
                weight_ref[slot, :, c * chunk : (c + 1) * chunk] = weights.astype(BF)
            if before is not None:
                accumulate(*before)
            before = (a, j)
    accumulate(*before)
    finish(shifts)
    fits = jnp.max(acc_ref[:, :, dim:]) < LIMIT

    @pl.when(jnp.logical_not(fits))
    def _():
        acc_ref[...] = jnp.zeros_like(acc_ref)
        tops = []
        for a in range(heads):

            def step(j, top):
                part = scores(a, j) * scale
                new = jnp.maximum(top, jnp.max(part, axis=1, keepdims=True))
                weights = jnp.exp2(part - new).astype(BF)
                acc_ref[a] = acc_ref[a] * jnp.exp2(top - new) + jnp.dot(
                    weights, values(a, j), preferred_element_type=F32
                )
                return new

            tops.append(lax.fori_loop(0, count, step, jnp.full((each, 1), -1e30, F32)))
        finish(tops)


def attend(q, keys_t, values, capacity, group):
    rows, dim = q.shape
    heads, count, _ = values.shape
    block = min(1024, count)
    chunk = min(256, block)
    return pl.pallas_call(
        functools.partial(attend_kernel, capacity, group, block, chunk),
        out_shape=jax.ShapeDtypeStruct((rows + EXTRA, dim), BF),
        scratch_shapes=[
            pltpu.VMEM((heads, rows // heads, 2 * dim), F32),
            pltpu.VMEM((2, rows // heads, block), BF),
        ],
        compiler_params=params(),
        cost_estimate=pl.CostEstimate(
            flops=8 * rows * count * dim, bytes_accessed=5 << 20, transcendentals=rows * count
        ),
        name="attend_prefix",
    )(q, keys_t, values)


def visibility(lengths, draft_count, suffix_count):
    position = jnp.arange(suffix_count + draft_count, dtype=jnp.int32)
    draft_pos = jnp.arange(draft_count, dtype=jnp.int32)
    earlier = position[None, None, :] < lengths[:, None, None]
    earlier = earlier & (position[None, None, :] < suffix_count)
    fresh = (position[None, :] >= suffix_count) & (
        position[None, :] - suffix_count <= draft_pos[:, None]
    )
    return earlier | fresh[None, :, :]


def local_attention(query_grid, key_rows, value_rows, visible):
    scale = query_grid.shape[-1] ** (-0.5)
    scores = (
        jnp.einsum("rtagd,rjad->rtagj", query_grid, key_rows, preferred_element_type=F32) * scale
    )
    visible_mask = visible[:, :, None, None, :]
    scores = jnp.where(visible_mask, scores, F32(-1e30))
    top = jnp.max(scores, axis=-1)
    exponent = jnp.where(visible_mask, jnp.exp(scores - top[..., None]), F32(0.0))
    denominator = jnp.sum(exponent, axis=-1)
    summed = jnp.einsum(
        "rtagj,rjad->rtagd", exponent.astype(BF), value_rows, preferred_element_type=F32
    )
    return summed / denominator[..., None], (top + jnp.log(denominator)) * F32(math.log2(math.e))


def join_kernel(capacity, count, base, order, target, own, *refs):
    del own
    received, refs = refs[:count], refs[count:]
    local, local_log, weight, out, blocks, block_logs, part, mine, logs, spread, att = refs
    rows, per, dim = part.shape
    held = capacity * per
    heads = att.shape[1] // dim
    draft = per // heads

    @pl.when(pl.program_id(0) == 0)
    def _():
        for s in range(count):
            values = received[s][...].astype(F32)
            blocks[s * capacity : (s + 1) * capacity] = values[:held].reshape(capacity, per, dim)
            block_logs[s * EXTRA : (s + 1) * EXTRA] = values[held:]

        def gather(i, _):
            at = order[base + i]
            slot = target[base + i]
            part[i] = blocks[slot]
            mine[i] = local[at]
            place = (slot // capacity) * EXTRA + slot % capacity
            logs[0, pl.ds(i, 1), :] = block_logs[pl.ds(place, 1), :]
            logs[1, pl.ds(i, 1), :] = local_log[pl.ds(at, 1), :]
            return 0

        lax.fori_loop(0, rows, gather, 0)
        lane = lax.broadcasted_iota(jnp.int32, (rows, dim), 1)
        first = logs[0] + pltpu.roll(logs[0], dim - per, axis=1)
        share = 1.0 / (1.0 + jnp.exp2(logs[1] - first))
        high = share.astype(BF).astype(F32)
        low = pltpu.roll(share - high, per, axis=1)
        logs[0] = jnp.where(lane < per, high, jnp.where(lane < 2 * per, low, 0.0))
        diagonal = lax.broadcasted_iota(jnp.int32, (per, dim), 1) % per
        diagonal = diagonal == lax.broadcasted_iota(jnp.int32, (per, dim), 0)

        def widen(i, _):
            row = logs[0, pl.ds(i, 1), :]
            spread[i] = jnp.where(diagonal, row, 0.0).astype(BF)
            return 0

        lax.fori_loop(0, rows, widen, 0)
        ones = jnp.ones((dim, dim), BF)
        shares = jnp.dot(
            spread[...].reshape(rows * per, dim), ones, preferred_element_type=F32
        ).reshape(rows, per, dim)
        mixed = mine[...] + shares * (part[...] - mine[...])
        part[...] = mixed
        flat = part.reshape(rows * per, dim)
        for h in range(heads):
            head = flat[pl.ds(h, rows * draft, stride=heads), :]
            att[:, h * dim : (h + 1) * dim] = head.astype(BF)

    out[...] = jnp.dot(att[...], weight[...], preferred_element_type=F32).astype(BF)


def join(received, local, local_log, order, target, own, weight, base, rows, capacity):
    count = len(received)
    per, dim = local.shape[1:]
    depth, width = weight.shape
    draft = per * dim // depth
    block = 512
    groups = lax.axis_size("tensor")
    each = width // groups // block

    def column(n, order, target, own):
        place = n // each
        chips = groups // 2
        core = jnp.where(place < chips, 1 - own[0] % 2, own[0] % 2)
        shard = 2 * (place % chips) + core
        return (0, shard * each + n % each)

    whole = lambda array: pl.BlockSpec(array.shape, lambda n, *_: (0,) * array.ndim)
    return pl.pallas_call(
        functools.partial(join_kernel, capacity, count, base),
        out_shape=jax.ShapeDtypeStruct((rows * draft, width), BF),
        grid_spec=pltpu.PrefetchScalarGridSpec(
            num_scalar_prefetch=3,
            grid=(width // block,),
            in_specs=[whole(array) for array in received]
            + [whole(local), whole(local_log), pl.BlockSpec((depth, block), column)],
            out_specs=pl.BlockSpec((rows * draft, block), lambda n, *_: (0, n)),
            scratch_shapes=[
                pltpu.VMEM((count * capacity, per, dim), F32),
                pltpu.VMEM((count * EXTRA, dim), F32),
                pltpu.VMEM((rows, per, dim), F32),
                pltpu.VMEM((rows, per, dim), F32),
                pltpu.VMEM((2, rows, dim), F32),
                pltpu.VMEM((rows, per, dim), BF),
                pltpu.VMEM((rows * draft, depth), BF),
            ],
        ),
        compiler_params=params(),
        cost_estimate=pl.CostEstimate(
            flops=2 * rows * draft * depth * width, bytes_accessed=24 << 20, transcendentals=0
        ),
        name="join_project",
    )(order, target, own, *received, local, local_log, weight)


def scatter_sum(terms, own):
    size = lax.axis_size("tensor")
    chips = size // 2
    width = terms.shape[1] // size
    half = chips * width
    there = lax.ppermute(terms[:, :half], "tensor", [(i, i ^ 1) for i in range(size)])
    both = terms[:, half:].astype(F32) + there.astype(F32)
    shares = [both[:, c * width : (c + 1) * width] for c in range(chips)]
    chip = own // 2

    def share_of(index):
        picked = shares[0]
        for c in range(1, chips):
            picked = jnp.where(index == c, shares[c], picked)
        return picked

    total = share_of(chip)
    for d in range(1, chips):
        pairs = [(i, i ^ (2 * d)) for i in range(size)]
        got = lax.ppermute(share_of(chip ^ d).astype(BF), "tensor", pairs)
        total = total + got.astype(F32)
    return total.astype(BF)


def hop(x, shift):
    size = lax.axis_size("dp")
    return lax.ppermute(x, "dp", [(i, i ^ shift) for i in range(size)])


def body(
    queries,
    draft_keys,
    draft_values,
    suffix_keys,
    suffix_values,
    suffix_len,
    prefix_keys,
    prefix_values,
    row_prefix,
    prefix_slot,
    out_weight,
):
    row_count, draft, query_heads, dim = queries.shape
    heads = draft_keys.shape[2]
    group = query_heads // heads
    per = draft * query_heads
    suffix_count = suffix_keys.shape[1]
    peers = lax.axis_size("dp")
    capacity = 2 * row_count // peers
    own = lax.axis_index("tensor").astype(jnp.int32)
    me = lax.axis_index("dp").astype(jnp.int32)

    slot_row, place, order, target = route(row_prefix, prefix_slot, me, peers, capacity)
    near, far = list(range(peers // 2)), list(range(peers // 2, peers))
    queried = dict(zip(far, pack(queries, slot_row, far, capacity)))
    queried.update(zip(near, pack(queries, slot_row, near, capacity)))
    arrived = {s: hop(queried[s], s) if s else queried[s] for s in far + near}

    keys_t, values = split_heads(prefix_keys[0], prefix_values[0])
    back = {}
    for s in near + far:
        result = attend(arrived[s], keys_t, values, capacity, group)
        back[s] = hop(result, s) if s else result

    query_grid = queries.reshape(row_count, draft, heads, group, dim)
    all_keys = jnp.concatenate([suffix_keys, draft_keys], axis=1)
    all_values = jnp.concatenate([suffix_values, draft_values], axis=1)
    visible = visibility(suffix_len, draft, suffix_count)
    local, local_log = local_attention(query_grid, all_keys, all_values, visible)
    local = local.reshape(row_count, per, dim)
    local_log = jnp.pad(local_log.reshape(row_count, per), ((0, 0), (0, dim - per)))

    rows = row_count // 2
    early = peers - rows // capacity
    outs = []
    for base, count in ((0, early), (rows, peers)):
        received = [back[s] for s in range(count)]
        partial = join(
            received, local, local_log, order, target, own.reshape(1), out_weight, base, rows, capacity
        )
        if base == 0:
            late = [back[s] for s in range(early, peers)]
            partial, late = lax.optimization_barrier((partial, late))
            back.update(zip(range(early, peers), late))
        outs.append(scatter_sum(partial, own))
    ordered = jnp.concatenate(outs, axis=0).reshape(row_count, -1)
    pick = (place[:, None] == jnp.arange(row_count, dtype=jnp.int32)[None, :]).astype(BF)
    result = jnp.dot(pick, ordered, preferred_element_type=F32).astype(BF)
    return result.reshape(row_count, draft, -1)


def solution(mesh):
    placed = (
        P("dp", None, "tensor", None),
        P("dp", None, "tensor", None),
        P("dp", None, "tensor", None),
        P("dp", None, "tensor", None),
        P("dp", None, "tensor", None),
        P("dp"),
        P("dp", None, "tensor", None),
        P("dp", None, "tensor", None),
        P("dp", None),
        P(),
        P("tensor", None),
    )
    return jax.shard_map(
        body, mesh=mesh, in_specs=placed, out_specs=P("dp", None, "tensor"), check_vma=False
    )
```

```python
import functools
import math

import jax
import jax.numpy as jnp
from jax import lax
from jax.experimental import pallas as pl
from jax.experimental.pallas import tpu as pltpu
from jax.sharding import PartitionSpec as P

BF = jnp.bfloat16
F32 = jnp.float32
EXTRA = 16
VMEM = 56 * 1024 * 1024
LIMIT = 1e30


def params():
    return pltpu.CompilerParams(vmem_limit_bytes=VMEM)


def route(row_prefix, prefix_slot, me, peers, capacity):
    rows = row_prefix.shape[0]
    prefixes = prefix_slot.shape[0]
    name = row_prefix[:, 0]
    row = jnp.arange(rows, dtype=jnp.int32)
    owner = jnp.sum(
        jnp.where(
            row_prefix == jnp.arange(prefixes, dtype=jnp.int32)[None, :], prefix_slot[None, :], 0
        ),
        axis=1,
    )
    same = (name[:, None] == name[None, :]) & (row[None, :] < row[:, None])
    rank = jnp.sum(same.astype(jnp.int32), axis=1)
    half = peers // 2
    shift = owner ^ me
    target = jnp.where(shift < half, owner % half, shift) * capacity + rank
    slots = jnp.arange(peers * capacity, dtype=jnp.int32)
    slot_row = jnp.sum(jnp.where(target[None, :] == slots[:, None], row[None, :], 0), axis=1)
    place = jnp.sum((target[None, :] < target[:, None]).astype(jnp.int32), axis=1)
    at = place[None, :] == row[:, None]
    order = jnp.sum(jnp.where(at, row[None, :], 0), axis=1)
    order_target = jnp.sum(jnp.where(at, target[None, :], 0), axis=1)
    return slot_row, place, order, order_target


def pack_kernel(first, joined, capacity, slot_row, q_ref, *outs):
    def one(k, _):
        if joined:
            outs[0][k] = q_ref[slot_row[first * capacity + k]]
        else:
            for block, out in enumerate(outs):
                out[k] = q_ref[slot_row[(first + block) * capacity + k]]
        return 0

    lax.fori_loop(0, outs[0].shape[0], one, 0)


def pack(queries, slot_row, first, blocks, capacity, joined):
    each = blocks * capacity if joined else capacity
    count = 1 if joined else blocks
    shape = jax.ShapeDtypeStruct((each,) + queries.shape[1:], BF)
    packed = pl.pallas_call(
        functools.partial(pack_kernel, first, joined, capacity),
        out_shape=[shape] * count,
        grid_spec=pltpu.PrefetchScalarGridSpec(
            num_scalar_prefetch=1,
            grid=(1,),
            in_specs=[pl.BlockSpec(queries.shape, lambda i, s: (0, 0, 0, 0))],
            out_specs=[pl.BlockSpec(shape.shape, lambda i, s: (0, 0, 0, 0))] * count,
        ),
        compiler_params=params(),
        cost_estimate=pl.CostEstimate(flops=0, bytes_accessed=4 << 20, transcendentals=0),
        name="pack_queries",
    )(slot_row, queries)
    return [x.reshape(-1, x.shape[-1]) for x in packed]


def split_kernel(heads, k_ref, v_ref, kt_ref, vs_ref, wide):
    count = v_ref.shape[0] // heads
    for source, is_key in ((k_ref, True), (v_ref, False)):
        wide[...] = source[...].astype(F32)
        for a in range(heads):
            part = wide[pl.ds(a, count, stride=heads), :]
            if is_key:
                kt_ref[a] = part.T.astype(BF)
            else:
                vs_ref[a] = part.astype(BF)


def split_heads(keys, values):
    count, heads, dim = keys.shape
    steps = 4
    each = count // steps
    rows = pl.BlockSpec((each * heads, dim), lambda i: (i, 0))
    return pl.pallas_call(
        functools.partial(split_kernel, heads),
        out_shape=[
            jax.ShapeDtypeStruct((heads, dim, count), BF),
            jax.ShapeDtypeStruct((heads, count, dim), BF),
        ],
        grid=(steps,),
        in_specs=[rows, rows],
        out_specs=[
            pl.BlockSpec((heads, dim, each), lambda i: (0, 0, i)),
            pl.BlockSpec((heads, each, dim), lambda i: (0, i, 0)),
        ],
        scratch_shapes=[pltpu.VMEM((each * heads, dim), F32)],
        compiler_params=params(),
        cost_estimate=pl.CostEstimate(flops=0, bytes_accessed=8 << 20, transcendentals=0),
        name="split_heads",
    )(keys.reshape(count * heads, dim), values.reshape(count * heads, dim))


def attend_kernel(capacity, group, block, chunk, q_ref, k_ref, v_ref, o_ref, acc_ref, weight_ref):
    heads, dim, keys = k_ref.shape
    rows = q_ref.shape[0]
    per = rows // capacity
    each = rows // heads
    scale = dim**-0.5 * math.log2(math.e)
    ones = jnp.ones((block, dim), BF)
    grid = q_ref[...].astype(F32).reshape(rows // (heads * group), heads, group, dim)
    queries = [grid[:, a].reshape(each, dim).astype(BF) for a in range(heads)]

    def scores(a, j):
        part = k_ref[a, :, pl.ds(j * block, block)]
        return jnp.dot(queries[a], part, preferred_element_type=F32)

    def values(a, j):
        return jnp.concatenate([v_ref[a, pl.ds(j * block, block), :], ones], axis=1)

    def natural(parts):
        split = [x.reshape(each // group, 1, group, dim) for x in parts]
        return jnp.concatenate(split, axis=1).reshape(rows, dim)

    def finish(shifts):
        sums = [acc_ref[a, :, dim:] for a in range(heads)]
        out = [acc_ref[a, :, :dim] / sums[a] for a in range(heads)]
        o_ref[:rows, :] = natural(out).astype(BF)
        log_sum = natural([shifts[a] + jnp.log2(sums[a]) for a in range(heads)])
        high = log_sum.astype(BF).astype(F32)
        lane = lax.broadcasted_iota(jnp.int32, (rows, dim), 1)
        row = lax.broadcasted_iota(jnp.int32, (rows, dim), 0)
        term = jnp.where(lane < per, high, log_sum - high)
        term = jnp.where((lane % per == row % per) & (lane < 2 * per), term, 0.0)
        slot = lax.broadcasted_iota(jnp.int32, (EXTRA, rows), 0)
        source = lax.broadcasted_iota(jnp.int32, (EXTRA, rows), 1) // per
        pick = jnp.where(source == slot, 1.0, 0.0).astype(BF)
        logs = jnp.dot(pick, term.astype(BF), preferred_element_type=F32)
        o_ref[rows:, :] = logs.astype(BF)

    count = keys // block
    steps = block // chunk

    def middle(part):
        weights = jnp.exp2(part - jnp.max(part, axis=1, keepdims=True))
        total = jnp.sum(weights, axis=1, keepdims=True)
        return jnp.sum(weights * part, axis=1, keepdims=True) / total

    def accumulate(a, j):
        slot = (a * count + j) % 2
        part = jnp.dot(weight_ref[slot], values(a, j), preferred_element_type=F32)
        if j == 0:
            acc_ref[a] = part
        else:
            acc_ref[a] += part

    shifts = []
    before = None
    for a in range(heads):
        for j in range(count):
            slot = (a * count + j) % 2
            for c in range(steps):
                first = j * block + c * chunk
                part = jnp.dot(
                    queries[a], k_ref[a, :, first : first + chunk], preferred_element_type=F32
                )
                if first == 0:
                    shifts.append(middle(part * scale))
                weights = jnp.exp2((part * scale - shifts[a]).astype(BF))
                weight_ref[slot, :, c * chunk : (c + 1) * chunk] = weights
            if before is not None:
                accumulate(*before)
            before = (a, j)
    accumulate(*before)
    finish(shifts)
    fits = jnp.max(acc_ref[:, :, dim:]) < LIMIT

    @pl.when(jnp.logical_not(fits))
    def _():
        acc_ref[...] = jnp.zeros_like(acc_ref)
        tops = []
        for a in range(heads):

            def step(j, top):
                part = scores(a, j) * scale
                new = jnp.maximum(top, jnp.max(part, axis=1, keepdims=True))
                weights = jnp.exp2(part - new).astype(BF)
                acc_ref[a] = acc_ref[a] * jnp.exp2(top - new) + jnp.dot(
                    weights, values(a, j), preferred_element_type=F32
                )
                return new

            tops.append(lax.fori_loop(0, count, step, jnp.full((each, 1), -1e30, F32)))
        finish(tops)


def attend(q, keys_t, values, blocks, capacity, group):
    rows, dim = q.shape[0] // blocks, q.shape[1]
    heads, count, _ = values.shape
    block = min(1024, count)
    chunk = min(256, block)
    return pl.pallas_call(
        functools.partial(attend_kernel, capacity, group, block, chunk),
        out_shape=jax.ShapeDtypeStruct((blocks * (rows + EXTRA), dim), BF),
        grid=(blocks,),
        in_specs=[
            pl.BlockSpec((rows, dim), lambda i: (i, 0)),
            pl.BlockSpec(keys_t.shape, lambda i: (0, 0, 0)),
            pl.BlockSpec(values.shape, lambda i: (0, 0, 0)),
        ],
        out_specs=pl.BlockSpec((rows + EXTRA, dim), lambda i: (i, 0)),
        scratch_shapes=[
            pltpu.VMEM((heads, rows // heads, 2 * dim), F32),
            pltpu.VMEM((2, rows // heads, block), BF),
        ],
        compiler_params=params(),
        cost_estimate=pl.CostEstimate(
            flops=8 * blocks * rows * count * dim,
            bytes_accessed=5 << 20,
            transcendentals=blocks * rows * count,
        ),
        name="attend_prefix",
    )(q, keys_t, values)


def visibility(lengths, draft_count, suffix_count):
    position = jnp.arange(suffix_count + draft_count, dtype=jnp.int32)
    draft_pos = jnp.arange(draft_count, dtype=jnp.int32)
    earlier = position[None, None, :] < lengths[:, None, None]
    earlier = earlier & (position[None, None, :] < suffix_count)
    fresh = (position[None, :] >= suffix_count) & (
        position[None, :] - suffix_count <= draft_pos[:, None]
    )
    return earlier | fresh[None, :, :]


def local_attention(query_grid, key_rows, value_rows, visible):
    scale = query_grid.shape[-1] ** (-0.5)
    scores = (
        jnp.einsum("rtagd,rjad->rtagj", query_grid, key_rows, preferred_element_type=F32) * scale
    )
    visible_mask = visible[:, :, None, None, :]
    scores = jnp.where(visible_mask, scores, F32(-1e30))
    top = jnp.max(scores, axis=-1)
    exponent = jnp.where(visible_mask, jnp.exp(scores - top[..., None]), F32(0.0))
    denominator = jnp.sum(exponent, axis=-1)
    summed = jnp.einsum(
        "rtagj,rjad->rtagd", exponent.astype(BF), value_rows, preferred_element_type=F32
    )
    return summed / denominator[..., None], (top + jnp.log(denominator)) * F32(math.log2(math.e))


def join_kernel(capacity, count, base, order, target, own, *refs):
    del own
    received, refs = refs[:count], refs[count:]
    local, local_log, weight, send, keep, blocks, block_logs, part, mine, logs, spread, att = refs
    rows, per, dim = part.shape
    held = capacity * per
    heads = att.shape[1] // dim
    draft = per // heads

    @pl.when(pl.program_id(0) == 0)
    def _():
        done = 0
        for array in received:
            for first in range(0, array.shape[0], held + EXTRA):
                values = array[first : first + held, :].astype(F32)
                blocks[done * capacity : (done + 1) * capacity] = values.reshape(capacity, per, dim)
                last = array[first + held : first + held + EXTRA, :].astype(F32)
                block_logs[done * EXTRA : (done + 1) * EXTRA] = last
                done += 1

        def gather(i, _):
            at = order[base + i]
            slot = target[base + i]
            part[i] = blocks[slot]
            mine[i] = local[at]
            place = (slot // capacity) * EXTRA + slot % capacity
            logs[0, pl.ds(i, 1), :] = block_logs[pl.ds(place, 1), :]
            logs[1, pl.ds(i, 1), :] = local_log[pl.ds(at, 1), :]
            return 0

        lax.fori_loop(0, rows, gather, 0)
        lane = lax.broadcasted_iota(jnp.int32, (rows, dim), 1)
        first = logs[0] + pltpu.roll(logs[0], dim - per, axis=1)
        share = 1.0 / (1.0 + jnp.exp2(logs[1] - first))
        high = share.astype(BF).astype(F32)
        low = pltpu.roll(share - high, per, axis=1)
        logs[0] = jnp.where(lane < per, high, jnp.where(lane < 2 * per, low, 0.0))
        diagonal = lax.broadcasted_iota(jnp.int32, (per, dim), 1) % per
        diagonal = diagonal == lax.broadcasted_iota(jnp.int32, (per, dim), 0)

        def widen(i, _):
            row = logs[0, pl.ds(i, 1), :]
            spread[i] = jnp.where(diagonal, row, 0.0).astype(BF)
            return 0

        lax.fori_loop(0, rows, widen, 0)
        ones = jnp.ones((dim, dim), BF)
        shares = jnp.dot(
            spread[...].reshape(rows * per, dim), ones, preferred_element_type=F32
        ).reshape(rows, per, dim)
        mixed = mine[...] + shares * (part[...] - mine[...])
        part[...] = mixed
        flat = part.reshape(rows * per, dim)
        for h in range(heads):
            head = flat[pl.ds(h, rows * draft, stride=heads), :]
            att[:, h * dim : (h + 1) * dim] = head.astype(BF)

    product = jnp.dot(att[...], weight[...], preferred_element_type=F32).astype(BF)
    for out, wanted in ((send, True), (keep, False)):

        @pl.when((pl.program_id(0) < pl.num_programs(0) // 2) == wanted)
        def _():
            out[...] = product


def join(received, local, local_log, order, target, own, weight, base, rows, capacity):
    count = len(received)
    per, dim = local.shape[1:]
    blocks = sum(array.shape[0] for array in received) // (capacity * per + EXTRA)
    depth, width = weight.shape
    draft = per * dim // depth
    block = 512
    groups = lax.axis_size("tensor")
    each = width // groups // block
    half = width // block // 2

    def column(n, order, target, own):
        place = n // each
        chips = groups // 2
        core = jnp.where(place < chips, 1 - own[0] % 2, own[0] % 2)
        shard = 2 * (place % chips) + core
        return (0, shard * each + n % each)

    whole = lambda array: pl.BlockSpec(array.shape, lambda n, *_: (0,) * array.ndim)
    return pl.pallas_call(
        functools.partial(join_kernel, capacity, count, base),
        out_shape=[jax.ShapeDtypeStruct((rows * draft, width // 2), BF)] * 2,
        grid_spec=pltpu.PrefetchScalarGridSpec(
            num_scalar_prefetch=3,
            grid=(2 * half,),
            in_specs=[whole(array) for array in received]
            + [whole(local), whole(local_log), pl.BlockSpec((depth, block), column)],
            out_specs=[
                pl.BlockSpec((rows * draft, block), lambda n, *_: (0, jnp.minimum(n, half - 1))),
                pl.BlockSpec((rows * draft, block), lambda n, *_: (0, jnp.maximum(n - half, 0))),
            ],
            scratch_shapes=[
                pltpu.VMEM((blocks * capacity, per, dim), F32),
                pltpu.VMEM((blocks * EXTRA, dim), F32),
                pltpu.VMEM((rows, per, dim), F32),
                pltpu.VMEM((rows, per, dim), F32),
                pltpu.VMEM((2, rows, dim), F32),
                pltpu.VMEM((rows, per, dim), BF),
                pltpu.VMEM((rows * draft, depth), BF),
            ],
        ),
        compiler_params=params(),
        cost_estimate=pl.CostEstimate(
            flops=2 * rows * draft * depth * width, bytes_accessed=24 << 20, transcendentals=0
        ),
        name="join_project",
    )(order, target, own, *received, local, local_log, weight)


def scatter_sum(send, keep, own):
    size = lax.axis_size("tensor")
    chips = size // 2
    width = keep.shape[1] // chips
    there = lax.ppermute(send, "tensor", [(i, i ^ 1) for i in range(size)])
    both = keep.astype(F32) + there.astype(F32)
    shares = [both[:, c * width : (c + 1) * width] for c in range(chips)]
    chip = own // 2

    def share_of(index):
        picked = shares[0]
        for c in range(1, chips):
            picked = jnp.where(index == c, shares[c], picked)
        return picked

    terms = [share_of(chip)]
    for d in range(1, chips):
        pairs = [(i, i ^ (2 * d)) for i in range(size)]
        terms.append(lax.ppermute(share_of(chip ^ d).astype(BF), "tensor", pairs))
    return terms


def arrange_kernel(counts, place_ref, *refs):
    out_ref = refs[-1]
    rows, draft, _ = out_ref.shape
    halves, start = [], 0
    for count in counts:
        total = refs[start][...]
        for term in refs[start + 1 : start + count]:
            total = total + term[...].astype(F32)
        halves.append(total.astype(BF))
        start += count
    values = jnp.concatenate(halves, axis=0)
    size = rows * draft
    pick = lax.broadcasted_iota(jnp.int32, (size, size), 1) == place_ref[...]
    result = jnp.dot(
        jnp.where(pick, 1.0, 0.0).astype(BF), values, preferred_element_type=F32
    )
    for r in range(rows):
        out_ref[r] = result[r * draft : (r + 1) * draft].astype(BF)


def arrange(halves, place, rows, draft):
    width = halves[0][0].shape[1]
    index = (place[:, None] * draft + jnp.arange(draft, dtype=jnp.int32)[None, :]).reshape(-1, 1)
    return pl.pallas_call(
        functools.partial(arrange_kernel, [len(half) for half in halves]),
        out_shape=jax.ShapeDtypeStruct((rows, draft, width), BF),
        compiler_params=params(),
        cost_estimate=pl.CostEstimate(flops=0, bytes_accessed=3 << 20, transcendentals=0),
        name="arrange_rows",
    )(index, *[term for half in halves for term in half])


def after(first, *values):
    return lax.optimization_barrier((first,) + values)[1:]


def exchange(x):
    size = lax.axis_size("dp")
    groups = [list(range(size // 2)), list(range(size // 2, size))]
    return lax.all_to_all(
        x, "dp", split_axis=0, concat_axis=0, axis_index_groups=groups, tiled=True
    )


def hop(x, shift):
    size = lax.axis_size("dp")
    return lax.ppermute(x, "dp", [(i, i ^ shift) for i in range(size)])


def body(
    queries,
    draft_keys,
    draft_values,
    suffix_keys,
    suffix_values,
    suffix_len,
    prefix_keys,
    prefix_values,
    row_prefix,
    prefix_slot,
    out_weight,
):
    row_count, draft, query_heads, dim = queries.shape
    heads = draft_keys.shape[2]
    group = query_heads // heads
    per = draft * query_heads
    suffix_count = suffix_keys.shape[1]
    peers = lax.axis_size("dp")
    capacity = 2 * row_count // peers
    own = lax.axis_index("tensor").astype(jnp.int32)
    me = lax.axis_index("dp").astype(jnp.int32)

    slot_row, place, order, target = route(row_prefix, prefix_slot, me, peers, capacity)
    half = peers // 2
    far = pack(queries, slot_row, half, half, capacity, False)
    near_rows, far[0] = lax.optimization_barrier((slot_row, far[0]))
    (near,) = pack(queries, near_rows, 0, half, capacity, True)
    far = [hop(far[d], half + d) for d in range(half)]
    near = exchange(near)

    keys_t, values = split_heads(prefix_keys[0], prefix_values[0])
    last = attend(near, keys_t, values, half, capacity, group)
    back = [exchange(last)]
    for d in range(half):
        (query,) = after(last, far[d])
        last = attend(query, keys_t, values, 1, capacity, group)
        back.append(hop(last, half + d))

    query_grid = queries.reshape(row_count, draft, heads, group, dim)
    all_keys = jnp.concatenate([suffix_keys, draft_keys], axis=1)
    all_values = jnp.concatenate([suffix_values, draft_values], axis=1)
    visible = visibility(suffix_len, draft, suffix_count)
    local, local_log = local_attention(query_grid, all_keys, all_values, visible)
    local = local.reshape(row_count, per, dim)
    local_log = jnp.pad(local_log.reshape(row_count, per), ((0, 0), (0, dim - per)))

    rows = row_count // 2
    early = 1 + half - rows // capacity
    outs = []
    for base in (0, rows):
        received = back if base else back[:early]
        send, keep = join(
            received, local, local_log, order, target, own.reshape(1), out_weight, base, rows, capacity
        )
        if base == 0:
            send, back[early:] = lax.optimization_barrier((send, back[early:]))
        outs.append(scatter_sum(send, keep, own))
    return arrange(outs, place, row_count, draft)


def solution(mesh):
    placed = (
        P("dp", None, "tensor", None),
        P("dp", None, "tensor", None),
        P("dp", None, "tensor", None),
        P("dp", None, "tensor", None),
        P("dp", None, "tensor", None),
        P("dp"),
        P("dp", None, "tensor", None),
        P("dp", None, "tensor", None),
        P("dp", None),
        P(),
        P("tensor", None),
    )
    return jax.shard_map(
        body, mesh=mesh, in_specs=placed, out_specs=P("dp", None, "tensor"), check_vma=False
    )
```

```python
import functools
import math

import jax
import jax.numpy as jnp
from jax import lax
from jax.experimental import pallas as pl
from jax.experimental.pallas import tpu as pltpu
from jax.sharding import PartitionSpec as P

BF = jnp.bfloat16
F32 = jnp.float32
EXTRA = 16
LIMIT = 1e30


def params(mebibytes):
    return pltpu.CompilerParams(vmem_limit_bytes=mebibytes * 1024 * 1024)


def route(row_prefix, prefix_slot, me, peers, capacity):
    rows = row_prefix.shape[0]
    prefixes = prefix_slot.shape[0]
    name = row_prefix[:, 0]
    row = jnp.arange(rows, dtype=jnp.int32)
    owner = jnp.sum(
        jnp.where(
            row_prefix == jnp.arange(prefixes, dtype=jnp.int32)[None, :], prefix_slot[None, :], 0
        ),
        axis=1,
    )
    same = (name[:, None] == name[None, :]) & (row[None, :] < row[:, None])
    rank = jnp.sum(same.astype(jnp.int32), axis=1)
    half = peers // 2
    shift = owner ^ me
    target = jnp.where(shift < half, owner % half, shift) * capacity + rank
    slots = jnp.arange(peers * capacity, dtype=jnp.int32)
    slot_row = jnp.sum(jnp.where(target[None, :] == slots[:, None], row[None, :], 0), axis=1)
    place = jnp.sum((target[None, :] < target[:, None]).astype(jnp.int32), axis=1)
    at = place[None, :] == row[:, None]
    order = jnp.sum(jnp.where(at, row[None, :], 0), axis=1)
    order_target = jnp.sum(jnp.where(at, target[None, :], 0), axis=1)
    return slot_row, place, order, order_target


def pack_kernel(pieces, capacity, slot_row, q_ref, *refs):
    outs = refs[-len(pieces) :]

    def one(k, _):
        for (first, blocks), out in zip(pieces, outs):
            for b in range(blocks):
                out[b * capacity + k] = q_ref[slot_row[(first + b) * capacity + k]]
        return 0

    lax.fori_loop(0, capacity, one, 0)


def pack(queries, slot_row, pieces, capacity, *before):
    shapes = [
        jax.ShapeDtypeStruct((blocks * capacity,) + queries.shape[1:], BF) for _, blocks in pieces
    ]
    whole = lambda array: pl.BlockSpec(array.shape, lambda i, s: (0, 0, 0, 0))
    packed = pl.pallas_call(
        functools.partial(pack_kernel, pieces, capacity),
        out_shape=shapes,
        grid_spec=pltpu.PrefetchScalarGridSpec(
            num_scalar_prefetch=1,
            grid=(1,),
            in_specs=[whole(queries)] + [pl.BlockSpec(memory_space=pl.ANY)] * len(before),
            out_specs=[whole(shape) for shape in shapes],
        ),
        compiler_params=params(16),
        cost_estimate=pl.CostEstimate(flops=0, bytes_accessed=4 << 20, transcendentals=0),
        name="pack_queries",
    )(slot_row, queries, *before)
    return [x.reshape(-1, x.shape[-1]) for x in packed]


def split_kernel(heads, k_ref, v_ref, kt_ref, vs_ref, wide):
    count = v_ref.shape[0] // heads
    for source, is_key in ((k_ref, True), (v_ref, False)):
        wide[...] = source[...].astype(F32)
        for a in range(heads):
            part = wide[pl.ds(a, count, stride=heads), :]
            if is_key:
                kt_ref[a] = part.T.astype(BF)
            else:
                vs_ref[a] = part.astype(BF)


def split_heads(keys, values):
    count, heads, dim = keys.shape
    steps = 4
    each = count // steps
    rows = pl.BlockSpec((each * heads, dim), lambda i: (i, 0))
    return pl.pallas_call(
        functools.partial(split_kernel, heads),
        out_shape=[
            jax.ShapeDtypeStruct((heads, dim, count), BF),
            jax.ShapeDtypeStruct((heads, count, dim), BF),
        ],
        grid=(steps,),
        in_specs=[rows, rows],
        out_specs=[
            pl.BlockSpec((heads, dim, each), lambda i: (0, 0, i)),
            pl.BlockSpec((heads, each, dim), lambda i: (0, i, 0)),
        ],
        scratch_shapes=[pltpu.VMEM((each * heads, dim), F32)],
        compiler_params=params(20),
        cost_estimate=pl.CostEstimate(flops=0, bytes_accessed=8 << 20, transcendentals=0),
        name="split_heads",
    )(keys.reshape(count * heads, dim), values.reshape(count * heads, dim))


def attend_kernel(capacity, group, block, chunk, q_ref, k_ref, v_ref, *refs):
    o_ref, acc_ref, weight_ref = refs[-3:]
    heads, dim, keys = k_ref.shape
    rows = q_ref.shape[0]
    per = rows // capacity
    each = rows // heads
    scale = dim**-0.5 * math.log2(math.e)
    ones = jnp.ones((block, dim), BF)
    grid = q_ref[...].astype(F32).reshape(rows // (heads * group), heads, group, dim)
    queries = [grid[:, a].reshape(each, dim).astype(BF) for a in range(heads)]

    def scores(a, j):
        part = k_ref[a, :, pl.ds(j * block, block)]
        return jnp.dot(queries[a], part, preferred_element_type=F32)

    def values(a, j):
        return jnp.concatenate([v_ref[a, pl.ds(j * block, block), :], ones], axis=1)

    def natural(parts):
        split = [x.reshape(each // group, 1, group, dim) for x in parts]
        return jnp.concatenate(split, axis=1).reshape(rows, dim)

    def finish(shifts):
        sums = [acc_ref[a, :, dim:] for a in range(heads)]
        out = [acc_ref[a, :, :dim] / sums[a] for a in range(heads)]
        o_ref[:rows, :] = natural(out).astype(BF)
        log_sum = natural([shifts[a] + jnp.log2(sums[a]) for a in range(heads)])
        high = log_sum.astype(BF).astype(F32)
        lane = lax.broadcasted_iota(jnp.int32, (rows, dim), 1)
        row = lax.broadcasted_iota(jnp.int32, (rows, dim), 0)
        term = jnp.where(lane < per, high, log_sum - high)
        term = jnp.where((lane % per == row % per) & (lane < 2 * per), term, 0.0)
        slot = lax.broadcasted_iota(jnp.int32, (EXTRA, rows), 0)
        source = lax.broadcasted_iota(jnp.int32, (EXTRA, rows), 1) // per
        pick = jnp.where(source == slot, 1.0, 0.0).astype(BF)
        logs = jnp.dot(pick, term.astype(BF), preferred_element_type=F32)
        o_ref[rows:, :] = logs.astype(BF)

    count = keys // block
    steps = block // chunk

    def middle(part):
        weights = jnp.exp2(part - jnp.max(part, axis=1, keepdims=True))
        total = jnp.sum(weights, axis=1, keepdims=True)
        return jnp.sum(weights * part, axis=1, keepdims=True) / total

    def accumulate(a, j):
        slot = (a * count + j) % 2
        part = jnp.dot(weight_ref[slot], values(a, j), preferred_element_type=F32)
        if j == 0:
            acc_ref[a] = part
        else:
            acc_ref[a] += part

    shifts = []
    before = None
    for a in range(heads):
        for j in range(count):
            slot = (a * count + j) % 2
            for c in range(steps):
                first = j * block + c * chunk
                part = jnp.dot(
                    queries[a], k_ref[a, :, first : first + chunk], preferred_element_type=F32
                )
                if first == 0:
                    shifts.append(middle(part * scale))
                weights = jnp.exp2((part * scale - shifts[a]).astype(BF))
                weight_ref[slot, :, c * chunk : (c + 1) * chunk] = weights
            if before is not None:
                accumulate(*before)
            before = (a, j)
    accumulate(*before)
    finish(shifts)
    fits = jnp.max(acc_ref[:, :, dim:]) < LIMIT

    @pl.when(jnp.logical_not(fits))
    def _():
        acc_ref[...] = jnp.zeros_like(acc_ref)
        tops = []
        for a in range(heads):

            def step(j, top):
                part = scores(a, j) * scale
                new = jnp.maximum(top, jnp.max(part, axis=1, keepdims=True))
                weights = jnp.exp2(part - new).astype(BF)
                acc_ref[a] = acc_ref[a] * jnp.exp2(top - new) + jnp.dot(
                    weights, values(a, j), preferred_element_type=F32
                )
                return new

            tops.append(lax.fori_loop(0, count, step, jnp.full((each, 1), -1e30, F32)))
        finish(tops)


def attend(q, keys_t, values, blocks, capacity, group, *before):
    rows, dim = q.shape[0] // blocks, q.shape[1]
    heads, count, _ = values.shape
    block = min(1024, count)
    chunk = min(256, block)
    return pl.pallas_call(
        functools.partial(attend_kernel, capacity, group, block, chunk),
        out_shape=jax.ShapeDtypeStruct((blocks * (rows + EXTRA), dim), BF),
        grid=(blocks,),
        in_specs=[
            pl.BlockSpec((rows, dim), lambda i: (i, 0)),
            pl.BlockSpec(keys_t.shape, lambda i: (0, 0, 0)),
            pl.BlockSpec(values.shape, lambda i: (0, 0, 0)),
        ]
        + [pl.BlockSpec(memory_space=pl.ANY)] * len(before),
        out_specs=pl.BlockSpec((rows + EXTRA, dim), lambda i: (i, 0)),
        scratch_shapes=[
            pltpu.VMEM((heads, rows // heads, 2 * dim), F32),
            pltpu.VMEM((2, rows // heads, block), BF),
        ],
        compiler_params=params(28),
        cost_estimate=pl.CostEstimate(
            flops=8 * blocks * rows * count * dim,
            bytes_accessed=5 << 20,
            transcendentals=blocks * rows * count,
        ),
        name="attend_prefix",
    )(q, keys_t, values, *before)


def visibility(lengths, draft_count, suffix_count):
    position = jnp.arange(suffix_count + draft_count, dtype=jnp.int32)
    draft_pos = jnp.arange(draft_count, dtype=jnp.int32)
    earlier = position[None, None, :] < lengths[:, None, None]
    earlier = earlier & (position[None, None, :] < suffix_count)
    fresh = (position[None, :] >= suffix_count) & (
        position[None, :] - suffix_count <= draft_pos[:, None]
    )
    return earlier | fresh[None, :, :]


def local_attention(query_grid, key_rows, value_rows, visible):
    scale = query_grid.shape[-1] ** (-0.5)
    scores = (
        jnp.einsum("rtagd,rjad->rtagj", query_grid, key_rows, preferred_element_type=F32) * scale
    )
    visible_mask = visible[:, :, None, None, :]
    scores = jnp.where(visible_mask, scores, F32(-1e30))
    top = jnp.max(scores, axis=-1)
    exponent = jnp.where(visible_mask, jnp.exp(scores - top[..., None]), F32(0.0))
    denominator = jnp.sum(exponent, axis=-1)
    summed = jnp.einsum(
        "rtagj,rjad->rtagd", exponent.astype(BF), value_rows, preferred_element_type=F32
    )
    return summed / denominator[..., None], (top + jnp.log(denominator)) * F32(math.log2(math.e))


def join_kernel(capacity, count, base, order, target, *refs):
    received, (local, local_log) = refs[:count], refs[count : count + 2]
    att, blocks, block_logs, part, mine, logs, spread = refs[-7:]
    rows, per, dim = part.shape
    held = capacity * per
    heads = att.shape[1] // dim
    draft = per // heads
    done = 0
    for array in received:
        for first in range(0, array.shape[0], held + EXTRA):
            values = array[first : first + held, :].astype(F32)
            blocks[done * capacity : (done + 1) * capacity] = values.reshape(capacity, per, dim)
            last = array[first + held : first + held + EXTRA, :].astype(F32)
            block_logs[done * EXTRA : (done + 1) * EXTRA] = last
            done += 1

    def gather(i, _):
        at = order[base + i]
        slot = target[base + i]
        part[i] = blocks[slot]
        mine[i] = local[at].astype(F32)
        place = (slot // capacity) * EXTRA + slot % capacity
        logs[0, pl.ds(i, 1), :] = block_logs[pl.ds(place, 1), :]
        logs[1, pl.ds(i, 1), :] = local_log[pl.ds(at, 1), :]
        return 0

    lax.fori_loop(0, rows, gather, 0)
    lane = lax.broadcasted_iota(jnp.int32, (rows, dim), 1)
    first = logs[0] + pltpu.roll(logs[0], dim - per, axis=1)
    share = 1.0 / (1.0 + jnp.exp2(logs[1] - first))
    high = share.astype(BF).astype(F32)
    low = pltpu.roll(share - high, per, axis=1)
    logs[0] = jnp.where(lane < per, high, jnp.where(lane < 2 * per, low, 0.0))
    diagonal = lax.broadcasted_iota(jnp.int32, (per, dim), 1) % per
    diagonal = diagonal == lax.broadcasted_iota(jnp.int32, (per, dim), 0)

    def widen(i, _):
        row = logs[0, pl.ds(i, 1), :]
        spread[i] = jnp.where(diagonal, row, 0.0).astype(BF)
        return 0

    lax.fori_loop(0, rows, widen, 0)
    ones = jnp.ones((dim, dim), BF)
    shares = jnp.dot(
        spread[...].reshape(rows * per, dim), ones, preferred_element_type=F32
    ).reshape(rows, per, dim)
    part[...] = mine[...] + shares * (part[...] - mine[...])
    flat = part.reshape(rows * per, dim)
    for h in range(heads):
        head = flat[pl.ds(h, rows * draft, stride=heads), :]
        att[:, h * dim : (h + 1) * dim] = head.astype(BF)


def join(received, local, local_log, order, target, heads, base, rows, capacity, *before):
    count = len(received)
    per, dim = local.shape[1:]
    blocks = sum(array.shape[0] for array in received) // (capacity * per + EXTRA)
    whole = lambda array: pl.BlockSpec(array.shape, lambda n, *_: (0,) * array.ndim)
    shape = jax.ShapeDtypeStruct((rows * per // heads, heads * dim), BF)
    return pl.pallas_call(
        functools.partial(join_kernel, capacity, count, base),
        out_shape=shape,
        grid_spec=pltpu.PrefetchScalarGridSpec(
            num_scalar_prefetch=2,
            grid=(1,),
            in_specs=[whole(array) for array in received]
            + [whole(local), whole(local_log)]
            + [pl.BlockSpec(memory_space=pl.ANY)] * len(before),
            out_specs=whole(shape),
            scratch_shapes=[
                pltpu.VMEM((blocks * capacity, per, dim), F32),
                pltpu.VMEM((blocks * EXTRA, dim), F32),
                pltpu.VMEM((rows, per, dim), F32),
                pltpu.VMEM((rows, per, dim), F32),
                pltpu.VMEM((2, rows, dim), F32),
                pltpu.VMEM((rows, per, dim), BF),
            ],
        ),
        compiler_params=params(36),
        cost_estimate=pl.CostEstimate(flops=0, bytes_accessed=12 << 20, transcendentals=0),
        name="join_parts",
    )(order, target, *received, local, local_log, *before)


def project_kernel(each, count, shards, att, weight, *refs):
    del shards
    outs = refs[-count:]
    product = jnp.dot(att[...], weight[...], preferred_element_type=F32).astype(BF)
    for k, out in enumerate(outs):

        @pl.when(pl.program_id(0) // each == k)
        def _():
            out[...] = product


def project(att, weight, shards, width, *before):
    rows, depth = att.shape
    count = shards.shape[0]
    block = min(512, width)
    each = width // block
    place = lambda k: lambda n, s: (0, jnp.clip(n - k * each, 0, each - 1))
    return pl.pallas_call(
        functools.partial(project_kernel, each, count),
        out_shape=[jax.ShapeDtypeStruct((rows, width), BF)] * count,
        grid_spec=pltpu.PrefetchScalarGridSpec(
            num_scalar_prefetch=1,
            grid=(count * each,),
            in_specs=[
                pl.BlockSpec((rows, depth), lambda n, s: (0, 0)),
                pl.BlockSpec((depth, block), lambda n, s: (0, s[n // each] * each + n % each)),
            ]
            + [pl.BlockSpec(memory_space=pl.ANY)] * len(before),
            out_specs=[pl.BlockSpec((rows, block), place(k)) for k in range(count)],
        ),
        compiler_params=params(20),
        cost_estimate=pl.CostEstimate(
            flops=2 * rows * depth * width * count,
            bytes_accessed=2 * depth * width * count,
            transcendentals=0,
        ),
        name="project",
    )(shards, att, weight, *before)


def project_shares(att, weight, own, split, *before):
    size = lax.axis_size("tensor")
    chips = size // 2
    width = weight.shape[1] // size
    pairs = [jnp.stack([own ^ (2 * d + 1), own ^ (2 * d)]) for d in list(range(1, chips)) + [0]]
    if split:
        return [project(att, weight, pair, width, *before) for pair in pairs]
    flat = project(att, weight, jnp.concatenate(pairs), width)
    return [flat[2 * k : 2 * k + 2] for k in range(chips)]


def sum_shares(products):
    size = lax.axis_size("tensor")
    terms, sent = [], []
    for d, (send, keep) in zip(list(range(1, size // 2)) + [0], products):
        there = lax.ppermute(send, "tensor", [(i, i ^ 1) for i in range(size)])
        total = keep.astype(F32) + there.astype(F32)
        if d:
            sent.append(total.astype(BF))
            total = lax.ppermute(sent[-1], "tensor", [(i, i ^ (2 * d)) for i in range(size)])
        terms.append(total)
    return terms[::-1], sent


def arrange_kernel(counts, place_ref, *refs):
    out_ref = refs[-1]
    rows, draft, _ = out_ref.shape
    halves, start = [], 0
    for count in counts:
        total = refs[start][...]
        for term in refs[start + 1 : start + count]:
            total = total + term[...].astype(F32)
        halves.append(total.astype(BF))
        start += count
    values = jnp.concatenate(halves, axis=0)
    size = rows * draft
    pick = lax.broadcasted_iota(jnp.int32, (size, size), 1) == place_ref[...]
    result = jnp.dot(
        jnp.where(pick, 1.0, 0.0).astype(BF), values, preferred_element_type=F32
    )
    for r in range(rows):
        out_ref[r] = result[r * draft : (r + 1) * draft].astype(BF)


def arrange(halves, place, rows, draft):
    width = halves[0][0].shape[1]
    index = (place[:, None] * draft + jnp.arange(draft, dtype=jnp.int32)[None, :]).reshape(-1, 1)
    return pl.pallas_call(
        functools.partial(arrange_kernel, [len(half) for half in halves]),
        out_shape=jax.ShapeDtypeStruct((rows, draft, width), BF),
        compiler_params=params(20),
        cost_estimate=pl.CostEstimate(flops=0, bytes_accessed=3 << 20, transcendentals=0),
        name="arrange_rows",
    )(index, *[term for half in halves for term in half])


def exchange(x):
    size = lax.axis_size("dp")
    groups = [list(range(size // 2)), list(range(size // 2, size))]
    return lax.all_to_all(
        x, "dp", split_axis=0, concat_axis=0, axis_index_groups=groups, tiled=True
    )


def hop(x, shift):
    size = lax.axis_size("dp")
    return lax.ppermute(x, "dp", [(i, i ^ shift) for i in range(size)])


def body(
    queries,
    draft_keys,
    draft_values,
    suffix_keys,
    suffix_values,
    suffix_len,
    prefix_keys,
    prefix_values,
    row_prefix,
    prefix_slot,
    out_weight,
):
    row_count, draft, query_heads, dim = queries.shape
    heads = draft_keys.shape[2]
    group = query_heads // heads
    per = draft * query_heads
    suffix_count = suffix_keys.shape[1]
    peers = lax.axis_size("dp")
    capacity = 2 * row_count // peers
    own = lax.axis_index("tensor").astype(jnp.int32)
    me = lax.axis_index("dp").astype(jnp.int32)

    slot_row, place, order, target = route(row_prefix, prefix_slot, me, peers, capacity)
    half = peers // 2
    lead = half // 2
    first = pack(queries, slot_row, [(half + d, 1) for d in range(lead)], capacity)
    near, *late = pack(
        queries,
        slot_row,
        [(0, half)] + [(half + d, 1) for d in range(lead, half)],
        capacity,
        first[0],
    )
    far = [hop(x, half + d) for d, x in enumerate(first + late)]
    near = exchange(near)

    keys_t, values = split_heads(prefix_keys[0], prefix_values[0])
    back, before = [None] * (half + 1), []
    for d in list(range(lead)) + [-1] + list(range(lead, half)):
        query, blocks = (near, half) if d < 0 else (far[d], 1)
        result = attend(query, keys_t, values, blocks, capacity, group, *before)
        before = [result]
        back[d + 1] = exchange(result) if d < 0 else hop(result, half + d)

    query_grid = queries.reshape(row_count, draft, heads, group, dim)
    all_keys = jnp.concatenate([suffix_keys, draft_keys], axis=1)
    all_values = jnp.concatenate([suffix_values, draft_values], axis=1)
    visible = visibility(suffix_len, draft, suffix_count)
    local, local_log = local_attention(query_grid, all_keys, all_values, visible)
    local = local.reshape(row_count, per, dim).astype(BF)
    local_log = jnp.pad(local_log.reshape(row_count, per), ((0, 0), (0, dim - per)))

    rows = row_count // 2
    early = 1 + half - rows // capacity
    outs, sent = [], []
    for base in (0, rows):
        received = back if base else back[:early]
        att = join(
            received, local, local_log, order, target, query_heads, base, rows, capacity, *before
        )
        products = project_shares(att, out_weight, own, base > 0, *sent)
        before = [products[0][0]]
        terms, sent = sum_shares(products)
        outs.append(terms)
    return arrange(outs, place, row_count, draft)


def solution(mesh):
    placed = (
        P("dp", None, "tensor", None),
        P("dp", None, "tensor", None),
        P("dp", None, "tensor", None),
        P("dp", None, "tensor", None),
        P("dp", None, "tensor", None),
        P("dp"),
        P("dp", None, "tensor", None),
        P("dp", None, "tensor", None),
        P("dp", None),
        P(),
        P("tensor", None),
    )
    return jax.shard_map(
        body, mesh=mesh, in_specs=placed, out_specs=P("dp", None, "tensor"), check_vma=False
    )
```

```python
import functools
import math

import jax
import jax.numpy as jnp
from jax import lax
from jax.experimental import pallas as pl
from jax.experimental.pallas import tpu as pltpu
from jax.sharding import PartitionSpec as P

BF = jnp.bfloat16
F32 = jnp.float32
EXTRA = 16
LIMIT = 1e30
SMALL = pl.CostEstimate(flops=1 << 20, bytes_accessed=1 << 10, transcendentals=0)


def params(mebibytes):
    return pltpu.CompilerParams(vmem_limit_bytes=mebibytes * 1024 * 1024)


def route(row_prefix, prefix_slot, me, peers, capacity):
    rows = row_prefix.shape[0]
    prefixes = prefix_slot.shape[0]
    name = row_prefix[:, 0]
    row = jnp.arange(rows, dtype=jnp.int32)
    owner = jnp.sum(
        jnp.where(
            row_prefix == jnp.arange(prefixes, dtype=jnp.int32)[None, :], prefix_slot[None, :], 0
        ),
        axis=1,
    )
    same = (name[:, None] == name[None, :]) & (row[None, :] < row[:, None])
    rank = jnp.sum(same.astype(jnp.int32), axis=1)
    half = peers // 2
    shift = owner ^ me
    sent = jnp.where(shift < half, owner % half, shift) * capacity + rank
    target = shift * capacity + rank
    slots = jnp.arange(peers * capacity, dtype=jnp.int32)
    slot_row = jnp.sum(jnp.where(sent[None, :] == slots[:, None], row[None, :], 0), axis=1)
    place = jnp.sum((target[None, :] < target[:, None]).astype(jnp.int32), axis=1)
    at = place[None, :] == row[:, None]
    order = jnp.sum(jnp.where(at, row[None, :], 0), axis=1)
    order_target = jnp.sum(jnp.where(at, target[None, :], 0), axis=1)
    return slot_row, place, order, order_target


def pack_kernel(pieces, capacity, slot_row, q_ref, *refs):
    outs = refs[-len(pieces) :]

    def one(k, _):
        for (first, blocks), out in zip(pieces, outs):
            for b in range(blocks):
                out[b * capacity + k] = q_ref[slot_row[(first + b) * capacity + k]]
        return 0

    lax.fori_loop(0, capacity, one, 0)


def pack(queries, slot_row, pieces, capacity, *before):
    shapes = [
        jax.ShapeDtypeStruct((blocks * capacity,) + queries.shape[1:], BF) for _, blocks in pieces
    ]
    whole = lambda array: pl.BlockSpec(array.shape, lambda i, s: (0, 0, 0, 0))
    packed = pl.pallas_call(
        functools.partial(pack_kernel, pieces, capacity),
        out_shape=shapes,
        grid_spec=pltpu.PrefetchScalarGridSpec(
            num_scalar_prefetch=1,
            grid=(1,),
            in_specs=[whole(queries)] + [pl.BlockSpec(memory_space=pl.ANY)] * len(before),
            out_specs=[whole(shape) for shape in shapes],
        ),
        compiler_params=params(16),
        cost_estimate=SMALL,
        name="pack_queries",
    )(slot_row, queries, *before)
    return [x.reshape(-1, x.shape[-1]) for x in packed]


def split_kernel(heads, k_ref, v_ref, kt_ref, vs_ref, wide):
    count = v_ref.shape[0] // heads
    for source, is_key in ((k_ref, True), (v_ref, False)):
        wide[...] = source[...].astype(F32)
        for a in range(heads):
            part = wide[pl.ds(a, count, stride=heads), :]
            if is_key:
                kt_ref[a] = part.T.astype(BF)
            else:
                vs_ref[a] = part.astype(BF)


def split_heads(keys, values):
    count, heads, dim = keys.shape
    steps = 4
    each = count // steps
    rows = pl.BlockSpec((each * heads, dim), lambda i: (i, 0))
    return pl.pallas_call(
        functools.partial(split_kernel, heads),
        out_shape=[
            jax.ShapeDtypeStruct((heads, dim, count), BF),
            jax.ShapeDtypeStruct((heads, count, dim), BF),
        ],
        grid=(steps,),
        in_specs=[rows, rows],
        out_specs=[
            pl.BlockSpec((heads, dim, each), lambda i: (0, 0, i)),
            pl.BlockSpec((heads, each, dim), lambda i: (0, i, 0)),
        ],
        scratch_shapes=[pltpu.VMEM((each * heads, dim), F32)],
        compiler_params=params(20),
        cost_estimate=SMALL,
        name="split_heads",
    )(keys.reshape(count * heads, dim), values.reshape(count * heads, dim))


def attend_kernel(capacity, per, group, block, chunk, count, outs, at_ref, *refs):
    q_refs, (k_ref, v_ref) = refs[:count], refs[count : count + 2]
    o_refs, (acc_ref, weight_ref) = refs[-2 - outs : -2], refs[-2:]
    heads, dim, keys = k_ref.shape
    rows = capacity * per
    total = outs * rows
    each = total // heads
    scale = dim**-0.5 * math.log2(math.e)
    ones = jnp.ones((block, dim), BF)
    parts = []
    for q_ref in q_refs:
        for t in range(q_ref.shape[0] // rows):
            first = pl.multiple_of((at_ref[0] ^ t) * rows, rows)
            parts.append(q_ref[pl.ds(first, rows), :].astype(F32))
    grid = jnp.concatenate(parts, axis=0)
    grid = grid.reshape(total // (heads * group), heads, group, dim)
    queries = [grid[:, a].reshape(each, dim).astype(BF) for a in range(heads)]

    def scores(a, j):
        part = k_ref[a, :, pl.ds(j * block, block)]
        return jnp.dot(queries[a], part, preferred_element_type=F32)

    def values(a, j):
        return jnp.concatenate([v_ref[a, pl.ds(j * block, block), :], ones], axis=1)

    def natural(parts):
        split = [x.reshape(each // group, 1, group, dim) for x in parts]
        return jnp.concatenate(split, axis=1).reshape(total, dim)

    def finish(shifts):
        sums = [acc_ref[a, :, dim:] for a in range(heads)]
        out = natural([acc_ref[a, :, :dim] / sums[a] for a in range(heads)]).astype(BF)
        log_sum = natural([shifts[a] + jnp.log2(sums[a]) for a in range(heads)])
        high = log_sum.astype(BF).astype(F32)
        lane = lax.broadcasted_iota(jnp.int32, (total, dim), 1)
        row = lax.broadcasted_iota(jnp.int32, (total, dim), 0)
        term = jnp.where(lane < per, high, log_sum - high)
        term = jnp.where((lane % per == row % per) & (lane < 2 * per), term, 0.0).astype(BF)
        slot = lax.broadcasted_iota(jnp.int32, (EXTRA, rows), 0)
        source = lax.broadcasted_iota(jnp.int32, (EXTRA, rows), 1) // per
        pick = jnp.where(source == slot, 1.0, 0.0).astype(BF)
        for t, o_ref in enumerate(o_refs):
            o_ref[:rows, :] = out[t * rows : (t + 1) * rows]
            logs = jnp.dot(pick, term[t * rows : (t + 1) * rows], preferred_element_type=F32)
            o_ref[rows:, :] = logs.astype(BF)

    turns = keys // block
    steps = block // chunk

    def middle(part):
        weights = jnp.exp2(part - jnp.max(part, axis=1, keepdims=True))
        total = jnp.sum(weights, axis=1, keepdims=True)
        return jnp.sum(weights * part, axis=1, keepdims=True) / total

    def accumulate(a, j):
        slot = (a * turns + j) % 2
        part = jnp.dot(weight_ref[slot], values(a, j), preferred_element_type=F32)
        if j == 0:
            acc_ref[a] = part
        else:
            acc_ref[a] += part

    shifts = []
    before = None
    for a in range(heads):
        for j in range(turns):
            slot = (a * turns + j) % 2
            for c in range(steps):
                first = j * block + c * chunk
                part = jnp.dot(
                    queries[a], k_ref[a, :, first : first + chunk], preferred_element_type=F32
                )
                if first == 0:
                    shifts.append(middle(part * scale))
                weights = jnp.exp2((part * scale - shifts[a]).astype(BF))
                weight_ref[slot, :, c * chunk : (c + 1) * chunk] = weights
            if before is not None:
                accumulate(*before)
            before = (a, j)
    accumulate(*before)
    finish(shifts)
    fits = jnp.max(acc_ref[:, :, dim:]) < LIMIT

    @pl.when(jnp.logical_not(fits))
    def _():
        acc_ref[...] = jnp.zeros_like(acc_ref)
        tops = []
        for a in range(heads):

            def step(j, top):
                part = scores(a, j) * scale
                new = jnp.maximum(top, jnp.max(part, axis=1, keepdims=True))
                weights = jnp.exp2(part - new).astype(BF)
                acc_ref[a] = acc_ref[a] * jnp.exp2(top - new) + jnp.dot(
                    weights, values(a, j), preferred_element_type=F32
                )
                return new

            tops.append(lax.fori_loop(0, turns, step, jnp.full((each, 1), -1e30, F32)))
        finish(tops)


def attend(queries, keys_t, values, at, capacity, per, group, limit, *before):
    dim = queries[0].shape[1]
    heads, keys, _ = values.shape
    rows = capacity * per
    blocks = sum(array.shape[0] for array in queries) // rows
    block = min(1024, keys)
    chunk = min(256, block)
    each = blocks * rows // heads
    whole = lambda array: pl.BlockSpec(array.shape, lambda i, s: (0,) * array.ndim)
    out = jax.ShapeDtypeStruct((rows + EXTRA, dim), BF)
    return pl.pallas_call(
        functools.partial(attend_kernel, capacity, per, group, block, chunk, len(queries), blocks),
        out_shape=[out] * blocks,
        grid_spec=pltpu.PrefetchScalarGridSpec(
            num_scalar_prefetch=1,
            grid=(1,),
            in_specs=[whole(array) for array in queries]
            + [whole(keys_t), whole(values)]
            + [pl.BlockSpec(memory_space=pl.ANY)] * len(before),
            out_specs=[whole(out)] * blocks,
            scratch_shapes=[
                pltpu.VMEM((heads, each, 2 * dim), F32),
                pltpu.VMEM((2, each, block), BF),
            ],
        ),
        compiler_params=params(limit),
        cost_estimate=SMALL,
        name="attend_prefix",
    )(at, *queries, keys_t, values, *before)


def visibility(lengths, draft_count, suffix_count):
    position = jnp.arange(suffix_count + draft_count, dtype=jnp.int32)
    draft_pos = jnp.arange(draft_count, dtype=jnp.int32)
    earlier = position[None, None, :] < lengths[:, None, None]
    earlier = earlier & (position[None, None, :] < suffix_count)
    fresh = (position[None, :] >= suffix_count) & (
        position[None, :] - suffix_count <= draft_pos[:, None]
    )
    return earlier | fresh[None, :, :]


def local_attention(query_grid, key_rows, value_rows, visible):
    scale = query_grid.shape[-1] ** (-0.5)
    scores = (
        jnp.einsum("rtagd,rjad->rtagj", query_grid, key_rows, preferred_element_type=F32) * scale
    )
    visible_mask = visible[:, :, None, None, :]
    scores = jnp.where(visible_mask, scores, F32(-1e30))
    top = jnp.max(scores, axis=-1)
    exponent = jnp.where(visible_mask, jnp.exp(scores - top[..., None]), F32(0.0))
    denominator = jnp.sum(exponent, axis=-1)
    summed = jnp.einsum(
        "rtagj,rjad->rtagd", exponent.astype(BF), value_rows, preferred_element_type=F32
    )
    return summed / denominator[..., None], (top + jnp.log(denominator)) * F32(math.log2(math.e))


def join_kernel(capacity, count, base, order, target, *refs):
    received, (local, local_log) = refs[:count], refs[count : count + 2]
    att, blocks, block_logs, part, mine, logs, spread = refs[-7:]
    rows, per, dim = part.shape
    held = capacity * per
    heads = att.shape[1] // dim
    draft = per // heads
    done = 0
    for array in received:
        for first in range(0, array.shape[0], held + EXTRA):
            values = array[first : first + held, :].astype(F32)
            blocks[done * capacity : (done + 1) * capacity] = values.reshape(capacity, per, dim)
            last = array[first + held : first + held + EXTRA, :].astype(F32)
            block_logs[done * EXTRA : (done + 1) * EXTRA] = last
            done += 1

    def gather(i, _):
        at = order[base + i]
        slot = target[base + i]
        part[i] = blocks[slot]
        mine[i] = local[at].astype(F32)
        place = (slot // capacity) * EXTRA + slot % capacity
        logs[0, pl.ds(i, 1), :] = block_logs[pl.ds(place, 1), :]
        logs[1, pl.ds(i, 1), :] = local_log[pl.ds(at, 1), :]
        return 0

    lax.fori_loop(0, rows, gather, 0)
    lane = lax.broadcasted_iota(jnp.int32, (rows, dim), 1)
    first = logs[0] + pltpu.roll(logs[0], dim - per, axis=1)
    share = 1.0 / (1.0 + jnp.exp2(logs[1] - first))
    high = share.astype(BF).astype(F32)
    low = pltpu.roll(share - high, per, axis=1)
    logs[0] = jnp.where(lane < per, high, jnp.where(lane < 2 * per, low, 0.0))
    diagonal = lax.broadcasted_iota(jnp.int32, (per, dim), 1) % per
    diagonal = diagonal == lax.broadcasted_iota(jnp.int32, (per, dim), 0)

    def widen(i, _):
        row = logs[0, pl.ds(i, 1), :]
        spread[i] = jnp.where(diagonal, row, 0.0).astype(BF)
        return 0

    lax.fori_loop(0, rows, widen, 0)
    ones = jnp.ones((dim, dim), BF)
    shares = jnp.dot(
        spread[...].reshape(rows * per, dim), ones, preferred_element_type=F32
    ).reshape(rows, per, dim)
    part[...] = mine[...] + shares * (part[...] - mine[...])
    flat = part.reshape(rows * per, dim)
    for h in range(heads):
        head = flat[pl.ds(h, rows * draft, stride=heads), :]
        att[:, h * dim : (h + 1) * dim] = head.astype(BF)


def join(received, local, local_log, order, target, heads, base, rows, capacity, *before):
    count = len(received)
    per, dim = local.shape[1:]
    blocks = sum(array.shape[0] for array in received) // (capacity * per + EXTRA)
    whole = lambda array: pl.BlockSpec(array.shape, lambda n, *_: (0,) * array.ndim)
    shape = jax.ShapeDtypeStruct((rows * per // heads, heads * dim), BF)
    return pl.pallas_call(
        functools.partial(join_kernel, capacity, count, base),
        out_shape=shape,
        grid_spec=pltpu.PrefetchScalarGridSpec(
            num_scalar_prefetch=2,
            grid=(1,),
            in_specs=[whole(array) for array in received]
            + [whole(local), whole(local_log)]
            + [pl.BlockSpec(memory_space=pl.ANY)] * len(before),
            out_specs=whole(shape),
            scratch_shapes=[
                pltpu.VMEM((blocks * capacity, per, dim), F32),
                pltpu.VMEM((blocks * EXTRA, dim), F32),
                pltpu.VMEM((rows, per, dim), F32),
                pltpu.VMEM((rows, per, dim), F32),
                pltpu.VMEM((2, rows, dim), F32),
                pltpu.VMEM((rows, per, dim), BF),
            ],
        ),
        compiler_params=params(20),
        cost_estimate=SMALL,
        name="join_parts",
    )(order, target, *received, local, local_log, *before)


def project_kernel(each, count, shards, att, weight, *refs):
    del shards
    outs = refs[-count:]
    product = jnp.dot(att[...], weight[...], preferred_element_type=F32).astype(BF)
    for k, out in enumerate(outs):

        @pl.when(pl.program_id(0) // each == k)
        def _():
            out[...] = product


def project(att, weight, shards, width, *before):
    rows, depth = att.shape
    count = shards.shape[0]
    block = min(512, width)
    each = width // block
    place = lambda k: lambda n, s: (0, jnp.clip(n - k * each, 0, each - 1))
    return pl.pallas_call(
        functools.partial(project_kernel, each, count),
        out_shape=[jax.ShapeDtypeStruct((rows, width), BF)] * count,
        grid_spec=pltpu.PrefetchScalarGridSpec(
            num_scalar_prefetch=1,
            grid=(count * each,),
            in_specs=[
                pl.BlockSpec((rows, depth), lambda n, s: (0, 0)),
                pl.BlockSpec((depth, block), lambda n, s: (0, s[n // each] * each + n % each)),
            ]
            + [pl.BlockSpec(memory_space=pl.ANY)] * len(before),
            out_specs=[pl.BlockSpec((rows, block), place(k)) for k in range(count)],
        ),
        compiler_params=params(56),
        cost_estimate=SMALL,
        name="project",
    )(shards, att, weight, *before)


def project_sum(att, weight, own, split, before):
    size = lax.axis_size("tensor")
    chips = size // 2
    width = weight.shape[1] // size
    order = list(range(1, chips)) + [0]
    pairs = [[own ^ (2 * d + 1), own ^ (2 * d)] for d in order]
    if not split:
        shards = jnp.stack([shard for pair in pairs for shard in pair])
        products = project(att, weight, shards, width, *before)
    terms, sent = [], []
    for k, d in enumerate(order):
        if split:
            waits = sent[-1:] or before
            send, keep = [project(att, weight, shard[None], width, *waits)[0] for shard in pairs[k]]
        else:
            send, keep = products[2 * k : 2 * k + 2]
        there = lax.ppermute(send, "tensor", [(i, i ^ 1) for i in range(size)])
        total = keep.astype(F32) + there.astype(F32)
        if d:
            sent.append(total.astype(BF))
            total = lax.ppermute(sent[-1], "tensor", [(i, i ^ (2 * d)) for i in range(size)])
        terms.append(total)
    return terms[::-1], sent, keep


def arrange_kernel(counts, place_ref, *refs):
    out_ref = refs[-1]
    rows, draft, _ = out_ref.shape
    halves, start = [], 0
    for count in counts:
        total = refs[start][...]
        for term in refs[start + 1 : start + count]:
            total = total + term[...].astype(F32)
        halves.append(total.astype(BF))
        start += count
    values = jnp.concatenate(halves, axis=0)
    size = rows * draft
    pick = lax.broadcasted_iota(jnp.int32, (size, size), 1) == place_ref[...]
    result = jnp.dot(
        jnp.where(pick, 1.0, 0.0).astype(BF), values, preferred_element_type=F32
    )
    for r in range(rows):
        out_ref[r] = result[r * draft : (r + 1) * draft].astype(BF)


def arrange(halves, place, rows, draft):
    width = halves[0][0].shape[1]
    index = (place[:, None] * draft + jnp.arange(draft, dtype=jnp.int32)[None, :]).reshape(-1, 1)
    return pl.pallas_call(
        functools.partial(arrange_kernel, [len(half) for half in halves]),
        out_shape=jax.ShapeDtypeStruct((rows, draft, width), BF),
        compiler_params=params(20),
        cost_estimate=SMALL,
        name="arrange_rows",
    )(index, *[term for half in halves for term in half])


def exchange(x):
    size = lax.axis_size("dp")
    groups = [list(range(size // 2)), list(range(size // 2, size))]
    return lax.all_to_all(
        x, "dp", split_axis=0, concat_axis=0, axis_index_groups=groups, tiled=True
    )


def hop(x, shift):
    size = lax.axis_size("dp")
    return lax.ppermute(x, "dp", [(i, i ^ shift) for i in range(size)])


def body(
    queries,
    draft_keys,
    draft_values,
    suffix_keys,
    suffix_values,
    suffix_len,
    prefix_keys,
    prefix_values,
    row_prefix,
    prefix_slot,
    out_weight,
):
    row_count, draft, query_heads, dim = queries.shape
    heads = draft_keys.shape[2]
    group = query_heads // heads
    per = draft * query_heads
    suffix_count = suffix_keys.shape[1]
    peers = lax.axis_size("dp")
    capacity = 2 * row_count // peers
    own = lax.axis_index("tensor").astype(jnp.int32)
    me = lax.axis_index("dp").astype(jnp.int32)

    slot_row, place, order, target = route(row_prefix, prefix_slot, me, peers, capacity)
    half = peers // 2
    lead = half // 2
    first = pack(queries, slot_row, [(half + d, 1) for d in range(lead)], capacity)
    near, *late = pack(
        queries,
        slot_row,
        [(0, half)] + [(half + d, 1) for d in range(lead, half)],
        capacity,
        first[0],
    )
    far = [hop(x, half + d) for d, x in enumerate(first + late)]
    near = exchange(near)

    keys_t, values = split_heads(prefix_keys[0], prefix_values[0])
    here = (me % half).reshape(1)
    zero = jnp.zeros((1,), jnp.int32)
    back, before = [None] * peers, []
    for batch in [range(half, half + lead), range(half)] + [[d] for d in range(half + lead, peers)]:
        arrays = [near] if batch[0] == 0 else [far[d - half] for d in batch]
        if batch[-1] == peers - 1:
            before = list(before) + back[half : half + lead]
        at, limit = (here, 44) if batch[0] == 0 else (zero, 14 + 7 * len(batch))
        results = attend(arrays, keys_t, values, at, capacity, per, group, limit, *before)
        before = results[:1]
        for d, result in zip(batch, results):
            back[d] = hop(result, d) if d else result

    query_grid = queries.reshape(row_count, draft, heads, group, dim)
    all_keys = jnp.concatenate([suffix_keys, draft_keys], axis=1)
    all_values = jnp.concatenate([suffix_values, draft_values], axis=1)
    visible = visibility(suffix_len, draft, suffix_count)
    local, local_log = local_attention(query_grid, all_keys, all_values, visible)
    local = local.reshape(row_count, per, dim).astype(BF)
    local_log = jnp.pad(local_log.reshape(row_count, per), ((0, 0), (0, dim - per)))

    rows = row_count // 2
    early = peers - rows // capacity
    outs, sent = [], []
    for base in (0, rows):
        received = back if base else back[:early]
        att = join(
            received, local, local_log, order, target, query_heads, base, rows, capacity, *before
        )
        terms, sent, product = project_sum(att, out_weight, own, base > 0, sent)
        before = [product]
        outs.append(terms)
    return arrange(outs, place, row_count, draft)


def solution(mesh):
    placed = (
        P("dp", None, "tensor", None),
        P("dp", None, "tensor", None),
        P("dp", None, "tensor", None),
        P("dp", None, "tensor", None),
        P("dp", None, "tensor", None),
        P("dp"),
        P("dp", None, "tensor", None),
        P("dp", None, "tensor", None),
        P("dp", None),
        P(),
        P("tensor", None),
    )
    return jax.shard_map(
        body, mesh=mesh, in_specs=placed, out_specs=P("dp", None, "tensor"), check_vma=False
    )
```

```python
import functools
import math

import jax
import jax.numpy as jnp
from jax import lax
from jax.experimental import pallas as pl
from jax.experimental.pallas import tpu as pltpu
from jax.sharding import PartitionSpec as P

BF = jnp.bfloat16
F32 = jnp.float32
EXTRA = 16
LIMIT = 1e30
SMALL = pl.CostEstimate(flops=1 << 20, bytes_accessed=1 << 10, transcendentals=0)


def params(mebibytes):
    return pltpu.CompilerParams(vmem_limit_bytes=mebibytes * 1024 * 1024)


def route(row_prefix, prefix_slot, me, peers, capacity):
    rows = row_prefix.shape[0]
    prefixes = prefix_slot.shape[0]
    name = row_prefix[:, 0]
    row = jnp.arange(rows, dtype=jnp.int32)
    owner = jnp.sum(
        jnp.where(
            row_prefix == jnp.arange(prefixes, dtype=jnp.int32)[None, :], prefix_slot[None, :], 0
        ),
        axis=1,
    )
    same = (name[:, None] == name[None, :]) & (row[None, :] < row[:, None])
    rank = jnp.sum(same.astype(jnp.int32), axis=1)
    half = peers // 2
    shift = owner ^ me
    sent = jnp.where(shift < half, owner % half, shift) * capacity + rank
    target = shift * capacity + rank
    slots = jnp.arange(peers * capacity, dtype=jnp.int32)
    slot_row = jnp.sum(jnp.where(sent[None, :] == slots[:, None], row[None, :], 0), axis=1)
    place = jnp.sum((target[None, :] < target[:, None]).astype(jnp.int32), axis=1)
    at = place[None, :] == row[:, None]
    order = jnp.sum(jnp.where(at, row[None, :], 0), axis=1)
    order_target = jnp.sum(jnp.where(at, target[None, :], 0), axis=1)
    return slot_row, place, order, order_target


def pack_kernel(pieces, capacity, slot_row, q_ref, *refs):
    outs = refs[-len(pieces) :]

    def one(k, _):
        for (first, blocks), out in zip(pieces, outs):
            for b in range(blocks):
                out[b * capacity + k] = q_ref[slot_row[(first + b) * capacity + k]]
        return 0

    lax.fori_loop(0, capacity, one, 0)


def pack(queries, slot_row, pieces, capacity, *before):
    shapes = [
        jax.ShapeDtypeStruct((blocks * capacity,) + queries.shape[1:], BF) for _, blocks in pieces
    ]
    whole = lambda array: pl.BlockSpec(array.shape, lambda i, s: (0, 0, 0, 0))
    packed = pl.pallas_call(
        functools.partial(pack_kernel, pieces, capacity),
        out_shape=shapes,
        grid_spec=pltpu.PrefetchScalarGridSpec(
            num_scalar_prefetch=1,
            grid=(1,),
            in_specs=[whole(queries)] + [pl.BlockSpec(memory_space=pl.ANY)] * len(before),
            out_specs=[whole(shape) for shape in shapes],
        ),
        compiler_params=params(16),
        cost_estimate=SMALL,
        name="pack_queries",
    )(slot_row, queries, *before)
    return [x.reshape(-1, x.shape[-1]) for x in packed]


def split_kernel(heads, steps, k_hbm, v_hbm, kt_ref, vs_ref, buffer, wide, sems):
    step = pl.program_id(0)
    each = buffer.shape[2]
    count = each // heads

    def copy(source, which, part):
        rows = source.at[pl.ds(part * each, each), :]
        return pltpu.make_async_copy(rows, buffer.at[which, part], sems.at[which, part])

    @pl.when(step == 0)
    def _():
        for part in range(steps):
            copy(k_hbm, 0, part).start()
            copy(v_hbm, 1, part).start()

    for which, source in ((0, k_hbm), (1, v_hbm)):
        copy(source, which, step).wait()
        wide[...] = buffer[which, step].astype(F32)
        for a in range(heads):
            part = wide[pl.ds(a, count, stride=heads), :]
            if which == 0:
                kt_ref[a] = part.T.astype(BF)
            else:
                vs_ref[a] = part.astype(BF)


def split_heads(keys, values):
    count, heads, dim = keys.shape
    steps = 4
    each = count // steps
    return pl.pallas_call(
        functools.partial(split_kernel, heads, steps),
        out_shape=[
            jax.ShapeDtypeStruct((heads, dim, count), BF),
            jax.ShapeDtypeStruct((heads, count, dim), BF),
        ],
        grid=(steps,),
        in_specs=[pl.BlockSpec(memory_space=pl.ANY)] * 2,
        out_specs=[
            pl.BlockSpec((heads, dim, each), lambda i: (0, 0, i)),
            pl.BlockSpec((heads, each, dim), lambda i: (0, i, 0)),
        ],
        scratch_shapes=[
            pltpu.VMEM((2, steps, each * heads, dim), BF),
            pltpu.VMEM((each * heads, dim), F32),
            pltpu.SemaphoreType.DMA((2, steps)),
        ],
        compiler_params=params(52),
        cost_estimate=SMALL,
        name="split_heads",
    )(keys.reshape(count * heads, dim), values.reshape(count * heads, dim))


def attend_kernel(capacity, per, group, block, chunk, count, outs, at_ref, *refs):
    del at_ref
    q_refs, (k_ref, v_ref) = refs[:count], refs[count : count + 2]
    o_refs, (acc_ref, weight_ref) = refs[-2 - outs : -2], refs[-2:]
    heads, dim, keys = k_ref.shape
    total = rows = capacity * per
    each = rows // heads
    scale = dim**-0.5 * math.log2(math.e)
    ones = jnp.ones((block, dim), BF)
    turn = pl.program_id(0)
    grid = q_refs[0][...].astype(F32)
    for t in range(1, count):
        grid = jnp.where(turn == t, q_refs[t][...].astype(F32), grid)
    grid = grid.reshape(total // (heads * group), heads, group, dim)
    queries = [grid[:, a].reshape(each, dim).astype(BF) for a in range(heads)]

    def scores(a, j):
        part = k_ref[a, :, pl.ds(j * block, block)]
        return jnp.dot(queries[a], part, preferred_element_type=F32)

    def values(a, j):
        return jnp.concatenate([v_ref[a, pl.ds(j * block, block), :], ones], axis=1)

    def natural(parts):
        split = [x.reshape(each // group, 1, group, dim) for x in parts]
        return jnp.concatenate(split, axis=1).reshape(total, dim)

    def finish(shifts):
        sums = [acc_ref[a, :, dim:] for a in range(heads)]
        out = natural([acc_ref[a, :, :dim] / sums[a] for a in range(heads)]).astype(BF)
        log_sum = natural([shifts[a] + jnp.log2(sums[a]) for a in range(heads)])
        high = log_sum.astype(BF).astype(F32)
        lane = lax.broadcasted_iota(jnp.int32, (total, dim), 1)
        row = lax.broadcasted_iota(jnp.int32, (total, dim), 0)
        term = jnp.where(lane < per, high, log_sum - high)
        term = jnp.where((lane % per == row % per) & (lane < 2 * per), term, 0.0).astype(BF)
        slot = lax.broadcasted_iota(jnp.int32, (EXTRA, rows), 0)
        source = lax.broadcasted_iota(jnp.int32, (EXTRA, rows), 1) // per
        pick = jnp.where(source == slot, 1.0, 0.0).astype(BF)
        logs = jnp.dot(pick, term, preferred_element_type=F32).astype(BF)
        for t, o_ref in enumerate(o_refs):

            @pl.when(turn == t)
            def _():
                o_ref[:rows, :] = out
                o_ref[rows:, :] = logs

    turns = keys // block
    steps = block // chunk

    def middle(part):
        weights = jnp.exp2(part - jnp.max(part, axis=1, keepdims=True))
        total = jnp.sum(weights, axis=1, keepdims=True)
        return jnp.sum(weights * part, axis=1, keepdims=True) / total

    def accumulate(a, j):
        slot = (a * turns + j) % 2
        part = jnp.dot(weight_ref[slot], values(a, j), preferred_element_type=F32)
        if j == 0:
            acc_ref[a] = part
        else:
            acc_ref[a] += part

    shifts = []
    before = None
    for a in range(heads):
        for j in range(turns):
            slot = (a * turns + j) % 2
            for c in range(steps):
                first = j * block + c * chunk
                part = jnp.dot(
                    queries[a], k_ref[a, :, first : first + chunk], preferred_element_type=F32
                )
                if first == 0:
                    shifts.append(middle(part * scale))
                weights = jnp.exp2((part * scale - shifts[a]).astype(BF))
                weight_ref[slot, :, c * chunk : (c + 1) * chunk] = weights
            if before is not None:
                accumulate(*before)
            before = (a, j)
    accumulate(*before)
    finish(shifts)
    fits = jnp.max(acc_ref[:, :, dim:]) < LIMIT

    @pl.when(jnp.logical_not(fits))
    def _():
        acc_ref[...] = jnp.zeros_like(acc_ref)
        tops = []
        for a in range(heads):

            def step(j, top):
                part = scores(a, j) * scale
                new = jnp.maximum(top, jnp.max(part, axis=1, keepdims=True))
                weights = jnp.exp2(part - new).astype(BF)
                acc_ref[a] = acc_ref[a] * jnp.exp2(top - new) + jnp.dot(
                    weights, values(a, j), preferred_element_type=F32
                )
                return new

            tops.append(lax.fori_loop(0, turns, step, jnp.full((each, 1), -1e30, F32)))
        finish(tops)


def attend(queries, keys_t, values, at, capacity, per, group, *before):
    dim = queries[0].shape[1]
    heads, keys, _ = values.shape
    rows = capacity * per
    count = len(queries)
    blocks = count if count > 1 else queries[0].shape[0] // rows
    block = min(1024, keys)
    chunk = min(256, block)
    once = lambda array: pl.BlockSpec(
        array.shape, lambda i, s: (0,) * array.ndim, pipeline_mode=pl.Buffered(1)
    )
    place = (lambda i, s: (0, 0)) if count > 1 else (lambda i, s: (s[0] ^ i, 0))
    out = jax.ShapeDtypeStruct((rows + EXTRA, dim), BF)
    return pl.pallas_call(
        functools.partial(attend_kernel, capacity, per, group, block, chunk, count, blocks),
        out_shape=[out] * blocks,
        grid_spec=pltpu.PrefetchScalarGridSpec(
            num_scalar_prefetch=1,
            grid=(blocks,),
            in_specs=[pl.BlockSpec((rows, dim), place)] * count
            + [once(keys_t), once(values)]
            + [pl.BlockSpec(memory_space=pl.ANY)] * len(before),
            out_specs=[pl.BlockSpec(out.shape, lambda i, s: (0, 0))] * blocks,
            scratch_shapes=[
                pltpu.VMEM((heads, rows // heads, 2 * dim), F32),
                pltpu.VMEM((2, rows // heads, block), BF),
            ],
        ),
        compiler_params=params(24),
        cost_estimate=SMALL,
        name="attend_prefix",
    )(at, *queries, keys_t, values, *before)


def visibility(lengths, draft_count, suffix_count):
    position = jnp.arange(suffix_count + draft_count, dtype=jnp.int32)
    draft_pos = jnp.arange(draft_count, dtype=jnp.int32)
    earlier = position[None, None, :] < lengths[:, None, None]
    earlier = earlier & (position[None, None, :] < suffix_count)
    fresh = (position[None, :] >= suffix_count) & (
        position[None, :] - suffix_count <= draft_pos[:, None]
    )
    return earlier | fresh[None, :, :]


def local_attention(query_grid, key_rows, value_rows, visible):
    scale = query_grid.shape[-1] ** (-0.5)
    scores = (
        jnp.einsum("rtagd,rjad->rtagj", query_grid, key_rows, preferred_element_type=F32) * scale
    )
    visible_mask = visible[:, :, None, None, :]
    scores = jnp.where(visible_mask, scores, F32(-1e30))
    top = jnp.max(scores, axis=-1)
    exponent = jnp.where(visible_mask, jnp.exp(scores - top[..., None]), F32(0.0))
    denominator = jnp.sum(exponent, axis=-1)
    summed = jnp.einsum(
        "rtagj,rjad->rtagd", exponent.astype(BF), value_rows, preferred_element_type=F32
    )
    return summed / denominator[..., None], (top + jnp.log(denominator)) * F32(math.log2(math.e))


def fetch(weight, shards, buffer, sems, width):
    count, _, block = buffer.shape
    each = width // block
    copies = []
    for n in range(count):
        column = pl.multiple_of(shards[n // each] * width + (n % each) * block, block)
        source = weight.at[:, pl.ds(column, block)]
        copies.append(pltpu.make_async_copy(source, buffer.at[n], sems.at[n]))
        copies[-1].start()
    return copies


def multiply(att, copies, buffer, outs):
    block = buffer.shape[2]
    each = len(copies) // len(outs)
    rows = att[...]
    for n, copy in enumerate(copies):
        copy.wait()
        product = jnp.dot(rows, buffer[n], preferred_element_type=F32).astype(BF)
        outs[n // each][:, n % each * block : (n % each + 1) * block] = product


def join_kernel(capacity, count, base, shares, order, target, shards, *refs):
    received, (local, local_log, weight) = refs[:count], refs[count : count + 3]
    att, *outs = refs[-8 - shares - 1 : -8]
    blocks, block_logs, part, mine, logs, spread, buffer, sems = refs[-8:]
    copies = fetch(weight, shards, buffer, sems, outs[0].shape[1])
    rows, per, dim = part.shape
    held = capacity * per
    heads = att.shape[1] // dim
    draft = per // heads
    done = 0
    for array in received:
        for first in range(0, array.shape[0], held + EXTRA):
            values = array[first : first + held, :].astype(F32)
            blocks[done * capacity : (done + 1) * capacity] = values.reshape(capacity, per, dim)
            last = array[first + held : first + held + EXTRA, :].astype(F32)
            block_logs[done * EXTRA : (done + 1) * EXTRA] = last
            done += 1

    def gather(i, _):
        at = order[base + i]
        slot = target[base + i]
        part[i] = blocks[slot]
        mine[i] = local[at].astype(F32)
        place = (slot // capacity) * EXTRA + slot % capacity
        logs[0, pl.ds(i, 1), :] = block_logs[pl.ds(place, 1), :]
        logs[1, pl.ds(i, 1), :] = local_log[pl.ds(at, 1), :]
        return 0

    lax.fori_loop(0, rows, gather, 0)
    lane = lax.broadcasted_iota(jnp.int32, (rows, dim), 1)
    first = logs[0] + pltpu.roll(logs[0], dim - per, axis=1)
    share = 1.0 / (1.0 + jnp.exp2(logs[1] - first))
    high = share.astype(BF).astype(F32)
    low = pltpu.roll(share - high, per, axis=1)
    logs[0] = jnp.where(lane < per, high, jnp.where(lane < 2 * per, low, 0.0))
    diagonal = lax.broadcasted_iota(jnp.int32, (per, dim), 1) % per
    diagonal = diagonal == lax.broadcasted_iota(jnp.int32, (per, dim), 0)

    def widen(i, _):
        row = logs[0, pl.ds(i, 1), :]
        spread[i] = jnp.where(diagonal, row, 0.0).astype(BF)
        return 0

    lax.fori_loop(0, rows, widen, 0)
    ones = jnp.ones((dim, dim), BF)
    shares = jnp.dot(
        spread[...].reshape(rows * per, dim), ones, preferred_element_type=F32
    ).reshape(rows, per, dim)
    part[...] = mine[...] + shares * (part[...] - mine[...])
    flat = part.reshape(rows * per, dim)
    for h in range(heads):
        head = flat[pl.ds(h, rows * draft, stride=heads), :]
        att[:, h * dim : (h + 1) * dim] = head.astype(BF)


    multiply(att, copies, buffer, outs)


def join(
    received, local, local_log, order, target, heads, base, rows, capacity, weight, shards, width, *before
):
    count = len(received)
    per, dim = local.shape[1:]
    blocks = sum(array.shape[0] for array in received) // (capacity * per + EXTRA)
    shares = shards.shape[0]
    lines = rows * per // heads
    block = min(256, width)
    whole = lambda array: pl.BlockSpec(array.shape, lambda n, *_: (0,) * array.ndim)
    att = jax.ShapeDtypeStruct((lines, heads * dim), BF)
    out = jax.ShapeDtypeStruct((lines, width), BF)
    return pl.pallas_call(
        functools.partial(join_kernel, capacity, count, base, shares),
        out_shape=[att] + [out] * shares,
        grid_spec=pltpu.PrefetchScalarGridSpec(
            num_scalar_prefetch=3,
            grid=(1,),
            in_specs=[whole(array) for array in received]
            + [whole(local), whole(local_log)]
            + [pl.BlockSpec(memory_space=pl.ANY)] * (1 + len(before)),
            out_specs=[whole(att)] + [whole(out)] * shares,
            scratch_shapes=[
                pltpu.VMEM((blocks * capacity, per, dim), F32),
                pltpu.VMEM((blocks * EXTRA, dim), F32),
                pltpu.VMEM((rows, per, dim), F32),
                pltpu.VMEM((rows, per, dim), F32),
                pltpu.VMEM((2, rows, dim), F32),
                pltpu.VMEM((rows, per, dim), BF),
                pltpu.VMEM((shares * width // block, heads * dim, block), BF),
                pltpu.SemaphoreType.DMA((shares * width // block,)),
            ],
        ),
        compiler_params=params(48),
        cost_estimate=SMALL,
        name="join_project",
    )(order, target, shards, *received, local, local_log, weight, *before)


def project_kernel(shares, shards, att, weight, *refs):
    outs, (buffer, sems) = refs[-2 - shares : -2], refs[-2:]
    multiply(att, fetch(weight, shards, buffer, sems, outs[0].shape[1]), buffer, outs)


def project(att, weight, shards, width, *before):
    rows, depth = att.shape
    shares = shards.shape[0]
    block = min(256, width)
    out = jax.ShapeDtypeStruct((rows, width), BF)
    whole = lambda array: pl.BlockSpec(array.shape, lambda n, *_: (0,) * array.ndim)
    return pl.pallas_call(
        functools.partial(project_kernel, shares),
        out_shape=[out] * shares,
        grid_spec=pltpu.PrefetchScalarGridSpec(
            num_scalar_prefetch=1,
            grid=(1,),
            in_specs=[whole(att)] + [pl.BlockSpec(memory_space=pl.ANY)] * (1 + len(before)),
            out_specs=[whole(out)] * shares,
            scratch_shapes=[
                pltpu.VMEM((shares * width // block, depth, block), BF),
                pltpu.SemaphoreType.DMA((shares * width // block,)),
            ],
        ),
        compiler_params=params(48),
        cost_estimate=SMALL,
        name="project",
    )(shards, att, weight, *before)


def project_sum(join_with, weight, own, split, before):
    size = lax.axis_size("tensor")
    chips = size // 2
    width = weight.shape[1] // size
    order = list(range(1, chips)) + [0]
    shards = [own ^ (2 * d + other) for d in order for other in (1, 0)]
    with_join = 1 if split else len(shards)
    att, *products = join_with(jnp.stack(shards[:with_join]), width)
    got = []
    for k, d in enumerate(order):
        while len(products) < 2 * k + 2:
            waits = before if d == 0 else []
            products += project(att, weight, shards[len(products)][None], width, *waits)
        send, keep = products[2 * k : 2 * k + 2]
        there = lax.ppermute(send, "tensor", [(i, i ^ 1) for i in range(size)])
        if d:
            total = (keep.astype(F32) + there.astype(F32)).astype(BF)
            before = list(before) + [total]
            got.append(lax.ppermute(total, "tensor", [(i, i ^ (2 * d)) for i in range(size)]))
    total = keep.astype(F32)
    for term in got:
        total = total + term.astype(F32)
    return [total, there], [total], keep


def arrange_kernel(counts, place_ref, *refs):
    out_ref = refs[-1]
    rows, draft, _ = out_ref.shape
    halves, start = [], 0
    for count in counts:
        total = refs[start][...]
        for term in refs[start + 1 : start + count]:
            total = total + term[...].astype(F32)
        halves.append(total.astype(BF))
        start += count
    values = jnp.concatenate(halves, axis=0)
    size = rows * draft
    pick = lax.broadcasted_iota(jnp.int32, (size, size), 1) == place_ref[...]
    result = jnp.dot(
        jnp.where(pick, 1.0, 0.0).astype(BF), values, preferred_element_type=F32
    )
    for r in range(rows):
        out_ref[r] = result[r * draft : (r + 1) * draft].astype(BF)


def arrange(halves, place, rows, draft):
    width = halves[0][0].shape[1]
    index = (place[:, None] * draft + jnp.arange(draft, dtype=jnp.int32)[None, :]).reshape(-1, 1)
    return pl.pallas_call(
        functools.partial(arrange_kernel, [len(half) for half in halves]),
        out_shape=jax.ShapeDtypeStruct((rows, draft, width), BF),
        compiler_params=params(20),
        cost_estimate=SMALL,
        name="arrange_rows",
    )(index, *[term for half in halves for term in half])


def exchange(x):
    size = lax.axis_size("dp")
    groups = [list(range(size // 2)), list(range(size // 2, size))]
    return lax.all_to_all(
        x, "dp", split_axis=0, concat_axis=0, axis_index_groups=groups, tiled=True
    )


def hop(x, shift):
    size = lax.axis_size("dp")
    return lax.ppermute(x, "dp", [(i, i ^ shift) for i in range(size)])


def body(
    queries,
    draft_keys,
    draft_values,
    suffix_keys,
    suffix_values,
    suffix_len,
    prefix_keys,
    prefix_values,
    row_prefix,
    prefix_slot,
    out_weight,
):
    row_count, draft, query_heads, dim = queries.shape
    heads = draft_keys.shape[2]
    group = query_heads // heads
    per = draft * query_heads
    suffix_count = suffix_keys.shape[1]
    peers = lax.axis_size("dp")
    capacity = 2 * row_count // peers
    own = lax.axis_index("tensor").astype(jnp.int32)
    me = lax.axis_index("dp").astype(jnp.int32)

    slot_row, place, order, target = route(row_prefix, prefix_slot, me, peers, capacity)
    half = peers // 2
    lead = half // 2
    first = pack(queries, slot_row, [(half + d, 1) for d in range(lead)], capacity)
    near, *late = pack(
        queries,
        slot_row,
        [(0, half)] + [(half + d, 1) for d in range(lead, half)],
        capacity,
        first[0],
    )
    far = [hop(x, half + d) for d, x in enumerate(first + late)]
    near = exchange(near)

    keys_t, values = split_heads(prefix_keys[0], prefix_values[0])
    here = (me % half).reshape(1)
    zero = jnp.zeros((1,), jnp.int32)
    back, before = [None] * peers, []
    for batch in [range(half, half + lead), range(half)] + [[d] for d in range(half + lead, peers)]:
        arrays = [near] if batch[0] == 0 else [far[d - half] for d in batch]
        if batch[-1] == peers - 1:
            before = list(before) + back[half : half + lead]
        at = here if batch[0] == 0 else zero
        results = attend(arrays, keys_t, values, at, capacity, per, group, *before)
        before = results[:1]
        for d, result in zip(batch, results):
            back[d] = hop(result, d) if d else result

    query_grid = queries.reshape(row_count, draft, heads, group, dim)
    all_keys = jnp.concatenate([suffix_keys, draft_keys], axis=1)
    all_values = jnp.concatenate([suffix_values, draft_values], axis=1)
    visible = visibility(suffix_len, draft, suffix_count)
    local, local_log = local_attention(query_grid, all_keys, all_values, visible)
    local = local.reshape(row_count, per, dim).astype(BF)
    local_log = jnp.pad(local_log.reshape(row_count, per), ((0, 0), (0, dim - per)))

    rows = row_count // 2
    early = peers - rows // capacity
    outs, waits = [], []
    for base in (0, rows):
        received = back if base else back[:early]

        def join_with(shards, width):
            return join(
                received,
                local,
                local_log,
                order,
                target,
                query_heads,
                base,
                rows,
                capacity,
                out_weight,
                shards,
                width,
                *before,
            )

        terms, waits, product = project_sum(join_with, out_weight, own, base > 0, waits)
        before = [product]
        outs.append(terms)
    return arrange(outs, place, row_count, draft)


def solution(mesh):
    placed = (
        P("dp", None, "tensor", None),
        P("dp", None, "tensor", None),
        P("dp", None, "tensor", None),
        P("dp", None, "tensor", None),
        P("dp", None, "tensor", None),
        P("dp"),
        P("dp", None, "tensor", None),
        P("dp", None, "tensor", None),
        P("dp", None),
        P(),
        P("tensor", None),
    )
    return jax.shard_map(
        body, mesh=mesh, in_specs=placed, out_specs=P("dp", None, "tensor"), check_vma=False
    )
```

```python
import functools
import math

import jax
import jax.numpy as jnp
from jax import lax
from jax.experimental import pallas as pl
from jax.experimental.pallas import tpu as pltpu
from jax.sharding import PartitionSpec as P

BF = jnp.bfloat16
F32 = jnp.float32
EXTRA = 16
LIMIT = 1e30
SMALL = pl.CostEstimate(flops=1 << 20, bytes_accessed=1 << 10, transcendentals=0)


def params(mebibytes):
    return pltpu.CompilerParams(vmem_limit_bytes=mebibytes * 1024 * 1024)


def route(row_prefix, prefix_slot, me, peers, capacity):
    rows = row_prefix.shape[0]
    prefixes = prefix_slot.shape[0]
    name = row_prefix[:, 0]
    row = jnp.arange(rows, dtype=jnp.int32)
    owner = jnp.sum(
        jnp.where(
            row_prefix == jnp.arange(prefixes, dtype=jnp.int32)[None, :], prefix_slot[None, :], 0
        ),
        axis=1,
    )
    same = (name[:, None] == name[None, :]) & (row[None, :] < row[:, None])
    rank = jnp.sum(same.astype(jnp.int32), axis=1)
    half = peers // 2
    shift = owner ^ me
    sent = jnp.where(shift < half, owner % half, shift) * capacity + rank
    target = shift * capacity + rank
    slots = jnp.arange(peers * capacity, dtype=jnp.int32)
    slot_row = jnp.sum(jnp.where(sent[None, :] == slots[:, None], row[None, :], 0), axis=1)
    place = jnp.sum((target[None, :] < target[:, None]).astype(jnp.int32), axis=1)
    at = place[None, :] == row[:, None]
    order = jnp.sum(jnp.where(at, row[None, :], 0), axis=1)
    order_target = jnp.sum(jnp.where(at, target[None, :], 0), axis=1)
    return slot_row, place, order, order_target


def pack_kernel(pieces, capacity, slot_row, q_ref, *refs):
    outs = refs[-len(pieces) :]

    def one(k, _):
        for (first, blocks), out in zip(pieces, outs):
            for b in range(blocks):
                out[b * capacity + k] = q_ref[slot_row[(first + b) * capacity + k]]
        return 0

    lax.fori_loop(0, capacity, one, 0)


def pack(queries, slot_row, pieces, capacity, *before):
    shapes = [
        jax.ShapeDtypeStruct((blocks * capacity,) + queries.shape[1:], BF) for _, blocks in pieces
    ]
    whole = lambda array: pl.BlockSpec(array.shape, lambda i, s: (0, 0, 0, 0))
    packed = pl.pallas_call(
        functools.partial(pack_kernel, pieces, capacity),
        out_shape=shapes,
        grid_spec=pltpu.PrefetchScalarGridSpec(
            num_scalar_prefetch=1,
            grid=(1,),
            in_specs=[whole(queries)] + [pl.BlockSpec(memory_space=pl.ANY)] * len(before),
            out_specs=[whole(shape) for shape in shapes],
        ),
        compiler_params=params(16),
        cost_estimate=SMALL,
        name="pack_queries",
    )(slot_row, queries, *before)
    return [x.reshape(-1, x.shape[-1]) for x in packed]


def split_kernel(heads, steps, k_hbm, v_hbm, kt_ref, vs_ref, buffer, wide, sems):
    step = pl.program_id(0)
    each = buffer.shape[2]
    count = each // heads

    def copy(source, which, part):
        rows = source.at[pl.ds(part * each, each), :]
        return pltpu.make_async_copy(rows, buffer.at[which, part], sems.at[which, part])

    @pl.when(step == 0)
    def _():
        for part in range(steps):
            copy(k_hbm, 0, part).start()
            copy(v_hbm, 1, part).start()

    for which, source in ((0, k_hbm), (1, v_hbm)):
        copy(source, which, step).wait()
        wide[...] = buffer[which, step].astype(F32)
        for a in range(heads):
            part = wide[pl.ds(a, count, stride=heads), :]
            if which == 0:
                kt_ref[a] = part.T.astype(BF)
            else:
                vs_ref[a] = part.astype(BF)


def split_heads(keys, values):
    count, heads, dim = keys.shape
    steps = 4
    each = count // steps
    return pl.pallas_call(
        functools.partial(split_kernel, heads, steps),
        out_shape=[
            jax.ShapeDtypeStruct((heads, dim, count), BF),
            jax.ShapeDtypeStruct((heads, count, dim), BF),
        ],
        grid=(steps,),
        in_specs=[pl.BlockSpec(memory_space=pl.ANY)] * 2,
        out_specs=[
            pl.BlockSpec((heads, dim, each), lambda i: (0, 0, i)),
            pl.BlockSpec((heads, each, dim), lambda i: (0, i, 0)),
        ],
        scratch_shapes=[
            pltpu.VMEM((2, steps, each * heads, dim), BF),
            pltpu.VMEM((each * heads, dim), F32),
            pltpu.SemaphoreType.DMA((2, steps)),
        ],
        compiler_params=params(52),
        cost_estimate=SMALL,
        name="split_heads",
    )(keys.reshape(count * heads, dim), values.reshape(count * heads, dim))


def attend_kernel(capacity, per, group, block, chunk, count, outs, at_ref, *refs):
    del at_ref
    q_refs, (k_hbm, v_hbm) = refs[:count], refs[count : count + 2]
    o_refs, (acc_ref, weight_ref, k_ref, v_ref, sems) = refs[-5 - outs : -5], refs[-5:]
    heads, dim, keys = k_ref.shape
    turn = pl.program_id(0)

    def pieces():
        for a in range(heads):
            for first, last in [(0, block), (block, keys)] if a == 0 else [(0, keys)]:
                if first < last:
                    yield a, first, last

    def copies(n, a, first, last):
        span = pl.ds(first, last - first)
        return [
            pltpu.make_async_copy(k_hbm.at[a, :, span], k_ref.at[a, :, span], sems.at[n, 0]),
            pltpu.make_async_copy(v_hbm.at[a, span, :], v_ref.at[a, span, :], sems.at[n, 1]),
        ]

    @pl.when(turn == 0)
    def _():
        for n, piece in enumerate(pieces()):
            for copy in copies(n, *piece):
                copy.start()

    def arrive(a, j):
        for n, piece in enumerate(pieces()):
            if piece[:2] == (a, j * block):

                @pl.when(turn == 0)
                def _():
                    for copy in copies(n, *piece):
                        copy.wait()

    total = rows = capacity * per
    each = rows // heads
    scale = dim**-0.5 * math.log2(math.e)
    ones = jnp.ones((block, dim), BF)
    grid = q_refs[0][...].astype(F32)
    for t in range(1, count):
        grid = jnp.where(turn == t, q_refs[t][...].astype(F32), grid)
    grid = grid.reshape(total // (heads * group), heads, group, dim)
    queries = [grid[:, a].reshape(each, dim).astype(BF) for a in range(heads)]

    def scores(a, j):
        part = k_ref[a, :, pl.ds(j * block, block)]
        return jnp.dot(queries[a], part, preferred_element_type=F32)

    def values(a, j):
        return jnp.concatenate([v_ref[a, pl.ds(j * block, block), :], ones], axis=1)

    def natural(parts):
        split = [x.reshape(each // group, 1, group, dim) for x in parts]
        return jnp.concatenate(split, axis=1).reshape(total, dim)

    def finish(shifts):
        sums = [acc_ref[a, :, dim:] for a in range(heads)]
        out = natural([acc_ref[a, :, :dim] / sums[a] for a in range(heads)]).astype(BF)
        log_sum = natural([shifts[a] + jnp.log2(sums[a]) for a in range(heads)])
        high = log_sum.astype(BF).astype(F32)
        lane = lax.broadcasted_iota(jnp.int32, (total, dim), 1)
        row = lax.broadcasted_iota(jnp.int32, (total, dim), 0)
        term = jnp.where(lane < per, high, log_sum - high)
        term = jnp.where((lane % per == row % per) & (lane < 2 * per), term, 0.0).astype(BF)
        slot = lax.broadcasted_iota(jnp.int32, (EXTRA, rows), 0)
        source = lax.broadcasted_iota(jnp.int32, (EXTRA, rows), 1) // per
        pick = jnp.where(source == slot, 1.0, 0.0).astype(BF)
        logs = jnp.dot(pick, term, preferred_element_type=F32).astype(BF)
        for t, o_ref in enumerate(o_refs):

            @pl.when(turn == t)
            def _():
                o_ref[:rows, :] = out
                o_ref[rows:, :] = logs

    turns = keys // block
    steps = block // chunk

    def middle(part):
        weights = jnp.exp2(part - jnp.max(part, axis=1, keepdims=True))
        total = jnp.sum(weights, axis=1, keepdims=True)
        return jnp.sum(weights * part, axis=1, keepdims=True) / total

    def accumulate(a, j):
        slot = (a * turns + j) % 2
        part = jnp.dot(weight_ref[slot], values(a, j), preferred_element_type=F32)
        if j == 0:
            acc_ref[a] = part
        else:
            acc_ref[a] += part

    shifts = []
    before = None
    for a in range(heads):
        for j in range(turns):
            arrive(a, j)
            slot = (a * turns + j) % 2
            for c in range(steps):
                first = j * block + c * chunk
                part = jnp.dot(
                    queries[a], k_ref[a, :, first : first + chunk], preferred_element_type=F32
                )
                if first == 0:
                    shifts.append(middle(part * scale))
                weights = jnp.exp2((part * scale - shifts[a]).astype(BF))
                weight_ref[slot, :, c * chunk : (c + 1) * chunk] = weights
            if before is not None:
                accumulate(*before)
            before = (a, j)
    accumulate(*before)
    finish(shifts)
    fits = jnp.max(acc_ref[:, :, dim:]) < LIMIT

    @pl.when(jnp.logical_not(fits))
    def _():
        acc_ref[...] = jnp.zeros_like(acc_ref)
        tops = []
        for a in range(heads):

            def step(j, top):
                part = scores(a, j) * scale
                new = jnp.maximum(top, jnp.max(part, axis=1, keepdims=True))
                weights = jnp.exp2(part - new).astype(BF)
                acc_ref[a] = acc_ref[a] * jnp.exp2(top - new) + jnp.dot(
                    weights, values(a, j), preferred_element_type=F32
                )
                return new

            tops.append(lax.fori_loop(0, turns, step, jnp.full((each, 1), -1e30, F32)))
        finish(tops)


def attend(queries, keys_t, values, at, capacity, per, group, *before):
    dim = queries[0].shape[1]
    heads, keys, _ = values.shape
    rows = capacity * per
    count = len(queries)
    blocks = count if count > 1 else queries[0].shape[0] // rows
    block = min(1024, keys)
    chunk = min(256, block)
    place = (lambda i, s: (0, 0)) if count > 1 else (lambda i, s: (s[0] ^ i, 0))
    out = jax.ShapeDtypeStruct((rows + EXTRA, dim), BF)
    return pl.pallas_call(
        functools.partial(attend_kernel, capacity, per, group, block, chunk, count, blocks),
        out_shape=[out] * blocks,
        grid_spec=pltpu.PrefetchScalarGridSpec(
            num_scalar_prefetch=1,
            grid=(blocks,),
            in_specs=[pl.BlockSpec((rows, dim), place)] * count
            + [pl.BlockSpec(memory_space=pl.ANY)] * (2 + len(before)),
            out_specs=[pl.BlockSpec(out.shape, lambda i, s: (0, 0))] * blocks,
            scratch_shapes=[
                pltpu.VMEM((heads, rows // heads, 2 * dim), F32),
                pltpu.VMEM((2, rows // heads, block), BF),
                pltpu.VMEM(keys_t.shape, BF),
                pltpu.VMEM(values.shape, BF),
                pltpu.SemaphoreType.DMA((heads + 1, 2)),
            ],
        ),
        compiler_params=params(60),
        cost_estimate=SMALL,
        name="attend_prefix",
    )(at, *queries, keys_t, values, *before)


def visibility(lengths, draft_count, suffix_count):
    position = jnp.arange(suffix_count + draft_count, dtype=jnp.int32)
    draft_pos = jnp.arange(draft_count, dtype=jnp.int32)
    earlier = position[None, None, :] < lengths[:, None, None]
    earlier = earlier & (position[None, None, :] < suffix_count)
    fresh = (position[None, :] >= suffix_count) & (
        position[None, :] - suffix_count <= draft_pos[:, None]
    )
    return earlier | fresh[None, :, :]


def local_attention(query_grid, key_rows, value_rows, visible):
    scale = query_grid.shape[-1] ** (-0.5)
    scores = (
        jnp.einsum("rtagd,rjad->rtagj", query_grid, key_rows, preferred_element_type=F32) * scale
    )
    visible_mask = visible[:, :, None, None, :]
    scores = jnp.where(visible_mask, scores, F32(-1e30))
    top = jnp.max(scores, axis=-1)
    exponent = jnp.where(visible_mask, jnp.exp(scores - top[..., None]), F32(0.0))
    denominator = jnp.sum(exponent, axis=-1)
    summed = jnp.einsum(
        "rtagj,rjad->rtagd", exponent.astype(BF), value_rows, preferred_element_type=F32
    )
    return summed / denominator[..., None], (top + jnp.log(denominator)) * F32(math.log2(math.e))


def fetch(weight, shards, buffer, sems, width):
    count, _, block = buffer.shape
    each = width // block
    copies = []
    for n in range(count):
        column = pl.multiple_of(shards[n // each] * width + (n % each) * block, block)
        source = weight.at[:, pl.ds(column, block)]
        copies.append(pltpu.make_async_copy(source, buffer.at[n], sems.at[n]))
        copies[-1].start()
    return copies


def multiply(att, copies, buffer, outs):
    block = buffer.shape[2]
    each = len(copies) // len(outs)
    rows = att[...]
    for n, copy in enumerate(copies):
        copy.wait()
        product = jnp.dot(rows, buffer[n], preferred_element_type=F32).astype(BF)
        outs[n // each][:, n % each * block : (n % each + 1) * block] = product


def join_kernel(capacity, count, base, shares, order, target, shards, *refs):
    received, (local, local_log, weight) = refs[:count], refs[count : count + 3]
    att, *outs = refs[-8 - shares - 1 : -8]
    blocks, block_logs, part, mine, logs, spread, buffer, sems = refs[-8:]
    copies = fetch(weight, shards, buffer, sems, outs[0].shape[1])
    rows, per, dim = part.shape
    held = capacity * per
    heads = att.shape[1] // dim
    draft = per // heads
    done = 0
    for array in received:
        for first in range(0, array.shape[0], held + EXTRA):
            values = array[first : first + held, :].astype(F32)
            blocks[done * capacity : (done + 1) * capacity] = values.reshape(capacity, per, dim)
            last = array[first + held : first + held + EXTRA, :].astype(F32)
            block_logs[done * EXTRA : (done + 1) * EXTRA] = last
            done += 1

    def gather(i, _):
        at = order[base + i]
        slot = target[base + i]
        part[i] = blocks[slot]
        mine[i] = local[at].astype(F32)
        place = (slot // capacity) * EXTRA + slot % capacity
        logs[0, pl.ds(i, 1), :] = block_logs[pl.ds(place, 1), :]
        logs[1, pl.ds(i, 1), :] = local_log[pl.ds(at, 1), :]
        return 0

    lax.fori_loop(0, rows, gather, 0)
    lane = lax.broadcasted_iota(jnp.int32, (rows, dim), 1)
    first = logs[0] + pltpu.roll(logs[0], dim - per, axis=1)
    share = 1.0 / (1.0 + jnp.exp2(logs[1] - first))
    high = share.astype(BF).astype(F32)
    low = pltpu.roll(share - high, per, axis=1)
    logs[0] = jnp.where(lane < per, high, jnp.where(lane < 2 * per, low, 0.0))
    diagonal = lax.broadcasted_iota(jnp.int32, (per, dim), 1) % per
    diagonal = diagonal == lax.broadcasted_iota(jnp.int32, (per, dim), 0)

    def widen(i, _):
        row = logs[0, pl.ds(i, 1), :]
        spread[i] = jnp.where(diagonal, row, 0.0).astype(BF)
        return 0

    lax.fori_loop(0, rows, widen, 0)
    ones = jnp.ones((dim, dim), BF)
    shares = jnp.dot(
        spread[...].reshape(rows * per, dim), ones, preferred_element_type=F32
    ).reshape(rows, per, dim)
    part[...] = mine[...] + shares * (part[...] - mine[...])
    flat = part.reshape(rows * per, dim)
    for h in range(heads):
        head = flat[pl.ds(h, rows * draft, stride=heads), :]
        att[:, h * dim : (h + 1) * dim] = head.astype(BF)


    multiply(att, copies, buffer, outs)


def join(
    received, local, local_log, order, target, heads, base, rows, capacity, weight, shards, width, *before
):
    count = len(received)
    per, dim = local.shape[1:]
    blocks = sum(array.shape[0] for array in received) // (capacity * per + EXTRA)
    shares = shards.shape[0]
    lines = rows * per // heads
    block = min(256, width)
    whole = lambda array: pl.BlockSpec(array.shape, lambda n, *_: (0,) * array.ndim)
    att = jax.ShapeDtypeStruct((lines, heads * dim), BF)
    out = jax.ShapeDtypeStruct((lines, width), BF)
    return pl.pallas_call(
        functools.partial(join_kernel, capacity, count, base, shares),
        out_shape=[att] + [out] * shares,
        grid_spec=pltpu.PrefetchScalarGridSpec(
            num_scalar_prefetch=3,
            grid=(1,),
            in_specs=[whole(array) for array in received]
            + [whole(local), whole(local_log)]
            + [pl.BlockSpec(memory_space=pl.ANY)] * (1 + len(before)),
            out_specs=[whole(att)] + [whole(out)] * shares,
            scratch_shapes=[
                pltpu.VMEM((blocks * capacity, per, dim), F32),
                pltpu.VMEM((blocks * EXTRA, dim), F32),
                pltpu.VMEM((rows, per, dim), F32),
                pltpu.VMEM((rows, per, dim), F32),
                pltpu.VMEM((2, rows, dim), F32),
                pltpu.VMEM((rows, per, dim), BF),
                pltpu.VMEM((shares * width // block, heads * dim, block), BF),
                pltpu.SemaphoreType.DMA((shares * width // block,)),
            ],
        ),
        compiler_params=params(48),
        cost_estimate=SMALL,
        name="join_project",
    )(order, target, shards, *received, local, local_log, weight, *before)


def project_kernel(shares, shards, att, weight, *refs):
    outs, (buffer, sems) = refs[-2 - shares : -2], refs[-2:]
    multiply(att, fetch(weight, shards, buffer, sems, outs[0].shape[1]), buffer, outs)


def project(att, weight, shards, width, *before):
    rows, depth = att.shape
    shares = shards.shape[0]
    block = min(256, width)
    out = jax.ShapeDtypeStruct((rows, width), BF)
    whole = lambda array: pl.BlockSpec(array.shape, lambda n, *_: (0,) * array.ndim)
    return pl.pallas_call(
        functools.partial(project_kernel, shares),
        out_shape=[out] * shares,
        grid_spec=pltpu.PrefetchScalarGridSpec(
            num_scalar_prefetch=1,
            grid=(1,),
            in_specs=[whole(att)] + [pl.BlockSpec(memory_space=pl.ANY)] * (1 + len(before)),
            out_specs=[whole(out)] * shares,
            scratch_shapes=[
                pltpu.VMEM((shares * width // block, depth, block), BF),
                pltpu.SemaphoreType.DMA((shares * width // block,)),
            ],
        ),
        compiler_params=params(48),
        cost_estimate=SMALL,
        name="project",
    )(shards, att, weight, *before)


def project_sum(join_with, weight, own, split, before):
    size = lax.axis_size("tensor")
    chips = size // 2
    width = weight.shape[1] // size
    order = list(range(1, chips)) + [0]
    shards = [own ^ (2 * d + other) for d in order for other in (1, 0)]
    with_join = 1 if split else len(shards)
    att, *products = join_with(jnp.stack(shards[:with_join]), width)
    got, sums = [], []
    for k, d in enumerate(order):
        while len(products) < 2 * k + 2:
            waits = sums + (before if d == 0 else [])
            products += project(att, weight, shards[len(products)][None], width, *waits)
        send, keep = products[2 * k : 2 * k + 2]
        there = lax.ppermute(send, "tensor", [(i, i ^ 1) for i in range(size)])
        if d:
            total = (keep.astype(F32) + there.astype(F32)).astype(BF)
            sums.append(total)
            got.append(lax.ppermute(total, "tensor", [(i, i ^ (2 * d)) for i in range(size)]))
    total = keep.astype(F32)
    for term in got:
        total = total + term.astype(F32)
    return [total, there], [total], keep


def arrange_kernel(counts, place_ref, *refs):
    out_ref = refs[-1]
    rows, draft, _ = out_ref.shape
    halves, start = [], 0
    for count in counts:
        total = refs[start][...]
        for term in refs[start + 1 : start + count]:
            total = total + term[...].astype(F32)
        halves.append(total.astype(BF))
        start += count
    values = jnp.concatenate(halves, axis=0)
    size = rows * draft
    pick = lax.broadcasted_iota(jnp.int32, (size, size), 1) == place_ref[...]
    result = jnp.dot(
        jnp.where(pick, 1.0, 0.0).astype(BF), values, preferred_element_type=F32
    )
    for r in range(rows):
        out_ref[r] = result[r * draft : (r + 1) * draft].astype(BF)


def arrange(halves, place, rows, draft):
    width = halves[0][0].shape[1]
    index = (place[:, None] * draft + jnp.arange(draft, dtype=jnp.int32)[None, :]).reshape(-1, 1)
    return pl.pallas_call(
        functools.partial(arrange_kernel, [len(half) for half in halves]),
        out_shape=jax.ShapeDtypeStruct((rows, draft, width), BF),
        compiler_params=params(20),
        cost_estimate=SMALL,
        name="arrange_rows",
    )(index, *[term for half in halves for term in half])


def exchange(x):
    size = lax.axis_size("dp")
    groups = [list(range(size // 2)), list(range(size // 2, size))]
    return lax.all_to_all(
        x, "dp", split_axis=0, concat_axis=0, axis_index_groups=groups, tiled=True
    )


def hop(x, shift):
    size = lax.axis_size("dp")
    return lax.ppermute(x, "dp", [(i, i ^ shift) for i in range(size)])


def body(
    queries,
    draft_keys,
    draft_values,
    suffix_keys,
    suffix_values,
    suffix_len,
    prefix_keys,
    prefix_values,
    row_prefix,
    prefix_slot,
    out_weight,
):
    row_count, draft, query_heads, dim = queries.shape
    heads = draft_keys.shape[2]
    group = query_heads // heads
    per = draft * query_heads
    suffix_count = suffix_keys.shape[1]
    peers = lax.axis_size("dp")
    capacity = 2 * row_count // peers
    own = lax.axis_index("tensor").astype(jnp.int32)
    me = lax.axis_index("dp").astype(jnp.int32)

    slot_row, place, order, target = route(row_prefix, prefix_slot, me, peers, capacity)
    half = peers // 2
    lead = half // 2
    first = pack(queries, slot_row, [(half + d, 1) for d in range(lead)], capacity)
    near, *late = pack(
        queries,
        slot_row,
        [(0, half)] + [(half + d, 1) for d in range(lead, half)],
        capacity,
        first[0],
    )
    far = [hop(x, half + d) for d, x in enumerate(first + late)]
    near = exchange(near)

    keys_t, values = split_heads(prefix_keys[0], prefix_values[0])
    here = (me % half).reshape(1)
    zero = jnp.zeros((1,), jnp.int32)
    back, before = [None] * peers, []
    for batch in [range(half, half + lead), range(half)] + [[d] for d in range(half + lead, peers)]:
        arrays = [near] if batch[0] == 0 else [far[d - half] for d in batch]
        if batch[-1] == peers - 1:
            before = list(before) + back[half : half + lead]
        at = here if batch[0] == 0 else zero
        results = attend(arrays, keys_t, values, at, capacity, per, group, *before)
        before = results[:1]
        for d, result in zip(batch, results):
            back[d] = hop(result, d) if d else result

    query_grid = queries.reshape(row_count, draft, heads, group, dim)
    all_keys = jnp.concatenate([suffix_keys, draft_keys], axis=1)
    all_values = jnp.concatenate([suffix_values, draft_values], axis=1)
    visible = visibility(suffix_len, draft, suffix_count)
    local, local_log = local_attention(query_grid, all_keys, all_values, visible)
    local = local.reshape(row_count, per, dim).astype(BF)
    local_log = jnp.pad(local_log.reshape(row_count, per), ((0, 0), (0, dim - per)))

    rows = row_count // 2
    early = peers - rows // capacity
    outs, waits = [], []
    for base in (0, rows):
        received = back if base else back[:early]

        def join_with(shards, width):
            return join(
                received,
                local,
                local_log,
                order,
                target,
                query_heads,
                base,
                rows,
                capacity,
                out_weight,
                shards,
                width,
                *before,
            )

        terms, waits, product = project_sum(join_with, out_weight, own, base > 0, waits)
        before = [product]
        outs.append(terms)
    return arrange(outs, place, row_count, draft)


def solution(mesh):
    placed = (
        P("dp", None, "tensor", None),
        P("dp", None, "tensor", None),
        P("dp", None, "tensor", None),
        P("dp", None, "tensor", None),
        P("dp", None, "tensor", None),
        P("dp"),
        P("dp", None, "tensor", None),
        P("dp", None, "tensor", None),
        P("dp", None),
        P(),
        P("tensor", None),
    )
    return jax.shard_map(
        body, mesh=mesh, in_specs=placed, out_specs=P("dp", None, "tensor"), check_vma=False
    )
```

```python
import functools
import math

import jax
import jax.numpy as jnp
from jax import lax
from jax.experimental import pallas as pl
from jax.experimental.pallas import tpu as pltpu
from jax.sharding import PartitionSpec as P

BF = jnp.bfloat16
F32 = jnp.float32
EXTRA = 16
LIMIT = 1e30
SMALL = pl.CostEstimate(flops=1 << 20, bytes_accessed=1 << 10, transcendentals=0)


def params(mebibytes):
    return pltpu.CompilerParams(vmem_limit_bytes=mebibytes * 1024 * 1024)


def route(row_prefix, prefix_slot, me, peers, capacity):
    rows = row_prefix.shape[0]
    prefixes = prefix_slot.shape[0]
    name = row_prefix[:, 0]
    row = jnp.arange(rows, dtype=jnp.int32)
    owner = jnp.sum(
        jnp.where(
            row_prefix == jnp.arange(prefixes, dtype=jnp.int32)[None, :], prefix_slot[None, :], 0
        ),
        axis=1,
    )
    same = (name[:, None] == name[None, :]) & (row[None, :] < row[:, None])
    rank = jnp.sum(same.astype(jnp.int32), axis=1)
    half = peers // 2
    shift = owner ^ me
    sent = jnp.where(shift < half, owner % half, shift) * capacity + rank
    target = shift * capacity + rank
    slots = jnp.arange(peers * capacity, dtype=jnp.int32)
    slot_row = jnp.sum(jnp.where(sent[None, :] == slots[:, None], row[None, :], 0), axis=1)
    place = jnp.sum((target[None, :] < target[:, None]).astype(jnp.int32), axis=1)
    at = place[None, :] == row[:, None]
    order = jnp.sum(jnp.where(at, row[None, :], 0), axis=1)
    order_target = jnp.sum(jnp.where(at, target[None, :], 0), axis=1)
    return slot_row, place, order, order_target


def pack_kernel(pieces, capacity, slot_row, q_ref, *refs):
    outs = refs[-len(pieces) :]

    def one(k, _):
        for (first, blocks), out in zip(pieces, outs):
            for b in range(blocks):
                out[b * capacity + k] = q_ref[slot_row[(first + b) * capacity + k]]
        return 0

    lax.fori_loop(0, capacity, one, 0)


def pack(queries, slot_row, pieces, capacity, *before):
    shapes = [
        jax.ShapeDtypeStruct((blocks * capacity,) + queries.shape[1:], BF) for _, blocks in pieces
    ]
    whole = lambda array: pl.BlockSpec(array.shape, lambda i, s: (0, 0, 0, 0))
    packed = pl.pallas_call(
        functools.partial(pack_kernel, pieces, capacity),
        out_shape=shapes,
        grid_spec=pltpu.PrefetchScalarGridSpec(
            num_scalar_prefetch=1,
            grid=(1,),
            in_specs=[whole(queries)] + [pl.BlockSpec(memory_space=pl.ANY)] * len(before),
            out_specs=[whole(shape) for shape in shapes],
        ),
        compiler_params=params(16),
        cost_estimate=SMALL,
        name="pack_queries",
    )(slot_row, queries, *before)
    return [x.reshape(-1, x.shape[-1]) for x in packed]


def split_kernel(heads, steps, k_hbm, v_hbm, kt_ref, vs_ref, buffer, wide, sems):
    step = pl.program_id(0)
    each = buffer.shape[2]
    count = each // heads

    def copy(source, which, part):
        rows = source.at[pl.ds(part * each, each), :]
        return pltpu.make_async_copy(rows, buffer.at[which, part], sems.at[which, part])

    @pl.when(step == 0)
    def _():
        for part in range(steps):
            copy(k_hbm, 0, part).start()
            copy(v_hbm, 1, part).start()

    for which, source in ((0, k_hbm), (1, v_hbm)):
        copy(source, which, step).wait()
        wide[...] = buffer[which, step].astype(F32)
        for a in range(heads):
            part = wide[pl.ds(a, count, stride=heads), :]
            if which == 0:
                kt_ref[a] = part.T.astype(BF)
            else:
                vs_ref[a] = part.astype(BF)


def split_heads(keys, values):
    count, heads, dim = keys.shape
    steps = 4
    each = count // steps
    return pl.pallas_call(
        functools.partial(split_kernel, heads, steps),
        out_shape=[
            jax.ShapeDtypeStruct((heads, dim, count), BF),
            jax.ShapeDtypeStruct((heads, count, dim), BF),
        ],
        grid=(steps,),
        in_specs=[pl.BlockSpec(memory_space=pl.ANY)] * 2,
        out_specs=[
            pl.BlockSpec((heads, dim, each), lambda i: (0, 0, i)),
            pl.BlockSpec((heads, each, dim), lambda i: (0, i, 0)),
        ],
        scratch_shapes=[
            pltpu.VMEM((2, steps, each * heads, dim), BF),
            pltpu.VMEM((each * heads, dim), F32),
            pltpu.SemaphoreType.DMA((2, steps)),
        ],
        compiler_params=params(52),
        cost_estimate=SMALL,
        name="split_heads",
    )(keys.reshape(count * heads, dim), values.reshape(count * heads, dim))


def attend_kernel(capacity, per, group, block, chunk, count, outs, at_ref, *refs):
    del at_ref
    q_refs, (k_hbm, v_hbm) = refs[:count], refs[count : count + 2]
    o_refs, (acc_ref, weight_ref, k_ref, v_ref, sems) = refs[-5 - outs : -5], refs[-5:]
    heads, dim, keys = k_ref.shape
    turn = pl.program_id(0)

    copies = [
        pltpu.make_async_copy(k_hbm, k_ref, sems.at[0]),
        pltpu.make_async_copy(v_hbm, v_ref, sems.at[1]),
    ]

    @pl.when(turn == 0)
    def _():
        for copy in copies:
            copy.start()
        for copy in copies:
            copy.wait()

    total = rows = capacity * per
    each = rows // heads
    scale = dim**-0.5 * math.log2(math.e)
    ones = jnp.ones((block, dim), BF)
    grid = q_refs[0][...].astype(F32)
    for t in range(1, count):
        grid = jnp.where(turn == t, q_refs[t][...].astype(F32), grid)
    grid = grid.reshape(total // (heads * group), heads, group, dim)
    queries = [grid[:, a].reshape(each, dim).astype(BF) for a in range(heads)]

    def scores(a, j):
        part = k_ref[a, :, pl.ds(j * block, block)]
        return jnp.dot(queries[a], part, preferred_element_type=F32)

    def values(a, j):
        return jnp.concatenate([v_ref[a, pl.ds(j * block, block), :], ones], axis=1)

    def natural(parts):
        split = [x.reshape(each // group, 1, group, dim) for x in parts]
        return jnp.concatenate(split, axis=1).reshape(total, dim)

    def finish(shifts):
        sums = [acc_ref[a, :, dim:] for a in range(heads)]
        out = natural([acc_ref[a, :, :dim] / sums[a] for a in range(heads)]).astype(BF)
        log_sum = natural([shifts[a] + jnp.log2(sums[a]) for a in range(heads)])
        high = log_sum.astype(BF).astype(F32)
        lane = lax.broadcasted_iota(jnp.int32, (total, dim), 1)
        row = lax.broadcasted_iota(jnp.int32, (total, dim), 0)
        term = jnp.where(lane < per, high, log_sum - high)
        term = jnp.where((lane % per == row % per) & (lane < 2 * per), term, 0.0).astype(BF)
        slot = lax.broadcasted_iota(jnp.int32, (EXTRA, rows), 0)
        source = lax.broadcasted_iota(jnp.int32, (EXTRA, rows), 1) // per
        pick = jnp.where(source == slot, 1.0, 0.0).astype(BF)
        logs = jnp.dot(pick, term, preferred_element_type=F32).astype(BF)
        for t, o_ref in enumerate(o_refs):

            @pl.when(turn == t)
            def _():
                o_ref[:rows, :] = out
                o_ref[rows:, :] = logs

    turns = keys // block
    steps = block // chunk

    def accumulate(a, j):
        slot = (j * heads + a) % 2
        part = jnp.dot(weight_ref[slot], values(a, j), preferred_element_type=F32)
        if j == 0:
            acc_ref[a] = part
        else:
            acc_ref[a] += part

    def chunk_scores(a, first):
        part = k_ref[a, :, first : first + chunk]
        return jnp.dot(queries[a], part, preferred_element_type=F32)

    opening = [chunk_scores(a, 0) for a in range(heads)]
    shifts = [jnp.max(x, axis=1, keepdims=True) * scale - 3.0 for x in opening]
    before = None
    for j in range(turns):
        for a in range(heads):
            slot = (j * heads + a) % 2
            for c in range(steps):
                first = j * block + c * chunk
                part = chunk_scores(a, first) if first else opening[a]
                weights = jnp.exp2((part * scale - shifts[a]).astype(BF))
                weight_ref[slot, :, c * chunk : (c + 1) * chunk] = weights
            if before is not None:
                accumulate(*before)
            before = (a, j)
    accumulate(*before)
    finish(shifts)
    fits = jnp.max(acc_ref[:, :, dim:]) < LIMIT

    @pl.when(jnp.logical_not(fits))
    def _():
        acc_ref[...] = jnp.zeros_like(acc_ref)
        tops = []
        for a in range(heads):

            def step(j, top):
                part = scores(a, j) * scale
                new = jnp.maximum(top, jnp.max(part, axis=1, keepdims=True))
                weights = jnp.exp2(part - new).astype(BF)
                acc_ref[a] = acc_ref[a] * jnp.exp2(top - new) + jnp.dot(
                    weights, values(a, j), preferred_element_type=F32
                )
                return new

            tops.append(lax.fori_loop(0, turns, step, jnp.full((each, 1), -1e30, F32)))
        finish(tops)


def attend(queries, keys_t, values, at, capacity, per, group, *before):
    dim = queries[0].shape[1]
    heads, keys, _ = values.shape
    rows = capacity * per
    count = len(queries)
    blocks = count if count > 1 else queries[0].shape[0] // rows
    block = min(1024, keys)
    chunk = min(256, block)
    place = (lambda i, s: (0, 0)) if count > 1 else (lambda i, s: (s[0] ^ i, 0))
    out = jax.ShapeDtypeStruct((rows + EXTRA, dim), BF)
    return pl.pallas_call(
        functools.partial(attend_kernel, capacity, per, group, block, chunk, count, blocks),
        out_shape=[out] * blocks,
        grid_spec=pltpu.PrefetchScalarGridSpec(
            num_scalar_prefetch=1,
            grid=(blocks,),
            in_specs=[pl.BlockSpec((rows, dim), place)] * count
            + [pl.BlockSpec(memory_space=pl.ANY)] * (2 + len(before)),
            out_specs=[pl.BlockSpec(out.shape, lambda i, s: (0, 0))] * blocks,
            scratch_shapes=[
                pltpu.VMEM((heads, rows // heads, 2 * dim), F32),
                pltpu.VMEM((2, rows // heads, block), BF),
                pltpu.VMEM(keys_t.shape, BF),
                pltpu.VMEM(values.shape, BF),
                pltpu.SemaphoreType.DMA((2,)),
            ],
        ),
        compiler_params=params(60),
        cost_estimate=SMALL,
        name="attend_prefix",
    )(at, *queries, keys_t, values, *before)


def visibility(lengths, draft_count, suffix_count):
    position = jnp.arange(suffix_count + draft_count, dtype=jnp.int32)
    draft_pos = jnp.arange(draft_count, dtype=jnp.int32)
    earlier = position[None, None, :] < lengths[:, None, None]
    earlier = earlier & (position[None, None, :] < suffix_count)
    fresh = (position[None, :] >= suffix_count) & (
        position[None, :] - suffix_count <= draft_pos[:, None]
    )
    return earlier | fresh[None, :, :]


def local_attention(query_grid, key_rows, value_rows, visible):
    scale = query_grid.shape[-1] ** (-0.5)
    scores = (
        jnp.einsum("rtagd,rjad->rtagj", query_grid, key_rows, preferred_element_type=F32) * scale
    )
    visible_mask = visible[:, :, None, None, :]
    scores = jnp.where(visible_mask, scores, F32(-1e30))
    top = jnp.max(scores, axis=-1)
    exponent = jnp.where(visible_mask, jnp.exp(scores - top[..., None]), F32(0.0))
    denominator = jnp.sum(exponent, axis=-1)
    summed = jnp.einsum(
        "rtagj,rjad->rtagd", exponent.astype(BF), value_rows, preferred_element_type=F32
    )
    return summed / denominator[..., None], (top + jnp.log(denominator)) * F32(math.log2(math.e))


def fetch(weight, shards, buffer, sems, width):
    count, _, block = buffer.shape
    each = width // block
    copies = []
    for n in range(count):
        column = pl.multiple_of(shards[n // each] * width + (n % each) * block, block)
        source = weight.at[:, pl.ds(column, block)]
        copies.append(pltpu.make_async_copy(source, buffer.at[n], sems.at[n]))
        copies[-1].start()
    return copies


def multiply(att, copies, buffer, outs):
    block = buffer.shape[2]
    each = len(copies) // len(outs)
    rows = att[...]
    for n, copy in enumerate(copies):
        copy.wait()
        product = jnp.dot(rows, buffer[n], preferred_element_type=F32).astype(BF)
        outs[n // each][:, n % each * block : (n % each + 1) * block] = product


def join_kernel(capacity, count, base, shares, order, target, shards, *refs):
    received, (local, local_log, weight) = refs[:count], refs[count : count + 3]
    att, *outs = refs[-8 - shares - 1 : -8]
    blocks, block_logs, part, mine, logs, spread, buffer, sems = refs[-8:]
    copies = fetch(weight, shards, buffer, sems, outs[0].shape[1])
    rows, per, dim = part.shape
    held = capacity * per
    heads = att.shape[1] // dim
    draft = per // heads
    done = 0
    for array in received:
        for first in range(0, array.shape[0], held + EXTRA):
            values = array[first : first + held, :].astype(F32)
            blocks[done * capacity : (done + 1) * capacity] = values.reshape(capacity, per, dim)
            last = array[first + held : first + held + EXTRA, :].astype(F32)
            block_logs[done * EXTRA : (done + 1) * EXTRA] = last
            done += 1

    def gather(i, _):
        at = order[base + i]
        slot = target[base + i]
        part[i] = blocks[slot]
        mine[i] = local[at].astype(F32)
        place = (slot // capacity) * EXTRA + slot % capacity
        logs[0, pl.ds(i, 1), :] = block_logs[pl.ds(place, 1), :]
        logs[1, pl.ds(i, 1), :] = local_log[pl.ds(at, 1), :]
        return 0

    lax.fori_loop(0, rows, gather, 0)
    lane = lax.broadcasted_iota(jnp.int32, (rows, dim), 1)
    first = logs[0] + pltpu.roll(logs[0], dim - per, axis=1)
    share = 1.0 / (1.0 + jnp.exp2(logs[1] - first))
    high = share.astype(BF).astype(F32)
    low = pltpu.roll(share - high, per, axis=1)
    logs[0] = jnp.where(lane < per, high, jnp.where(lane < 2 * per, low, 0.0))
    diagonal = lax.broadcasted_iota(jnp.int32, (per, dim), 1) % per
    diagonal = diagonal == lax.broadcasted_iota(jnp.int32, (per, dim), 0)

    def widen(i, _):
        row = logs[0, pl.ds(i, 1), :]
        spread[i] = jnp.where(diagonal, row, 0.0).astype(BF)
        return 0

    lax.fori_loop(0, rows, widen, 0)
    ones = jnp.ones((dim, dim), BF)
    shares = jnp.dot(
        spread[...].reshape(rows * per, dim), ones, preferred_element_type=F32
    ).reshape(rows, per, dim)
    part[...] = mine[...] + shares * (part[...] - mine[...])
    flat = part.reshape(rows * per, dim)
    for h in range(heads):
        head = flat[pl.ds(h, rows * draft, stride=heads), :]
        att[:, h * dim : (h + 1) * dim] = head.astype(BF)


    multiply(att, copies, buffer, outs)


def join(
    received, local, local_log, order, target, heads, base, rows, capacity, weight, shards, width, *before
):
    count = len(received)
    per, dim = local.shape[1:]
    blocks = sum(array.shape[0] for array in received) // (capacity * per + EXTRA)
    shares = shards.shape[0]
    lines = rows * per // heads
    block = min(256, width)
    whole = lambda array: pl.BlockSpec(array.shape, lambda n, *_: (0,) * array.ndim)
    att = jax.ShapeDtypeStruct((lines, heads * dim), BF)
    out = jax.ShapeDtypeStruct((lines, width), BF)
    return pl.pallas_call(
        functools.partial(join_kernel, capacity, count, base, shares),
        out_shape=[att] + [out] * shares,
        grid_spec=pltpu.PrefetchScalarGridSpec(
            num_scalar_prefetch=3,
            grid=(1,),
            in_specs=[whole(array) for array in received]
            + [whole(local), whole(local_log)]
            + [pl.BlockSpec(memory_space=pl.ANY)] * (1 + len(before)),
            out_specs=[whole(att)] + [whole(out)] * shares,
            scratch_shapes=[
                pltpu.VMEM((blocks * capacity, per, dim), F32),
                pltpu.VMEM((blocks * EXTRA, dim), F32),
                pltpu.VMEM((rows, per, dim), F32),
                pltpu.VMEM((rows, per, dim), F32),
                pltpu.VMEM((2, rows, dim), F32),
                pltpu.VMEM((rows, per, dim), BF),
                pltpu.VMEM((shares * width // block, heads * dim, block), BF),
                pltpu.SemaphoreType.DMA((shares * width // block,)),
            ],
        ),
        compiler_params=params(48),
        cost_estimate=SMALL,
        name="join_project",
    )(order, target, shards, *received, local, local_log, weight, *before)


def project_kernel(shares, shards, att, weight, *refs):
    outs, (buffer, sems) = refs[-2 - shares : -2], refs[-2:]
    multiply(att, fetch(weight, shards, buffer, sems, outs[0].shape[1]), buffer, outs)


def project(att, weight, shards, width, *before):
    rows, depth = att.shape
    shares = shards.shape[0]
    block = min(256, width)
    out = jax.ShapeDtypeStruct((rows, width), BF)
    whole = lambda array: pl.BlockSpec(array.shape, lambda n, *_: (0,) * array.ndim)
    return pl.pallas_call(
        functools.partial(project_kernel, shares),
        out_shape=[out] * shares,
        grid_spec=pltpu.PrefetchScalarGridSpec(
            num_scalar_prefetch=1,
            grid=(1,),
            in_specs=[whole(att)] + [pl.BlockSpec(memory_space=pl.ANY)] * (1 + len(before)),
            out_specs=[whole(out)] * shares,
            scratch_shapes=[
                pltpu.VMEM((shares * width // block, depth, block), BF),
                pltpu.SemaphoreType.DMA((shares * width // block,)),
            ],
        ),
        compiler_params=params(48),
        cost_estimate=SMALL,
        name="project",
    )(shards, att, weight, *before)


def project_sum(join_with, weight, own, split, before):
    size = lax.axis_size("tensor")
    chips = size // 2
    width = weight.shape[1] // size
    order = list(range(1, chips)) + [0]
    shards = [own ^ (2 * d + other) for d in order for other in (1, 0)]
    with_join = 1 if split else len(shards)
    att, *products = join_with(jnp.stack(shards[:with_join]), width)
    got, sums = [], []
    for k, d in enumerate(order):
        while len(products) < 2 * k + 2:
            waits = sums + (before if d == 0 else [])
            wanted = shards[len(products) :] if d == 0 else shards[len(products) : len(products) + 1]
            products += project(att, weight, jnp.stack(wanted), width, *waits)
        send, keep = products[2 * k : 2 * k + 2]
        there = lax.ppermute(send, "tensor", [(i, i ^ 1) for i in range(size)])
        if d:
            total = (keep.astype(F32) + there.astype(F32)).astype(BF)
            sums.append(total)
            got.append(lax.ppermute(total, "tensor", [(i, i ^ (2 * d)) for i in range(size)]))
    total = keep.astype(F32)
    for term in got:
        total = total + term.astype(F32)
    return [total, there], [total], keep


def arrange_kernel(counts, place_ref, *refs):
    out_ref = refs[-1]
    rows, draft, _ = out_ref.shape
    halves, start = [], 0
    for count in counts:
        total = refs[start][...]
        for term in refs[start + 1 : start + count]:
            total = total + term[...].astype(F32)
        halves.append(total.astype(BF))
        start += count
    values = jnp.concatenate(halves, axis=0)
    size = rows * draft
    pick = lax.broadcasted_iota(jnp.int32, (size, size), 1) == place_ref[...]
    result = jnp.dot(
        jnp.where(pick, 1.0, 0.0).astype(BF), values, preferred_element_type=F32
    )
    for r in range(rows):
        out_ref[r] = result[r * draft : (r + 1) * draft].astype(BF)


def arrange(halves, place, rows, draft):
    width = halves[0][0].shape[1]
    index = (place[:, None] * draft + jnp.arange(draft, dtype=jnp.int32)[None, :]).reshape(-1, 1)
    return pl.pallas_call(
        functools.partial(arrange_kernel, [len(half) for half in halves]),
        out_shape=jax.ShapeDtypeStruct((rows, draft, width), BF),
        compiler_params=params(20),
        cost_estimate=SMALL,
        name="arrange_rows",
    )(index, *[term for half in halves for term in half])


def exchange(x):
    size = lax.axis_size("dp")
    groups = [list(range(size // 2)), list(range(size // 2, size))]
    return lax.all_to_all(
        x, "dp", split_axis=0, concat_axis=0, axis_index_groups=groups, tiled=True
    )


def hop(x, shift):
    size = lax.axis_size("dp")
    return lax.ppermute(x, "dp", [(i, i ^ shift) for i in range(size)])


def body(
    queries,
    draft_keys,
    draft_values,
    suffix_keys,
    suffix_values,
    suffix_len,
    prefix_keys,
    prefix_values,
    row_prefix,
    prefix_slot,
    out_weight,
):
    row_count, draft, query_heads, dim = queries.shape
    heads = draft_keys.shape[2]
    group = query_heads // heads
    per = draft * query_heads
    suffix_count = suffix_keys.shape[1]
    peers = lax.axis_size("dp")
    capacity = 2 * row_count // peers
    own = lax.axis_index("tensor").astype(jnp.int32)
    me = lax.axis_index("dp").astype(jnp.int32)

    slot_row, place, order, target = route(row_prefix, prefix_slot, me, peers, capacity)
    half = peers // 2
    lead = half // 2
    first = pack(queries, slot_row, [(half + d, 1) for d in range(lead)], capacity)
    near, *late = pack(
        queries,
        slot_row,
        [(0, half)] + [(half + d, 1) for d in range(lead, half)],
        capacity,
        first[0],
    )
    far = [hop(x, half + d) for d, x in enumerate(first + late)]
    near = exchange(near)

    keys_t, values = split_heads(prefix_keys[0], prefix_values[0])
    here = (me % half).reshape(1)
    zero = jnp.zeros((1,), jnp.int32)
    back, before = [None] * peers, []
    for batch in [range(half, half + lead), range(half)] + [[d] for d in range(half + lead, peers)]:
        arrays = [near] if batch[0] == 0 else [far[d - half] for d in batch]
        if batch[-1] == peers - 1:
            before = list(before) + back[half : half + lead]
        at = here if batch[0] == 0 else zero
        results = attend(arrays, keys_t, values, at, capacity, per, group, *before)
        before = results[:1]
        for d, result in zip(batch, results):
            back[d] = hop(result, d) if d else result

    query_grid = queries.reshape(row_count, draft, heads, group, dim)
    all_keys = jnp.concatenate([suffix_keys, draft_keys], axis=1)
    all_values = jnp.concatenate([suffix_values, draft_values], axis=1)
    visible = visibility(suffix_len, draft, suffix_count)
    local, local_log = local_attention(query_grid, all_keys, all_values, visible)
    local = local.reshape(row_count, per, dim).astype(BF)
    local_log = jnp.pad(local_log.reshape(row_count, per), ((0, 0), (0, dim - per)))

    rows = row_count // 2
    early = peers - rows // capacity
    outs, waits = [], []
    for base in (0, rows):
        received = back if base else back[:early]

        def join_with(shards, width):
            return join(
                received,
                local,
                local_log,
                order,
                target,
                query_heads,
                base,
                rows,
                capacity,
                out_weight,
                shards,
                width,
                *before,
            )

        terms, waits, product = project_sum(join_with, out_weight, own, base > 0, waits)
        before = [product]
        outs.append(terms)
    return arrange(outs, place, row_count, draft)


def solution(mesh):
    placed = (
        P("dp", None, "tensor", None),
        P("dp", None, "tensor", None),
        P("dp", None, "tensor", None),
        P("dp", None, "tensor", None),
        P("dp", None, "tensor", None),
        P("dp"),
        P("dp", None, "tensor", None),
        P("dp", None, "tensor", None),
        P("dp", None),
        P(),
        P("tensor", None),
    )
    return jax.shard_map(
        body, mesh=mesh, in_specs=placed, out_specs=P("dp", None, "tensor"), check_vma=False
    )
```

```python
import functools
import math

import jax
import jax.numpy as jnp
from jax import lax
from jax.experimental import pallas as pl
from jax.experimental.pallas import tpu as pltpu
from jax.sharding import PartitionSpec as P

BF = jnp.bfloat16
F32 = jnp.float32
EXTRA = 16
LIMIT = 1e30
SMALL = pl.CostEstimate(flops=1 << 20, bytes_accessed=1 << 10, transcendentals=0)


def params(mebibytes):
    return pltpu.CompilerParams(vmem_limit_bytes=mebibytes * 1024 * 1024)


def route(row_prefix, prefix_slot, me, peers, capacity):
    rows = row_prefix.shape[0]
    prefixes = prefix_slot.shape[0]
    name = row_prefix[:, 0]
    row = jnp.arange(rows, dtype=jnp.int32)
    owner = jnp.sum(
        jnp.where(
            row_prefix == jnp.arange(prefixes, dtype=jnp.int32)[None, :], prefix_slot[None, :], 0
        ),
        axis=1,
    )
    same = (name[:, None] == name[None, :]) & (row[None, :] < row[:, None])
    rank = jnp.sum(same.astype(jnp.int32), axis=1)
    half = peers // 2
    shift = owner ^ me
    sent = jnp.where(shift < half, owner % half, shift) * capacity + rank
    target = shift * capacity + rank
    slots = jnp.arange(peers * capacity, dtype=jnp.int32)
    slot_row = jnp.sum(jnp.where(sent[None, :] == slots[:, None], row[None, :], 0), axis=1)
    place = jnp.sum((target[None, :] < target[:, None]).astype(jnp.int32), axis=1)
    at = place[None, :] == row[:, None]
    order = jnp.sum(jnp.where(at, row[None, :], 0), axis=1)
    order_target = jnp.sum(jnp.where(at, target[None, :], 0), axis=1)
    return slot_row, place, order, order_target


def pack_kernel(pieces, capacity, slot_row, marks, q_ref, *refs):
    del marks
    outs = refs[-len(pieces) :]

    def one(k, _):
        for (first, blocks), out in zip(pieces, outs):
            for b in range(blocks):
                out[b * capacity + k] = q_ref[slot_row[(first + b) * capacity + k]]
        return 0

    lax.fori_loop(0, capacity, one, 0)


def pack(queries, slot_row, pieces, capacity, marks, *before):
    shapes = [
        jax.ShapeDtypeStruct((blocks * capacity,) + queries.shape[1:], BF) for _, blocks in pieces
    ]
    whole = lambda array: pl.BlockSpec(array.shape, lambda i, *_: (0, 0, 0, 0))
    packed = pl.pallas_call(
        functools.partial(pack_kernel, pieces, capacity),
        out_shape=shapes,
        grid_spec=pltpu.PrefetchScalarGridSpec(
            num_scalar_prefetch=2,
            grid=(1,),
            in_specs=[whole(queries)] + [pl.BlockSpec(memory_space=pl.ANY)] * len(before),
            out_specs=[whole(shape) for shape in shapes],
        ),
        compiler_params=params(16),
        cost_estimate=SMALL,
        name="pack_queries",
    )(slot_row, marks, queries, *before)
    return [x.reshape(-1, x.shape[-1]) for x in packed]


def split_kernel(heads, steps, k_hbm, v_hbm, kt_ref, *refs):
    v_refs, (buffer, wide, sems) = refs[:heads], refs[heads:]
    step = pl.program_id(0)
    each = buffer.shape[2]
    count = each // heads

    def copy(source, which, part):
        rows = source.at[pl.ds(part * each, each), :]
        return pltpu.make_async_copy(rows, buffer.at[which, part], sems.at[which, part])

    @pl.when(step == 0)
    def _():
        for part in range(steps):
            copy(k_hbm, 0, part).start()
            copy(v_hbm, 1, part).start()

    for which, source in ((0, k_hbm), (1, v_hbm)):
        copy(source, which, step).wait()
        wide[...] = buffer[which, step].astype(F32)
        for a in range(heads):
            part = wide[pl.ds(a, count, stride=heads), :]
            if which == 0:
                kt_ref[a] = part.T.astype(BF)
            else:
                v_refs[a][...] = part.astype(BF)


def split_heads(keys, values):
    count, heads, dim = keys.shape
    steps = 4
    each = count // steps
    return pl.pallas_call(
        functools.partial(split_kernel, heads, steps),
        out_shape=[
            jax.ShapeDtypeStruct((heads, dim, count), BF),
        ]
        + [jax.ShapeDtypeStruct((count, dim), BF)] * heads,
        grid=(steps,),
        in_specs=[pl.BlockSpec(memory_space=pl.ANY)] * 2,
        out_specs=[
            pl.BlockSpec((heads, dim, each), lambda i: (0, 0, i)),
        ]
        + [pl.BlockSpec((each, dim), lambda i: (i, 0))] * heads,
        scratch_shapes=[
            pltpu.VMEM((2, steps, each * heads, dim), BF),
            pltpu.VMEM((each * heads, dim), F32),
            pltpu.SemaphoreType.DMA((2, steps)),
        ],
        compiler_params=params(48),
        cost_estimate=SMALL,
        name="split_heads",
    )(keys.reshape(count * heads, dim), values.reshape(count * heads, dim))


def attend_kernel(capacity, per, group, block, chunk, count, outs, at_ref, *refs):
    del at_ref
    q_refs, k_ref = refs[:count], refs[count]
    heads, dim, keys = k_ref.shape
    v_refs = refs[count + 1 : count + 1 + heads]
    o_refs, (acc_ref, weight_ref) = refs[-2 - outs : -2], refs[-2:]
    turn = pl.program_id(0)
    total = rows = capacity * per
    each = rows // heads
    scale = dim**-0.5 * math.log2(math.e)
    ones = jnp.ones((block, dim), BF)
    grid = q_refs[0][...].astype(F32)
    for t in range(1, count):
        grid = jnp.where(turn == t, q_refs[t][...].astype(F32), grid)
    grid = grid.reshape(total // (heads * group), heads, group, dim)
    queries = [grid[:, a].reshape(each, dim).astype(BF) for a in range(heads)]

    def scores(a, j):
        part = k_ref[a, :, pl.ds(j * block, block)]
        return jnp.dot(queries[a], part, preferred_element_type=F32)

    def values(a, j):
        return jnp.concatenate([v_refs[a][pl.ds(j * block, block), :], ones], axis=1)

    def natural(parts):
        split = [x.reshape(each // group, 1, group, dim) for x in parts]
        return jnp.concatenate(split, axis=1).reshape(total, dim)

    def finish(shifts):
        sums = [acc_ref[a, :, dim:] for a in range(heads)]
        out = natural([acc_ref[a, :, :dim] / sums[a] for a in range(heads)]).astype(BF)
        log_sum = natural([shifts[a] + jnp.log2(sums[a]) for a in range(heads)])
        high = log_sum.astype(BF).astype(F32)
        lane = lax.broadcasted_iota(jnp.int32, (total, dim), 1)
        row = lax.broadcasted_iota(jnp.int32, (total, dim), 0)
        term = jnp.where(lane < per, high, log_sum - high)
        term = jnp.where((lane % per == row % per) & (lane < 2 * per), term, 0.0).astype(BF)
        slot = lax.broadcasted_iota(jnp.int32, (EXTRA, rows), 0)
        source = lax.broadcasted_iota(jnp.int32, (EXTRA, rows), 1) // per
        pick = jnp.where(source == slot, 1.0, 0.0).astype(BF)
        logs = jnp.dot(pick, term, preferred_element_type=F32).astype(BF)
        for t, o_ref in enumerate(o_refs):

            @pl.when(turn == t)
            def _():
                o_ref[:rows, :] = out
                o_ref[rows:, :] = logs

    turns = keys // block
    steps = block // chunk

    def accumulate(a, j):
        slot = (j * heads + a) % 2
        part = jnp.dot(weight_ref[slot], values(a, j), preferred_element_type=F32)
        if j == 0:
            acc_ref[a] = part
        else:
            acc_ref[a] += part

    def chunk_scores(a, first):
        part = k_ref[a, :, first : first + chunk]
        return jnp.dot(queries[a], part, preferred_element_type=F32)

    opening = [chunk_scores(a, 0) for a in range(heads)]
    shifts = [jnp.max(x, axis=1, keepdims=True) * scale - 3.0 for x in opening]
    before = None
    for j in range(turns):
        for a in range(heads):
            slot = (j * heads + a) % 2
            for c in range(steps):
                first = j * block + c * chunk
                part = chunk_scores(a, first) if first else opening[a]
                weights = jnp.exp2((part * scale - shifts[a]).astype(BF))
                weight_ref[slot, :, c * chunk : (c + 1) * chunk] = weights
            if before is not None:
                accumulate(*before)
            before = (a, j)
    accumulate(*before)
    finish(shifts)
    fits = jnp.max(acc_ref[:, :, dim:]) < LIMIT

    @pl.when(jnp.logical_not(fits))
    def _():
        acc_ref[...] = jnp.zeros_like(acc_ref)
        tops = []
        for a in range(heads):

            def step(j, top):
                part = scores(a, j) * scale
                new = jnp.maximum(top, jnp.max(part, axis=1, keepdims=True))
                weights = jnp.exp2(part - new).astype(BF)
                acc_ref[a] = acc_ref[a] * jnp.exp2(top - new) + jnp.dot(
                    weights, values(a, j), preferred_element_type=F32
                )
                return new

            tops.append(lax.fori_loop(0, turns, step, jnp.full((each, 1), -1e30, F32)))
        finish(tops)


def attend(queries, keys_t, values, marks, near, capacity, per, group, *before):
    dim = queries[0].shape[1]
    heads, _, keys = keys_t.shape
    rows = capacity * per
    count = len(queries)
    blocks = queries[0].shape[0] // rows if near else count
    block = min(1024, keys)
    chunk = min(256, block)
    once = lambda array: pl.BlockSpec(
        array.shape, lambda i, s: (0,) * array.ndim, pipeline_mode=pl.Buffered(1)
    )
    place = (lambda i, s: (s[0] ^ i, 0)) if near else (lambda i, s: (0, 0))
    out = jax.ShapeDtypeStruct((rows + EXTRA, dim), BF)
    return pl.pallas_call(
        functools.partial(attend_kernel, capacity, per, group, block, chunk, count, blocks),
        out_shape=[out] * blocks,
        grid_spec=pltpu.PrefetchScalarGridSpec(
            num_scalar_prefetch=1,
            grid=(blocks,),
            in_specs=[pl.BlockSpec((rows, dim), place)] * count
            + [once(keys_t)]
            + [once(array) for array in values]
            + [pl.BlockSpec(memory_space=pl.ANY)] * len(before),
            out_specs=[pl.BlockSpec(out.shape, lambda i, s: (0, 0))] * blocks,
            scratch_shapes=[
                pltpu.VMEM((heads, rows // heads, 2 * dim), F32),
                pltpu.VMEM((2, rows // heads, block), BF),
            ],
        ),
        compiler_params=params(20),
        cost_estimate=SMALL,
        name="attend_prefix",
    )(marks, *queries, keys_t, *values, *before)


def visibility(lengths, draft_count, suffix_count):
    position = jnp.arange(suffix_count + draft_count, dtype=jnp.int32)
    draft_pos = jnp.arange(draft_count, dtype=jnp.int32)
    earlier = position[None, None, :] < lengths[:, None, None]
    earlier = earlier & (position[None, None, :] < suffix_count)
    fresh = (position[None, :] >= suffix_count) & (
        position[None, :] - suffix_count <= draft_pos[:, None]
    )
    return earlier | fresh[None, :, :]


def local_attention(query_grid, key_rows, value_rows, visible):
    scale = query_grid.shape[-1] ** (-0.5)
    scores = (
        jnp.einsum("rtagd,rjad->rtagj", query_grid, key_rows, preferred_element_type=F32) * scale
    )
    visible_mask = visible[:, :, None, None, :]
    scores = jnp.where(visible_mask, scores, F32(-1e30))
    top = jnp.max(scores, axis=-1)
    exponent = jnp.where(visible_mask, jnp.exp(scores - top[..., None]), F32(0.0))
    denominator = jnp.sum(exponent, axis=-1)
    summed = jnp.einsum(
        "rtagj,rjad->rtagd", exponent.astype(BF), value_rows, preferred_element_type=F32
    )
    return summed / denominator[..., None], (top + jnp.log(denominator)) * F32(math.log2(math.e))


def fetch(weight, marks, first, buffer, sems, width):
    count, _, block = buffer.shape
    each = width // block
    copies = []
    for n in range(count):
        column = pl.multiple_of(marks[first + n // each] * width + (n % each) * block, block)
        source = weight.at[:, pl.ds(column, block)]
        copies.append(pltpu.make_async_copy(source, buffer.at[n], sems.at[n]))
        copies[-1].start()
    return copies


def multiply(att, copies, buffer, outs):
    block = buffer.shape[2]
    each = len(copies) // len(outs)
    rows = att[...]
    for n, copy in enumerate(copies):
        copy.wait()
        product = jnp.dot(rows, buffer[n], preferred_element_type=F32).astype(BF)
        outs[n // each][:, n % each * block : (n % each + 1) * block] = product


def join_kernel(capacity, count, base, shares, order, target, marks, *refs):
    received, (local, local_log, weight) = refs[:count], refs[count : count + 3]
    att, *outs = refs[-8 - shares - 1 : -8]
    blocks, block_logs, part, mine, logs, spread, buffer, sems = refs[-8:]
    copies = fetch(weight, marks, 1, buffer, sems, outs[0].shape[1])
    rows, per, dim = part.shape
    held = capacity * per
    heads = att.shape[1] // dim
    draft = per // heads
    done = 0
    for array in received:
        for first in range(0, array.shape[0], held + EXTRA):
            values = array[first : first + held, :].astype(F32)
            blocks[done * capacity : (done + 1) * capacity] = values.reshape(capacity, per, dim)
            last = array[first + held : first + held + EXTRA, :].astype(F32)
            block_logs[done * EXTRA : (done + 1) * EXTRA] = last
            done += 1

    def gather(i, _):
        at = order[base + i]
        slot = target[base + i]
        part[i] = blocks[slot]
        mine[i] = local[at].astype(F32)
        place = (slot // capacity) * EXTRA + slot % capacity
        logs[0, pl.ds(i, 1), :] = block_logs[pl.ds(place, 1), :]
        logs[1, pl.ds(i, 1), :] = local_log[pl.ds(at, 1), :]
        return 0

    lax.fori_loop(0, rows, gather, 0)
    lane = lax.broadcasted_iota(jnp.int32, (rows, dim), 1)
    first = logs[0] + pltpu.roll(logs[0], dim - per, axis=1)
    share = 1.0 / (1.0 + jnp.exp2(logs[1] - first))
    high = share.astype(BF).astype(F32)
    low = pltpu.roll(share - high, per, axis=1)
    logs[0] = jnp.where(lane < per, high, jnp.where(lane < 2 * per, low, 0.0))
    diagonal = lax.broadcasted_iota(jnp.int32, (per, dim), 1) % per
    diagonal = diagonal == lax.broadcasted_iota(jnp.int32, (per, dim), 0)

    def widen(i, _):
        row = logs[0, pl.ds(i, 1), :]
        spread[i] = jnp.where(diagonal, row, 0.0).astype(BF)
        return 0

    lax.fori_loop(0, rows, widen, 0)
    ones = jnp.ones((dim, dim), BF)
    shares = jnp.dot(
        spread[...].reshape(rows * per, dim), ones, preferred_element_type=F32
    ).reshape(rows, per, dim)
    part[...] = mine[...] + shares * (part[...] - mine[...])
    flat = part.reshape(rows * per, dim)
    for h in range(heads):
        head = flat[pl.ds(h, rows * draft, stride=heads), :]
        att[:, h * dim : (h + 1) * dim] = head.astype(BF)


    multiply(att, copies, buffer, outs)


def join(
    received, local, local_log, order, target, heads, base, rows, capacity, weight, marks, shares, width, *before
):
    count = len(received)
    per, dim = local.shape[1:]
    blocks = sum(array.shape[0] for array in received) // (capacity * per + EXTRA)
    lines = rows * per // heads
    block = min(256, width)
    whole = lambda array: pl.BlockSpec(array.shape, lambda n, *_: (0,) * array.ndim)
    att = jax.ShapeDtypeStruct((lines, heads * dim), BF)
    out = jax.ShapeDtypeStruct((lines, width), BF)
    return pl.pallas_call(
        functools.partial(join_kernel, capacity, count, base, shares),
        out_shape=[att] + [out] * shares,
        grid_spec=pltpu.PrefetchScalarGridSpec(
            num_scalar_prefetch=3,
            grid=(1,),
            in_specs=[whole(array) for array in received]
            + [whole(local), whole(local_log)]
            + [pl.BlockSpec(memory_space=pl.ANY)] * (1 + len(before)),
            out_specs=[whole(att)] + [whole(out)] * shares,
            scratch_shapes=[
                pltpu.VMEM((blocks * capacity, per, dim), F32),
                pltpu.VMEM((blocks * EXTRA, dim), F32),
                pltpu.VMEM((rows, per, dim), F32),
                pltpu.VMEM((rows, per, dim), F32),
                pltpu.VMEM((2, rows, dim), F32),
                pltpu.VMEM((rows, per, dim), BF),
                pltpu.VMEM((shares * width // block, heads * dim, block), BF),
                pltpu.SemaphoreType.DMA((shares * width // block,)),
            ],
        ),
        compiler_params=params(34),
        cost_estimate=SMALL,
        name="join_project",
    )(order, target, marks, *received, local, local_log, weight, *before)


def project_kernel(shares, first, marks, att, weight, *refs):
    outs, (buffer, sems) = refs[-2 - shares : -2], refs[-2:]
    multiply(att, fetch(weight, marks, first, buffer, sems, outs[0].shape[1]), buffer, outs)


def project(att, weight, marks, first, shares, width, *before):
    rows, depth = att.shape
    block = min(256, width)
    out = jax.ShapeDtypeStruct((rows, width), BF)
    whole = lambda array: pl.BlockSpec(array.shape, lambda n, *_: (0,) * array.ndim)
    return pl.pallas_call(
        functools.partial(project_kernel, shares, first),
        out_shape=[out] * shares,
        grid_spec=pltpu.PrefetchScalarGridSpec(
            num_scalar_prefetch=1,
            grid=(1,),
            in_specs=[whole(att)] + [pl.BlockSpec(memory_space=pl.ANY)] * (1 + len(before)),
            out_specs=[whole(out)] * shares,
            scratch_shapes=[
                pltpu.VMEM((shares * width // block, depth, block), BF),
                pltpu.SemaphoreType.DMA((shares * width // block,)),
            ],
        ),
        compiler_params=params(20),
        cost_estimate=SMALL,
        name="project",
    )(marks, att, weight, *before)


def project_sum(join_with, weight, marks, split, before):
    size = lax.axis_size("tensor")
    chips = size // 2
    width = weight.shape[1] // size
    order = list(range(1, chips)) + [0]
    att, *products = join_with(1 if split else size, width)
    got, sums = [], []
    for k, d in enumerate(order):
        while len(products) < 2 * k + 2:
            waits = sums + (before if d == 0 else [])
            shares = 1 if d else size - len(products)
            products += project(att, weight, marks, 1 + len(products), shares, width, *waits)
        send, keep = products[2 * k : 2 * k + 2]
        there = lax.ppermute(send, "tensor", [(i, i ^ 1) for i in range(size)])
        if d:
            total = (keep.astype(F32) + there.astype(F32)).astype(BF)
            sums.append(total)
            got.append(lax.ppermute(total, "tensor", [(i, i ^ (2 * d)) for i in range(size)]))
    total = keep.astype(F32)
    for term in got:
        total = total + term.astype(F32)
    return [total, there], [total], keep


def arrange_kernel(counts, place_ref, *refs):
    out_ref = refs[-1]
    rows, draft, _ = out_ref.shape
    halves, start = [], 0
    for count in counts:
        total = refs[start][...]
        for term in refs[start + 1 : start + count]:
            total = total + term[...].astype(F32)
        halves.append(total.astype(BF))
        start += count
    values = jnp.concatenate(halves, axis=0)
    size = rows * draft
    pick = lax.broadcasted_iota(jnp.int32, (size, size), 1) == place_ref[...]
    result = jnp.dot(
        jnp.where(pick, 1.0, 0.0).astype(BF), values, preferred_element_type=F32
    )
    for r in range(rows):
        out_ref[r] = result[r * draft : (r + 1) * draft].astype(BF)


def arrange(halves, place, rows, draft):
    width = halves[0][0].shape[1]
    index = (place[:, None] * draft + jnp.arange(draft, dtype=jnp.int32)[None, :]).reshape(-1, 1)
    return pl.pallas_call(
        functools.partial(arrange_kernel, [len(half) for half in halves]),
        out_shape=jax.ShapeDtypeStruct((rows, draft, width), BF),
        compiler_params=params(20),
        cost_estimate=SMALL,
        name="arrange_rows",
    )(index, *[term for half in halves for term in half])


def exchange(x):
    size = lax.axis_size("dp")
    groups = [list(range(size // 2)), list(range(size // 2, size))]
    return lax.all_to_all(
        x, "dp", split_axis=0, concat_axis=0, axis_index_groups=groups, tiled=True
    )


def hop(x, shift):
    size = lax.axis_size("dp")
    return lax.ppermute(x, "dp", [(i, i ^ shift) for i in range(size)])


def body(
    queries,
    draft_keys,
    draft_values,
    suffix_keys,
    suffix_values,
    suffix_len,
    prefix_keys,
    prefix_values,
    row_prefix,
    prefix_slot,
    out_weight,
):
    row_count, draft, query_heads, dim = queries.shape
    heads = draft_keys.shape[2]
    group = query_heads // heads
    per = draft * query_heads
    suffix_count = suffix_keys.shape[1]
    peers = lax.axis_size("dp")
    capacity = 2 * row_count // peers
    own = lax.axis_index("tensor").astype(jnp.int32)
    me = lax.axis_index("dp").astype(jnp.int32)

    size = lax.axis_size("tensor")
    half = peers // 2
    shards = [own ^ (2 * d + other) for d in list(range(1, size // 2)) + [0] for other in (1, 0)]
    marks = jnp.stack([me % half] + shards)

    slot_row, place, order, target = route(row_prefix, prefix_slot, me, peers, capacity)
    lead = half // 2
    first = pack(queries, slot_row, [(half + d, 1) for d in range(lead)], capacity, marks)
    near, *late = pack(
        queries,
        slot_row,
        [(0, half)] + [(half + d, 1) for d in range(lead, half)],
        capacity,
        marks,
        first[0],
    )
    far = [hop(x, half + d) for d, x in enumerate(first + late)]
    near = exchange(near)

    keys_t, *values = split_heads(prefix_keys[0], prefix_values[0])
    back, before = [None] * peers, []
    for batch in [range(half, half + lead), range(half)] + [[d] for d in range(half + lead, peers)]:
        arrays = [near] if batch[0] == 0 else [far[d - half] for d in batch]
        if batch[-1] == peers - 1:
            before = list(before) + back[half : half + lead]
        results = attend(arrays, keys_t, values, marks, batch[0] == 0, capacity, per, group, *before)
        before = results[:1]
        for d, result in zip(batch, results):
            back[d] = hop(result, d) if d else result

    query_grid = queries.reshape(row_count, draft, heads, group, dim)
    all_keys = jnp.concatenate([suffix_keys, draft_keys], axis=1)
    all_values = jnp.concatenate([suffix_values, draft_values], axis=1)
    visible = visibility(suffix_len, draft, suffix_count)
    local, local_log = local_attention(query_grid, all_keys, all_values, visible)
    local = local.reshape(row_count, per, dim).astype(BF)
    local_log = jnp.pad(local_log.reshape(row_count, per), ((0, 0), (0, dim - per)))

    rows = row_count // 2
    early = peers - rows // capacity
    outs, waits = [], []
    for base in (0, rows):
        received = back if base else back[:early]

        def join_with(shares, width):
            return join(
                received,
                local,
                local_log,
                order,
                target,
                query_heads,
                base,
                rows,
                capacity,
                out_weight,
                marks,
                shares,
                width,
                *before,
            )

        terms, waits, product = project_sum(join_with, out_weight, marks, base > 0, waits)
        before = [product]
        outs.append(terms)
    return arrange(outs, place, row_count, draft)


def solution(mesh):
    placed = (
        P("dp", None, "tensor", None),
        P("dp", None, "tensor", None),
        P("dp", None, "tensor", None),
        P("dp", None, "tensor", None),
        P("dp", None, "tensor", None),
        P("dp"),
        P("dp", None, "tensor", None),
        P("dp", None, "tensor", None),
        P("dp", None),
        P(),
        P("tensor", None),
    )
    return jax.shard_map(
        body, mesh=mesh, in_specs=placed, out_specs=P("dp", None, "tensor"), check_vma=False
    )
```

```python
import functools
import math

import jax
import jax.numpy as jnp
from jax import lax
from jax.experimental import pallas as pl
from jax.experimental.pallas import tpu as pltpu
from jax.sharding import PartitionSpec as P

BF = jnp.bfloat16
F32 = jnp.float32
EXTRA = 16
LIMIT = 1e30
SMALL = pl.CostEstimate(flops=1 << 20, bytes_accessed=1 << 10, transcendentals=0)


def params(mebibytes):
    return pltpu.CompilerParams(vmem_limit_bytes=mebibytes * 1024 * 1024)


def route(row_prefix, prefix_slot, me, peers, capacity):
    rows = row_prefix.shape[0]
    prefixes = prefix_slot.shape[0]
    name = row_prefix[:, 0]
    row = jnp.arange(rows, dtype=jnp.int32)
    owner = jnp.sum(
        jnp.where(
            row_prefix == jnp.arange(prefixes, dtype=jnp.int32)[None, :], prefix_slot[None, :], 0
        ),
        axis=1,
    )
    same = (name[:, None] == name[None, :]) & (row[None, :] < row[:, None])
    rank = jnp.sum(same.astype(jnp.int32), axis=1)
    half = peers // 2
    shift = owner ^ me
    sent = jnp.where(shift < half, owner % half, shift) * capacity + rank
    target = shift * capacity + rank
    slots = jnp.arange(peers * capacity, dtype=jnp.int32)
    slot_row = jnp.sum(jnp.where(sent[None, :] == slots[:, None], row[None, :], 0), axis=1)
    place = jnp.sum((target[None, :] < target[:, None]).astype(jnp.int32), axis=1)
    at = place[None, :] == row[:, None]
    order = jnp.sum(jnp.where(at, row[None, :], 0), axis=1)
    order_target = jnp.sum(jnp.where(at, target[None, :], 0), axis=1)
    return slot_row, place, order, order_target


def pack_kernel(pieces, capacity, slot_row, marks, q_ref, *refs):
    del marks
    outs = refs[-len(pieces) :]

    def one(k, _):
        for (first, blocks), out in zip(pieces, outs):
            for b in range(blocks):
                out[b * capacity + k] = q_ref[slot_row[(first + b) * capacity + k]]
        return 0

    lax.fori_loop(0, capacity, one, 0)


def pack(queries, slot_row, pieces, capacity, marks, *before):
    shapes = [
        jax.ShapeDtypeStruct((blocks * capacity,) + queries.shape[1:], BF) for _, blocks in pieces
    ]
    whole = lambda array: pl.BlockSpec(array.shape, lambda i, *_: (0, 0, 0, 0))
    packed = pl.pallas_call(
        functools.partial(pack_kernel, pieces, capacity),
        out_shape=shapes,
        grid_spec=pltpu.PrefetchScalarGridSpec(
            num_scalar_prefetch=2,
            grid=(1,),
            in_specs=[whole(queries)] + [pl.BlockSpec(memory_space=pl.ANY)] * len(before),
            out_specs=[whole(shape) for shape in shapes],
        ),
        compiler_params=params(16),
        cost_estimate=SMALL,
        name="pack_queries",
    )(slot_row, marks, queries, *before)
    return [x.reshape(-1, x.shape[-1]) for x in packed]


def split_kernel(heads, steps, k_hbm, v_hbm, kt_ref, *refs):
    v_refs, (buffer, wide, sems) = refs[:heads], refs[heads:]
    step = pl.program_id(0)
    each = buffer.shape[2]
    count = each // heads

    def copy(source, which, part):
        rows = source.at[pl.ds(part * each, each), :]
        return pltpu.make_async_copy(rows, buffer.at[which, part], sems.at[which, part])

    @pl.when(step == 0)
    def _():
        for part in range(steps):
            copy(k_hbm, 0, part).start()
            copy(v_hbm, 1, part).start()

    for which, source in ((0, k_hbm), (1, v_hbm)):
        copy(source, which, step).wait()
        wide[...] = buffer[which, step].astype(F32)
        for a in range(heads):
            part = wide[pl.ds(a, count, stride=heads), :]
            if which == 0:
                kt_ref[a] = part.T.astype(BF)
            else:
                v_refs[a][...] = part.astype(BF)


def split_heads(keys, values):
    count, heads, dim = keys.shape
    steps = 4
    each = count // steps
    return pl.pallas_call(
        functools.partial(split_kernel, heads, steps),
        out_shape=[
            jax.ShapeDtypeStruct((heads, dim, count), BF),
        ]
        + [jax.ShapeDtypeStruct((count, dim), BF)] * heads,
        grid=(steps,),
        in_specs=[pl.BlockSpec(memory_space=pl.ANY)] * 2,
        out_specs=[
            pl.BlockSpec((heads, dim, each), lambda i: (0, 0, i)),
        ]
        + [pl.BlockSpec((each, dim), lambda i: (i, 0))] * heads,
        scratch_shapes=[
            pltpu.VMEM((2, steps, each * heads, dim), BF),
            pltpu.VMEM((each * heads, dim), F32),
            pltpu.SemaphoreType.DMA((2, steps)),
        ],
        compiler_params=params(48),
        cost_estimate=SMALL,
        name="split_heads",
    )(keys.reshape(count * heads, dim), values.reshape(count * heads, dim))


def attend_kernel(capacity, per, group, block, chunk, count, outs, at_ref, *refs):
    del at_ref
    q_refs, k_ref = refs[:count], refs[count]
    heads, dim, keys = k_ref.shape
    v_refs = refs[count + 1 : count + 1 + heads]
    o_refs, (acc_ref, weight_ref) = refs[-2 - outs : -2], refs[-2:]
    turn = pl.program_id(0)
    total = rows = capacity * per
    each = rows // heads
    scale = dim**-0.5 * math.log2(math.e)
    ones = jnp.ones((block, dim), BF)
    grid = q_refs[0][...].astype(F32)
    for t in range(1, count):
        grid = jnp.where(turn == t, q_refs[t][...].astype(F32), grid)
    grid = grid.reshape(total // (heads * group), heads, group, dim)
    queries = [grid[:, a].reshape(each, dim).astype(BF) for a in range(heads)]

    def scores(a, j):
        part = k_ref[a, :, pl.ds(j * block, block)]
        return jnp.dot(queries[a], part, preferred_element_type=F32)

    def values(a, j):
        return jnp.concatenate([v_refs[a][pl.ds(j * block, block), :], ones], axis=1)

    def natural(parts):
        split = [x.reshape(each // group, 1, group, dim) for x in parts]
        return jnp.concatenate(split, axis=1).reshape(total, dim)

    def finish(shifts):
        sums = [acc_ref[a, :, dim:] for a in range(heads)]
        out = natural([acc_ref[a, :, :dim] / sums[a] for a in range(heads)]).astype(BF)
        log_sum = natural([shifts[a] + jnp.log2(sums[a]) for a in range(heads)])
        high = log_sum.astype(BF).astype(F32)
        lane = lax.broadcasted_iota(jnp.int32, (total, dim), 1)
        row = lax.broadcasted_iota(jnp.int32, (total, dim), 0)
        term = jnp.where(lane < per, high, log_sum - high)
        term = jnp.where((lane % per == row % per) & (lane < 2 * per), term, 0.0).astype(BF)
        slot = lax.broadcasted_iota(jnp.int32, (EXTRA, rows), 0)
        source = lax.broadcasted_iota(jnp.int32, (EXTRA, rows), 1) // per
        pick = jnp.where(source == slot, 1.0, 0.0).astype(BF)
        logs = jnp.dot(pick, term, preferred_element_type=F32).astype(BF)
        for t, o_ref in enumerate(o_refs):

            @pl.when(turn == t)
            def _():
                o_ref[:rows, :] = out
                o_ref[rows:, :] = logs

    turns = keys // block
    steps = block // chunk

    def middle(part):
        weights = jnp.exp2(part - jnp.max(part, axis=1, keepdims=True))
        total = jnp.sum(weights, axis=1, keepdims=True)
        return jnp.sum(weights * part, axis=1, keepdims=True) / total

    def accumulate(a, j):
        slot = (a * turns + j) % 2
        part = jnp.dot(weight_ref[slot], values(a, j), preferred_element_type=F32)
        if j == 0:
            acc_ref[a] = part
        else:
            acc_ref[a] += part

    shifts = []
    before = None
    for a in range(heads):
        for j in range(turns):
            slot = (a * turns + j) % 2
            for c in range(steps):
                first = j * block + c * chunk
                part = jnp.dot(
                    queries[a], k_ref[a, :, first : first + chunk], preferred_element_type=F32
                )
                if first == 0:
                    shifts.append(middle(part * scale))
                weights = jnp.exp2((part * scale - shifts[a]).astype(BF))
                weight_ref[slot, :, c * chunk : (c + 1) * chunk] = weights
            if before is not None:
                accumulate(*before)
            before = (a, j)
    accumulate(*before)
    finish(shifts)
    fits = jnp.max(acc_ref[:, :, dim:]) < LIMIT

    @pl.when(jnp.logical_not(fits))
    def _():
        acc_ref[...] = jnp.zeros_like(acc_ref)
        tops = []
        for a in range(heads):

            def step(j, top):
                part = scores(a, j) * scale
                new = jnp.maximum(top, jnp.max(part, axis=1, keepdims=True))
                weights = jnp.exp2(part - new).astype(BF)
                acc_ref[a] = acc_ref[a] * jnp.exp2(top - new) + jnp.dot(
                    weights, values(a, j), preferred_element_type=F32
                )
                return new

            tops.append(lax.fori_loop(0, turns, step, jnp.full((each, 1), -1e30, F32)))
        finish(tops)


def attend(queries, keys_t, values, marks, near, capacity, per, group, *before):
    dim = queries[0].shape[1]
    heads, _, keys = keys_t.shape
    rows = capacity * per
    count = len(queries)
    blocks = queries[0].shape[0] // rows if near else count
    block = min(1024, keys)
    chunk = min(256, block)
    once = lambda array: pl.BlockSpec(
        array.shape, lambda i, s: (0,) * array.ndim, pipeline_mode=pl.Buffered(1)
    )
    place = (lambda i, s: (s[0] ^ i, 0)) if near else (lambda i, s: (0, 0))
    out = jax.ShapeDtypeStruct((rows + EXTRA, dim), BF)
    return pl.pallas_call(
        functools.partial(attend_kernel, capacity, per, group, block, chunk, count, blocks),
        out_shape=[out] * blocks,
        grid_spec=pltpu.PrefetchScalarGridSpec(
            num_scalar_prefetch=1,
            grid=(blocks,),
            in_specs=[pl.BlockSpec((rows, dim), place)] * count
            + [once(keys_t)]
            + [once(array) for array in values]
            + [pl.BlockSpec(memory_space=pl.ANY)] * len(before),
            out_specs=[pl.BlockSpec(out.shape, lambda i, s: (0, 0))] * blocks,
            scratch_shapes=[
                pltpu.VMEM((heads, rows // heads, 2 * dim), F32),
                pltpu.VMEM((2, rows // heads, block), BF),
            ],
        ),
        compiler_params=params(24),
        cost_estimate=SMALL,
        name="attend_prefix",
    )(marks, *queries, keys_t, *values, *before)


def visibility(lengths, draft_count, suffix_count):
    position = jnp.arange(suffix_count + draft_count, dtype=jnp.int32)
    draft_pos = jnp.arange(draft_count, dtype=jnp.int32)
    earlier = position[None, None, :] < lengths[:, None, None]
    earlier = earlier & (position[None, None, :] < suffix_count)
    fresh = (position[None, :] >= suffix_count) & (
        position[None, :] - suffix_count <= draft_pos[:, None]
    )
    return earlier | fresh[None, :, :]


def local_attention(query_grid, key_rows, value_rows, visible):
    scale = query_grid.shape[-1] ** (-0.5)
    scores = (
        jnp.einsum("rtagd,rjad->rtagj", query_grid, key_rows, preferred_element_type=F32) * scale
    )
    visible_mask = visible[:, :, None, None, :]
    scores = jnp.where(visible_mask, scores, F32(-1e30))
    top = jnp.max(scores, axis=-1)
    exponent = jnp.where(visible_mask, jnp.exp(scores - top[..., None]), F32(0.0))
    denominator = jnp.sum(exponent, axis=-1)
    summed = jnp.einsum(
        "rtagj,rjad->rtagd", exponent.astype(BF), value_rows, preferred_element_type=F32
    )
    return summed / denominator[..., None], (top + jnp.log(denominator)) * F32(math.log2(math.e))


def fetch(weight, marks, first, buffer, sems, width):
    count, _, block = buffer.shape
    each = width // block
    copies = []
    for n in range(count):
        column = pl.multiple_of(marks[first + n // each] * width + (n % each) * block, block)
        source = weight.at[:, pl.ds(column, block)]
        copies.append(pltpu.make_async_copy(source, buffer.at[n], sems.at[n]))
        copies[-1].start()
    return copies


def multiply(att, copies, buffer, outs):
    block = buffer.shape[2]
    each = len(copies) // len(outs)
    rows = att[...]
    for n, copy in enumerate(copies):
        copy.wait()
        product = jnp.dot(rows, buffer[n], preferred_element_type=F32).astype(BF)
        outs[n // each][:, n % each * block : (n % each + 1) * block] = product


def join_kernel(capacity, count, base, shares, order, target, marks, *refs):
    received, (local, local_log, weight) = refs[:count], refs[count : count + 3]
    att, *outs = refs[-8 - shares - 1 : -8]
    blocks, block_logs, part, mine, logs, spread, buffer, sems = refs[-8:]
    copies = fetch(weight, marks, 1, buffer, sems, outs[0].shape[1])
    rows, per, dim = part.shape
    held = capacity * per
    heads = att.shape[1] // dim
    draft = per // heads
    done = 0
    for array in received:
        for first in range(0, array.shape[0], held + EXTRA):
            values = array[first : first + held, :].astype(F32)
            blocks[done * capacity : (done + 1) * capacity] = values.reshape(capacity, per, dim)
            last = array[first + held : first + held + EXTRA, :].astype(F32)
            block_logs[done * EXTRA : (done + 1) * EXTRA] = last
            done += 1

    def gather(i, _):
        at = order[base + i]
        slot = target[base + i]
        part[i] = blocks[slot]
        mine[i] = local[at].astype(F32)
        place = (slot // capacity) * EXTRA + slot % capacity
        logs[0, pl.ds(i, 1), :] = block_logs[pl.ds(place, 1), :]
        logs[1, pl.ds(i, 1), :] = local_log[pl.ds(at, 1), :]
        return 0

    lax.fori_loop(0, rows, gather, 0)
    lane = lax.broadcasted_iota(jnp.int32, (rows, dim), 1)
    first = logs[0] + pltpu.roll(logs[0], dim - per, axis=1)
    share = 1.0 / (1.0 + jnp.exp2(logs[1] - first))
    high = share.astype(BF).astype(F32)
    low = pltpu.roll(share - high, per, axis=1)
    logs[0] = jnp.where(lane < per, high, jnp.where(lane < 2 * per, low, 0.0))
    diagonal = lax.broadcasted_iota(jnp.int32, (per, dim), 1) % per
    diagonal = diagonal == lax.broadcasted_iota(jnp.int32, (per, dim), 0)

    def widen(i, _):
        row = logs[0, pl.ds(i, 1), :]
        spread[i] = jnp.where(diagonal, row, 0.0).astype(BF)
        return 0

    lax.fori_loop(0, rows, widen, 0)
    ones = jnp.ones((dim, dim), BF)
    shares = jnp.dot(
        spread[...].reshape(rows * per, dim), ones, preferred_element_type=F32
    ).reshape(rows, per, dim)
    part[...] = mine[...] + shares * (part[...] - mine[...])
    flat = part.reshape(rows * per, dim)
    for h in range(heads):
        head = flat[pl.ds(h, rows * draft, stride=heads), :]
        att[:, h * dim : (h + 1) * dim] = head.astype(BF)


    multiply(att, copies, buffer, outs)


def join(
    received, local, local_log, order, target, heads, base, rows, capacity, weight, marks, shares, width, *before
):
    count = len(received)
    per, dim = local.shape[1:]
    blocks = sum(array.shape[0] for array in received) // (capacity * per + EXTRA)
    lines = rows * per // heads
    block = min(256, width)
    whole = lambda array: pl.BlockSpec(array.shape, lambda n, *_: (0,) * array.ndim)
    att = jax.ShapeDtypeStruct((lines, heads * dim), BF)
    out = jax.ShapeDtypeStruct((lines, width), BF)
    return pl.pallas_call(
        functools.partial(join_kernel, capacity, count, base, shares),
        out_shape=[att] + [out] * shares,
        grid_spec=pltpu.PrefetchScalarGridSpec(
            num_scalar_prefetch=3,
            grid=(1,),
            in_specs=[whole(array) for array in received]
            + [whole(local), whole(local_log)]
            + [pl.BlockSpec(memory_space=pl.ANY)] * (1 + len(before)),
            out_specs=[whole(att)] + [whole(out)] * shares,
            scratch_shapes=[
                pltpu.VMEM((blocks * capacity, per, dim), F32),
                pltpu.VMEM((blocks * EXTRA, dim), F32),
                pltpu.VMEM((rows, per, dim), F32),
                pltpu.VMEM((rows, per, dim), F32),
                pltpu.VMEM((2, rows, dim), F32),
                pltpu.VMEM((rows, per, dim), BF),
                pltpu.VMEM((shares * width // block, heads * dim, block), BF),
                pltpu.SemaphoreType.DMA((shares * width // block,)),
            ],
        ),
        compiler_params=params(34),
        cost_estimate=SMALL,
        name="join_project",
    )(order, target, marks, *received, local, local_log, weight, *before)


def project_kernel(shares, first, marks, att, weight, *refs):
    outs, (buffer, sems) = refs[-2 - shares : -2], refs[-2:]
    multiply(att, fetch(weight, marks, first, buffer, sems, outs[0].shape[1]), buffer, outs)


def project(att, weight, marks, first, shares, width, *before):
    rows, depth = att.shape
    block = min(256, width)
    out = jax.ShapeDtypeStruct((rows, width), BF)
    whole = lambda array: pl.BlockSpec(array.shape, lambda n, *_: (0,) * array.ndim)
    return pl.pallas_call(
        functools.partial(project_kernel, shares, first),
        out_shape=[out] * shares,
        grid_spec=pltpu.PrefetchScalarGridSpec(
            num_scalar_prefetch=1,
            grid=(1,),
            in_specs=[whole(att)] + [pl.BlockSpec(memory_space=pl.ANY)] * (1 + len(before)),
            out_specs=[whole(out)] * shares,
            scratch_shapes=[
                pltpu.VMEM((shares * width // block, depth, block), BF),
                pltpu.SemaphoreType.DMA((shares * width // block,)),
            ],
        ),
        compiler_params=params(20),
        cost_estimate=SMALL,
        name="project",
    )(marks, att, weight, *before)


def project_sum(join_with, weight, marks, split, before):
    size = lax.axis_size("tensor")
    chips = size // 2
    width = weight.shape[1] // size
    order = list(range(1, chips)) + [0]
    att, *products = join_with(1 if split else size, width)
    got, sums = [], []
    for k, d in enumerate(order):
        while len(products) < 2 * k + 2:
            waits = sums + (before if d == 0 else [])
            shares = 1 if d else size - len(products)
            products += project(att, weight, marks, 1 + len(products), shares, width, *waits)
        send, keep = products[2 * k : 2 * k + 2]
        there = lax.ppermute(send, "tensor", [(i, i ^ 1) for i in range(size)])
        if d:
            total = (keep.astype(F32) + there.astype(F32)).astype(BF)
            sums.append(total)
            got.append(lax.ppermute(total, "tensor", [(i, i ^ (2 * d)) for i in range(size)]))
    total = keep.astype(F32)
    for term in got:
        total = total + term.astype(F32)
    return [total, there], [total], keep


def arrange_kernel(counts, place_ref, *refs):
    out_ref = refs[-1]
    rows, draft, _ = out_ref.shape
    halves, start = [], 0
    for count in counts:
        total = refs[start][...]
        for term in refs[start + 1 : start + count]:
            total = total + term[...].astype(F32)
        halves.append(total.astype(BF))
        start += count
    values = jnp.concatenate(halves, axis=0)
    size = rows * draft
    pick = lax.broadcasted_iota(jnp.int32, (size, size), 1) == place_ref[...]
    result = jnp.dot(
        jnp.where(pick, 1.0, 0.0).astype(BF), values, preferred_element_type=F32
    )
    for r in range(rows):
        out_ref[r] = result[r * draft : (r + 1) * draft].astype(BF)


def arrange(halves, place, rows, draft):
    width = halves[0][0].shape[1]
    index = (place[:, None] * draft + jnp.arange(draft, dtype=jnp.int32)[None, :]).reshape(-1, 1)
    return pl.pallas_call(
        functools.partial(arrange_kernel, [len(half) for half in halves]),
        out_shape=jax.ShapeDtypeStruct((rows, draft, width), BF),
        compiler_params=params(20),
        cost_estimate=SMALL,
        name="arrange_rows",
    )(index, *[term for half in halves for term in half])


def exchange(x):
    size = lax.axis_size("dp")
    groups = [list(range(size // 2)), list(range(size // 2, size))]
    return lax.all_to_all(
        x, "dp", split_axis=0, concat_axis=0, axis_index_groups=groups, tiled=True
    )


def hop(x, shift):
    size = lax.axis_size("dp")
    return lax.ppermute(x, "dp", [(i, i ^ shift) for i in range(size)])


def body(
    queries,
    draft_keys,
    draft_values,
    suffix_keys,
    suffix_values,
    suffix_len,
    prefix_keys,
    prefix_values,
    row_prefix,
    prefix_slot,
    out_weight,
):
    row_count, draft, query_heads, dim = queries.shape
    heads = draft_keys.shape[2]
    group = query_heads // heads
    per = draft * query_heads
    suffix_count = suffix_keys.shape[1]
    peers = lax.axis_size("dp")
    capacity = 2 * row_count // peers
    own = lax.axis_index("tensor").astype(jnp.int32)
    me = lax.axis_index("dp").astype(jnp.int32)

    size = lax.axis_size("tensor")
    half = peers // 2
    shards = [own ^ (2 * d + other) for d in list(range(1, size // 2)) + [0] for other in (1, 0)]
    marks = jnp.stack([me % half] + shards)

    slot_row, place, order, target = route(row_prefix, prefix_slot, me, peers, capacity)
    lead = half // 2
    first = pack(queries, slot_row, [(half + d, 1) for d in range(lead)], capacity, marks)
    (near,) = pack(queries, slot_row, [(0, half)], capacity, marks, first[0])
    far = [hop(x, half + d) for d, x in enumerate(first)]
    near = exchange(near)
    keys_t, *values = split_heads(prefix_keys[0], prefix_values[0])
    rest = [(half + d, 1) for d in range(lead, half)]
    far += [
        hop(x, half + lead + d)
        for d, x in enumerate(pack(queries, slot_row, rest, capacity, marks, far[0], values[-1]))
    ]

    back, before = [None] * peers, []
    for batch in [range(half, half + lead), range(half)] + [[d] for d in range(half + lead, peers)]:
        arrays = [near] if batch[0] == 0 else [far[d - half] for d in batch]
        if batch[-1] == peers - 1:
            before = list(before) + back[half : half + lead]
        results = attend(arrays, keys_t, values, marks, batch[0] == 0, capacity, per, group, *before)
        before = results[:1]
        for d, result in zip(batch, results):
            back[d] = hop(result, d) if d else result

    query_grid = queries.reshape(row_count, draft, heads, group, dim)
    all_keys = jnp.concatenate([suffix_keys, draft_keys], axis=1)
    all_values = jnp.concatenate([suffix_values, draft_values], axis=1)
    visible = visibility(suffix_len, draft, suffix_count)
    local, local_log = local_attention(query_grid, all_keys, all_values, visible)
    local = local.reshape(row_count, per, dim).astype(BF)
    local_log = jnp.pad(local_log.reshape(row_count, per), ((0, 0), (0, dim - per)))

    rows = row_count // 2
    early = peers - rows // capacity
    outs, waits = [], []
    for base in (0, rows):
        received = back if base else back[:early]

        def join_with(shares, width):
            return join(
                received,
                local,
                local_log,
                order,
                target,
                query_heads,
                base,
                rows,
                capacity,
                out_weight,
                marks,
                shares,
                width,
                *before,
            )

        terms, waits, product = project_sum(join_with, out_weight, marks, base > 0, waits)
        before = [product]
        outs.append(terms)
    return arrange(outs, place, row_count, draft)


def solution(mesh):
    placed = (
        P("dp", None, "tensor", None),
        P("dp", None, "tensor", None),
        P("dp", None, "tensor", None),
        P("dp", None, "tensor", None),
        P("dp", None, "tensor", None),
        P("dp"),
        P("dp", None, "tensor", None),
        P("dp", None, "tensor", None),
        P("dp", None),
        P(),
        P("tensor", None),
    )
    return jax.shard_map(
        body, mesh=mesh, in_specs=placed, out_specs=P("dp", None, "tensor"), check_vma=False
    )
```

```python
import functools
import math

import jax
import jax.numpy as jnp
from jax import lax
from jax.experimental import pallas as pl
from jax.experimental.pallas import tpu as pltpu
from jax.sharding import PartitionSpec as P

BF = jnp.bfloat16
F32 = jnp.float32
EXTRA = 16
LIMIT = 1e30
SMALL = pl.CostEstimate(flops=1 << 20, bytes_accessed=1 << 10, transcendentals=0)


def params(mebibytes):
    return pltpu.CompilerParams(vmem_limit_bytes=mebibytes * 1024 * 1024)


def route(row_prefix, prefix_slot, me, peers, capacity):
    rows = row_prefix.shape[0]
    prefixes = prefix_slot.shape[0]
    name = row_prefix[:, 0]
    row = jnp.arange(rows, dtype=jnp.int32)
    owner = jnp.sum(
        jnp.where(
            row_prefix == jnp.arange(prefixes, dtype=jnp.int32)[None, :], prefix_slot[None, :], 0
        ),
        axis=1,
    )
    same = (name[:, None] == name[None, :]) & (row[None, :] < row[:, None])
    rank = jnp.sum(same.astype(jnp.int32), axis=1)
    half = peers // 2
    shift = owner ^ me
    sent = jnp.where(shift < half, owner % half, shift) * capacity + rank
    target = shift * capacity + rank
    slots = jnp.arange(peers * capacity, dtype=jnp.int32)
    slot_row = jnp.sum(jnp.where(sent[None, :] == slots[:, None], row[None, :], 0), axis=1)
    place = jnp.sum((target[None, :] < target[:, None]).astype(jnp.int32), axis=1)
    at = place[None, :] == row[:, None]
    order = jnp.sum(jnp.where(at, row[None, :], 0), axis=1)
    order_target = jnp.sum(jnp.where(at, target[None, :], 0), axis=1)
    return slot_row, place, order, order_target


def pack_kernel(pieces, capacity, slot_row, q_ref, *refs):
    outs = refs[-len(pieces) :]

    def one(k, _):
        for (first, blocks), out in zip(pieces, outs):
            for b in range(blocks):
                out[b * capacity + k] = q_ref[slot_row[(first + b) * capacity + k]]
        return 0

    lax.fori_loop(0, capacity, one, 0)


def pack(queries, slot_row, pieces, capacity, *before):
    shapes = [
        jax.ShapeDtypeStruct((blocks * capacity,) + queries.shape[1:], BF) for _, blocks in pieces
    ]
    whole = lambda array: pl.BlockSpec(array.shape, lambda i, s: (0, 0, 0, 0))
    packed = pl.pallas_call(
        functools.partial(pack_kernel, pieces, capacity),
        out_shape=shapes,
        grid_spec=pltpu.PrefetchScalarGridSpec(
            num_scalar_prefetch=1,
            grid=(1,),
            in_specs=[whole(queries)] + [pl.BlockSpec(memory_space=pl.ANY)] * len(before),
            out_specs=[whole(shape) for shape in shapes],
        ),
        compiler_params=params(16),
        cost_estimate=SMALL,
        name="pack_queries",
    )(slot_row, queries, *before)
    return [x.reshape(-1, x.shape[-1]) for x in packed]


def split_kernel(heads, steps, k_hbm, v_hbm, kt_ref, vs_ref, buffer, wide, sems):
    step = pl.program_id(0)
    each = buffer.shape[2]
    count = each // heads

    def copy(source, which, part):
        rows = source.at[pl.ds(part * each, each), :]
        return pltpu.make_async_copy(rows, buffer.at[which, part], sems.at[which, part])

    @pl.when(step == 0)
    def _():
        for part in range(steps):
            copy(k_hbm, 0, part).start()
            copy(v_hbm, 1, part).start()

    for which, source in ((0, k_hbm), (1, v_hbm)):
        copy(source, which, step).wait()
        wide[...] = buffer[which, step].astype(F32)
        for a in range(heads):
            part = wide[pl.ds(a, count, stride=heads), :]
            if which == 0:
                kt_ref[a] = part.T.astype(BF)
            else:
                vs_ref[a] = part.astype(BF)


def split_heads(keys, values):
    count, heads, dim = keys.shape
    steps = 4
    each = count // steps
    return pl.pallas_call(
        functools.partial(split_kernel, heads, steps),
        out_shape=[
            jax.ShapeDtypeStruct((heads, dim, count), BF),
            jax.ShapeDtypeStruct((heads, count, dim), BF),
        ],
        grid=(steps,),
        in_specs=[pl.BlockSpec(memory_space=pl.ANY)] * 2,
        out_specs=[
            pl.BlockSpec((heads, dim, each), lambda i: (0, 0, i)),
            pl.BlockSpec((heads, each, dim), lambda i: (0, i, 0)),
        ],
        scratch_shapes=[
            pltpu.VMEM((2, steps, each * heads, dim), BF),
            pltpu.VMEM((each * heads, dim), F32),
            pltpu.SemaphoreType.DMA((2, steps)),
        ],
        compiler_params=params(48),
        cost_estimate=SMALL,
        name="split_heads",
    )(keys.reshape(count * heads, dim), values.reshape(count * heads, dim))


def attend_kernel(capacity, per, group, block, chunk, count, outs, at_ref, *refs):
    del at_ref
    q_refs, (k_ref, v_ref) = refs[:count], refs[count : count + 2]
    o_refs, (acc_ref, weight_ref) = refs[-2 - outs : -2], refs[-2:]
    heads, dim, keys = k_ref.shape
    total = rows = capacity * per
    each = rows // heads
    scale = dim**-0.5 * math.log2(math.e)
    ones = jnp.ones((block, dim), BF)
    turn = pl.program_id(0)
    grid = q_refs[0][...].astype(F32)
    for t in range(1, count):
        grid = jnp.where(turn == t, q_refs[t][...].astype(F32), grid)
    grid = grid.reshape(total // (heads * group), heads, group, dim)
    queries = [grid[:, a].reshape(each, dim).astype(BF) for a in range(heads)]

    def scores(a, j):
        part = k_ref[a, :, pl.ds(j * block, block)]
        return jnp.dot(queries[a], part, preferred_element_type=F32)

    def values(a, j):
        return jnp.concatenate([v_ref[a, pl.ds(j * block, block), :], ones], axis=1)

    def natural(parts):
        split = [x.reshape(each // group, 1, group, dim) for x in parts]
        return jnp.concatenate(split, axis=1).reshape(total, dim)

    def finish(shifts):
        sums = [acc_ref[a, :, dim:] for a in range(heads)]
        out = natural([acc_ref[a, :, :dim] / sums[a] for a in range(heads)]).astype(BF)
        log_sum = natural([shifts[a] + jnp.log2(sums[a]) for a in range(heads)])
        high = log_sum.astype(BF).astype(F32)
        lane = lax.broadcasted_iota(jnp.int32, (total, dim), 1)
        row = lax.broadcasted_iota(jnp.int32, (total, dim), 0)
        term = jnp.where(lane < per, high, log_sum - high)
        term = jnp.where((lane % per == row % per) & (lane < 2 * per), term, 0.0).astype(BF)
        slot = lax.broadcasted_iota(jnp.int32, (EXTRA, rows), 0)
        source = lax.broadcasted_iota(jnp.int32, (EXTRA, rows), 1) // per
        pick = jnp.where(source == slot, 1.0, 0.0).astype(BF)
        logs = jnp.dot(pick, term, preferred_element_type=F32).astype(BF)
        for t, o_ref in enumerate(o_refs):

            @pl.when(turn == t)
            def _():
                o_ref[:rows, :] = out
                o_ref[rows:, :] = logs

    turns = keys // block
    steps = block // chunk

    def middle(part):
        weights = jnp.exp2(part - jnp.max(part, axis=1, keepdims=True))
        total = jnp.sum(weights, axis=1, keepdims=True)
        return jnp.sum(weights * part, axis=1, keepdims=True) / total

    def accumulate(a, j):
        slot = (a * turns + j) % 2
        part = jnp.dot(weight_ref[slot], values(a, j), preferred_element_type=F32)
        if j == 0:
            acc_ref[a] = part
        else:
            acc_ref[a] += part

    shifts = []
    before = None
    for a in range(heads):
        for j in range(turns):
            slot = (a * turns + j) % 2
            for c in range(steps):
                first = j * block + c * chunk
                part = jnp.dot(
                    queries[a], k_ref[a, :, first : first + chunk], preferred_element_type=F32
                )
                if first == 0:
                    shifts.append(middle(part * scale))
                weights = jnp.exp2((part * scale - shifts[a]).astype(BF))
                weight_ref[slot, :, c * chunk : (c + 1) * chunk] = weights
            if before is not None:
                accumulate(*before)
            before = (a, j)
    accumulate(*before)
    finish(shifts)
    fits = jnp.max(acc_ref[:, :, dim:]) < LIMIT

    @pl.when(jnp.logical_not(fits))
    def _():
        acc_ref[...] = jnp.zeros_like(acc_ref)
        tops = []
        for a in range(heads):

            def step(j, top):
                part = scores(a, j) * scale
                new = jnp.maximum(top, jnp.max(part, axis=1, keepdims=True))
                weights = jnp.exp2(part - new).astype(BF)
                acc_ref[a] = acc_ref[a] * jnp.exp2(top - new) + jnp.dot(
                    weights, values(a, j), preferred_element_type=F32
                )
                return new

            tops.append(lax.fori_loop(0, turns, step, jnp.full((each, 1), -1e30, F32)))
        finish(tops)


def attend(queries, keys_t, values, at, capacity, per, group, *before):
    dim = queries[0].shape[1]
    heads, keys, _ = values.shape
    rows = capacity * per
    count = len(queries)
    blocks = count if count > 1 else queries[0].shape[0] // rows
    block = min(1024, keys)
    chunk = min(256, block)
    once = lambda array: pl.BlockSpec(
        array.shape, lambda i, s: (0,) * array.ndim, pipeline_mode=pl.Buffered(1)
    )
    place = (lambda i, s: (0, 0)) if count > 1 else (lambda i, s: (s[0] ^ i, 0))
    out = jax.ShapeDtypeStruct((rows + EXTRA, dim), BF)
    return pl.pallas_call(
        functools.partial(attend_kernel, capacity, per, group, block, chunk, count, blocks),
        out_shape=[out] * blocks,
        grid_spec=pltpu.PrefetchScalarGridSpec(
            num_scalar_prefetch=1,
            grid=(blocks,),
            in_specs=[pl.BlockSpec((rows, dim), place)] * count
            + [once(keys_t), once(values)]
            + [pl.BlockSpec(memory_space=pl.ANY)] * len(before),
            out_specs=[pl.BlockSpec(out.shape, lambda i, s: (0, 0))] * blocks,
            scratch_shapes=[
                pltpu.VMEM((heads, rows // heads, 2 * dim), F32),
                pltpu.VMEM((2, rows // heads, block), BF),
            ],
        ),
        compiler_params=params(24),
        cost_estimate=SMALL,
        name="attend_prefix",
    )(at, *queries, keys_t, values, *before)


def visibility(lengths, draft_count, suffix_count):
    position = jnp.arange(suffix_count + draft_count, dtype=jnp.int32)
    draft_pos = jnp.arange(draft_count, dtype=jnp.int32)
    earlier = position[None, None, :] < lengths[:, None, None]
    earlier = earlier & (position[None, None, :] < suffix_count)
    fresh = (position[None, :] >= suffix_count) & (
        position[None, :] - suffix_count <= draft_pos[:, None]
    )
    return earlier | fresh[None, :, :]


def local_attention(query_grid, key_rows, value_rows, visible):
    scale = query_grid.shape[-1] ** (-0.5)
    scores = (
        jnp.einsum("rtagd,rjad->rtagj", query_grid, key_rows, preferred_element_type=F32) * scale
    )
    visible_mask = visible[:, :, None, None, :]
    scores = jnp.where(visible_mask, scores, F32(-1e30))
    top = jnp.max(scores, axis=-1)
    exponent = jnp.where(visible_mask, jnp.exp(scores - top[..., None]), F32(0.0))
    denominator = jnp.sum(exponent, axis=-1)
    summed = jnp.einsum(
        "rtagj,rjad->rtagd", exponent.astype(BF), value_rows, preferred_element_type=F32
    )
    return summed / denominator[..., None], (top + jnp.log(denominator)) * F32(math.log2(math.e))


def fetch(weight, shards, buffer, sems, width):
    count, _, block = buffer.shape
    each = width // block
    copies = []
    for n in range(count):
        column = pl.multiple_of(shards[n // each] * width + (n % each) * block, block)
        source = weight.at[:, pl.ds(column, block)]
        copies.append(pltpu.make_async_copy(source, buffer.at[n], sems.at[n]))
        copies[-1].start()
    return copies


def multiply(att, copies, buffer, outs):
    block = buffer.shape[2]
    each = len(copies) // len(outs)
    rows = att[...]
    for n, copy in enumerate(copies):
        copy.wait()
        product = jnp.dot(rows, buffer[n], preferred_element_type=F32).astype(BF)
        outs[n // each][:, n % each * block : (n % each + 1) * block] = product


def join_kernel(capacity, count, base, shares, order, target, shards, *refs):
    received, (local, local_log, weight) = refs[:count], refs[count : count + 3]
    att, *outs = refs[-8 - shares - 1 : -8]
    blocks, block_logs, part, mine, logs, spread, buffer, sems = refs[-8:]
    copies = fetch(weight, shards, buffer, sems, outs[0].shape[1])
    rows, per, dim = part.shape
    held = capacity * per
    heads = att.shape[1] // dim
    draft = per // heads
    done = 0
    for array in received:
        for first in range(0, array.shape[0], held + EXTRA):
            values = array[first : first + held, :].astype(F32)
            blocks[done * capacity : (done + 1) * capacity] = values.reshape(capacity, per, dim)
            last = array[first + held : first + held + EXTRA, :].astype(F32)
            block_logs[done * EXTRA : (done + 1) * EXTRA] = last
            done += 1

    def gather(i, _):
        at = order[base + i]
        slot = target[base + i]
        part[i] = blocks[slot]
        mine[i] = local[at].astype(F32)
        place = (slot // capacity) * EXTRA + slot % capacity
        logs[0, pl.ds(i, 1), :] = block_logs[pl.ds(place, 1), :]
        logs[1, pl.ds(i, 1), :] = local_log[pl.ds(at, 1), :]
        return 0

    lax.fori_loop(0, rows, gather, 0)
    lane = lax.broadcasted_iota(jnp.int32, (rows, dim), 1)
    first = logs[0] + pltpu.roll(logs[0], dim - per, axis=1)
    share = 1.0 / (1.0 + jnp.exp2(logs[1] - first))
    high = share.astype(BF).astype(F32)
    low = pltpu.roll(share - high, per, axis=1)
    logs[0] = jnp.where(lane < per, high, jnp.where(lane < 2 * per, low, 0.0))
    diagonal = lax.broadcasted_iota(jnp.int32, (per, dim), 1) % per
    diagonal = diagonal == lax.broadcasted_iota(jnp.int32, (per, dim), 0)

    def widen(i, _):
        row = logs[0, pl.ds(i, 1), :]
        spread[i] = jnp.where(diagonal, row, 0.0).astype(BF)
        return 0

    lax.fori_loop(0, rows, widen, 0)
    ones = jnp.ones((dim, dim), BF)
    shares = jnp.dot(
        spread[...].reshape(rows * per, dim), ones, preferred_element_type=F32
    ).reshape(rows, per, dim)
    part[...] = mine[...] + shares * (part[...] - mine[...])
    flat = part.reshape(rows * per, dim)
    for h in range(heads):
        head = flat[pl.ds(h, rows * draft, stride=heads), :]
        att[:, h * dim : (h + 1) * dim] = head.astype(BF)


    multiply(att, copies, buffer, outs)


def join(
    received, local, local_log, order, target, heads, base, rows, capacity, weight, shards, width, *before
):
    count = len(received)
    per, dim = local.shape[1:]
    blocks = sum(array.shape[0] for array in received) // (capacity * per + EXTRA)
    shares = shards.shape[0]
    lines = rows * per // heads
    block = min(256, width)
    whole = lambda array: pl.BlockSpec(array.shape, lambda n, *_: (0,) * array.ndim)
    att = jax.ShapeDtypeStruct((lines, heads * dim), BF)
    out = jax.ShapeDtypeStruct((lines, width), BF)
    return pl.pallas_call(
        functools.partial(join_kernel, capacity, count, base, shares),
        out_shape=[att] + [out] * shares,
        grid_spec=pltpu.PrefetchScalarGridSpec(
            num_scalar_prefetch=3,
            grid=(1,),
            in_specs=[whole(array) for array in received]
            + [whole(local), whole(local_log)]
            + [pl.BlockSpec(memory_space=pl.ANY)] * (1 + len(before)),
            out_specs=[whole(att)] + [whole(out)] * shares,
            scratch_shapes=[
                pltpu.VMEM((blocks * capacity, per, dim), F32),
                pltpu.VMEM((blocks * EXTRA, dim), F32),
                pltpu.VMEM((rows, per, dim), F32),
                pltpu.VMEM((rows, per, dim), F32),
                pltpu.VMEM((2, rows, dim), F32),
                pltpu.VMEM((rows, per, dim), BF),
                pltpu.VMEM((shares * width // block, heads * dim, block), BF),
                pltpu.SemaphoreType.DMA((shares * width // block,)),
            ],
        ),
        compiler_params=params(48),
        cost_estimate=SMALL,
        name="join_project",
    )(order, target, shards, *received, local, local_log, weight, *before)


def project_kernel(shares, shards, att, weight, *refs):
    outs, (buffer, sems) = refs[-2 - shares : -2], refs[-2:]
    multiply(att, fetch(weight, shards, buffer, sems, outs[0].shape[1]), buffer, outs)


def project(att, weight, shards, width, *before):
    rows, depth = att.shape
    shares = shards.shape[0]
    block = min(256, width)
    out = jax.ShapeDtypeStruct((rows, width), BF)
    whole = lambda array: pl.BlockSpec(array.shape, lambda n, *_: (0,) * array.ndim)
    return pl.pallas_call(
        functools.partial(project_kernel, shares),
        out_shape=[out] * shares,
        grid_spec=pltpu.PrefetchScalarGridSpec(
            num_scalar_prefetch=1,
            grid=(1,),
            in_specs=[whole(att)] + [pl.BlockSpec(memory_space=pl.ANY)] * (1 + len(before)),
            out_specs=[whole(out)] * shares,
            scratch_shapes=[
                pltpu.VMEM((shares * width // block, depth, block), BF),
                pltpu.SemaphoreType.DMA((shares * width // block,)),
            ],
        ),
        compiler_params=params(48),
        cost_estimate=SMALL,
        name="project",
    )(shards, att, weight, *before)


def project_sum(join_with, weight, own, split, before):
    size = lax.axis_size("tensor")
    chips = size // 2
    width = weight.shape[1] // size
    order = list(range(1, chips)) + [0]
    shards = [own ^ (2 * d + other) for d in order for other in (1, 0)]
    with_join = 1 if split else len(shards)
    att, *products = join_with(jnp.stack(shards[:with_join]), width)
    got = []
    for k, d in enumerate(order):
        while len(products) < 2 * k + 2:
            waits = before if d == 0 else []
            wanted = shards[len(products) :] if d == 0 else shards[len(products) : len(products) + 1]
            products += project(att, weight, jnp.stack(wanted), width, *waits)
        send, keep = products[2 * k : 2 * k + 2]
        there = lax.ppermute(send, "tensor", [(i, i ^ 1) for i in range(size)])
        if d:
            total = (keep.astype(F32) + there.astype(F32)).astype(BF)
            before = list(before) + [total]
            got.append(lax.ppermute(total, "tensor", [(i, i ^ (2 * d)) for i in range(size)]))
    total = keep.astype(F32)
    for term in got:
        total = total + term.astype(F32)
    return [total, there], [total], keep


def arrange_kernel(counts, place_ref, *refs):
    out_ref = refs[-1]
    rows, draft, _ = out_ref.shape
    halves, start = [], 0
    for count in counts:
        total = refs[start][...]
        for term in refs[start + 1 : start + count]:
            total = total + term[...].astype(F32)
        halves.append(total.astype(BF))
        start += count
    values = jnp.concatenate(halves, axis=0)
    size = rows * draft
    pick = lax.broadcasted_iota(jnp.int32, (size, size), 1) == place_ref[...]
    result = jnp.dot(
        jnp.where(pick, 1.0, 0.0).astype(BF), values, preferred_element_type=F32
    )
    for r in range(rows):
        out_ref[r] = result[r * draft : (r + 1) * draft].astype(BF)


def arrange(halves, place, rows, draft):
    width = halves[0][0].shape[1]
    index = (place[:, None] * draft + jnp.arange(draft, dtype=jnp.int32)[None, :]).reshape(-1, 1)
    return pl.pallas_call(
        functools.partial(arrange_kernel, [len(half) for half in halves]),
        out_shape=jax.ShapeDtypeStruct((rows, draft, width), BF),
        compiler_params=params(20),
        cost_estimate=SMALL,
        name="arrange_rows",
    )(index, *[term for half in halves for term in half])


def exchange(x):
    size = lax.axis_size("dp")
    groups = [list(range(size // 2)), list(range(size // 2, size))]
    return lax.all_to_all(
        x, "dp", split_axis=0, concat_axis=0, axis_index_groups=groups, tiled=True
    )


def hop(x, shift):
    size = lax.axis_size("dp")
    return lax.ppermute(x, "dp", [(i, i ^ shift) for i in range(size)])


def body(
    queries,
    draft_keys,
    draft_values,
    suffix_keys,
    suffix_values,
    suffix_len,
    prefix_keys,
    prefix_values,
    row_prefix,
    prefix_slot,
    out_weight,
):
    row_count, draft, query_heads, dim = queries.shape
    heads = draft_keys.shape[2]
    group = query_heads // heads
    per = draft * query_heads
    suffix_count = suffix_keys.shape[1]
    peers = lax.axis_size("dp")
    capacity = 2 * row_count // peers
    own = lax.axis_index("tensor").astype(jnp.int32)
    me = lax.axis_index("dp").astype(jnp.int32)

    slot_row, place, order, target = route(row_prefix, prefix_slot, me, peers, capacity)
    half = peers // 2
    lead = half // 2
    first = pack(queries, slot_row, [(half + d, 1) for d in range(lead)], capacity)
    near, *late = pack(
        queries,
        slot_row,
        [(0, half)] + [(half + d, 1) for d in range(lead, half)],
        capacity,
        first[0],
    )
    far = [hop(x, half + d) for d, x in enumerate(first + late)]
    near = exchange(near)

    keys_t, values = split_heads(prefix_keys[0], prefix_values[0])
    here = (me % half).reshape(1)
    zero = jnp.zeros((1,), jnp.int32)
    back, before = [None] * peers, []
    for batch in [range(half, half + lead), range(half)] + [[d] for d in range(half + lead, peers)]:
        arrays = [near] if batch[0] == 0 else [far[d - half] for d in batch]
        if batch[-1] == peers - 1:
            before = list(before) + back[half : half + lead]
        at = here if batch[0] == 0 else zero
        results = attend(arrays, keys_t, values, at, capacity, per, group, *before)
        before = results[:1]
        for d, result in zip(batch, results):
            back[d] = hop(result, d) if d else result

    query_grid = queries.reshape(row_count, draft, heads, group, dim)
    all_keys = jnp.concatenate([suffix_keys, draft_keys], axis=1)
    all_values = jnp.concatenate([suffix_values, draft_values], axis=1)
    visible = visibility(suffix_len, draft, suffix_count)
    local, local_log = local_attention(query_grid, all_keys, all_values, visible)
    local = local.reshape(row_count, per, dim).astype(BF)
    local_log = jnp.pad(local_log.reshape(row_count, per), ((0, 0), (0, dim - per)))

    rows = row_count // 2
    early = peers - rows // capacity
    outs, waits = [], []
    for base in (0, rows):
        received = back if base else back[:early]

        def join_with(shards, width):
            return join(
                received,
                local,
                local_log,
                order,
                target,
                query_heads,
                base,
                rows,
                capacity,
                out_weight,
                shards,
                width,
                *before,
            )

        terms, waits, product = project_sum(join_with, out_weight, own, base > 0, waits)
        before = [product]
        outs.append(terms)
    return arrange(outs, place, row_count, draft)


def solution(mesh):
    placed = (
        P("dp", None, "tensor", None),
        P("dp", None, "tensor", None),
        P("dp", None, "tensor", None),
        P("dp", None, "tensor", None),
        P("dp", None, "tensor", None),
        P("dp"),
        P("dp", None, "tensor", None),
        P("dp", None, "tensor", None),
        P("dp", None),
        P(),
        P("tensor", None),
    )
    return jax.shard_map(
        body, mesh=mesh, in_specs=placed, out_specs=P("dp", None, "tensor"), check_vma=False
    )
```

```python
import functools
import math

import jax
import jax.numpy as jnp
from jax import lax
from jax.experimental import pallas as pl
from jax.experimental.pallas import tpu as pltpu
from jax.sharding import PartitionSpec as P

BF = jnp.bfloat16
F32 = jnp.float32
EXTRA = 16
LIMIT = 1e30
SMALL = pl.CostEstimate(flops=1 << 20, bytes_accessed=1 << 10, transcendentals=0)


def params(mebibytes):
    return pltpu.CompilerParams(vmem_limit_bytes=mebibytes * 1024 * 1024)


def route(row_prefix, prefix_slot, me, peers, capacity):
    rows = row_prefix.shape[0]
    prefixes = prefix_slot.shape[0]
    name = row_prefix[:, 0]
    row = jnp.arange(rows, dtype=jnp.int32)
    owner = jnp.sum(
        jnp.where(
            row_prefix == jnp.arange(prefixes, dtype=jnp.int32)[None, :], prefix_slot[None, :], 0
        ),
        axis=1,
    )
    same = (name[:, None] == name[None, :]) & (row[None, :] < row[:, None])
    rank = jnp.sum(same.astype(jnp.int32), axis=1)
    half = peers // 2
    shift = owner ^ me
    sent = jnp.where(shift < half, owner % half, shift) * capacity + rank
    target = shift * capacity + rank
    slots = jnp.arange(peers * capacity, dtype=jnp.int32)
    slot_row = jnp.sum(jnp.where(sent[None, :] == slots[:, None], row[None, :], 0), axis=1)
    place = jnp.sum((target[None, :] < target[:, None]).astype(jnp.int32), axis=1)
    at = place[None, :] == row[:, None]
    order = jnp.sum(jnp.where(at, row[None, :], 0), axis=1)
    order_target = jnp.sum(jnp.where(at, target[None, :], 0), axis=1)
    return slot_row, place, order, order_target


def pack_kernel(pieces, capacity, slot_row, q_ref, *refs):
    outs = refs[-len(pieces) :]

    def one(k, _):
        for (first, blocks), out in zip(pieces, outs):
            for b in range(blocks):
                out[b * capacity + k] = q_ref[slot_row[(first + b) * capacity + k]]
        return 0

    lax.fori_loop(0, capacity, one, 0)


def pack(queries, slot_row, pieces, capacity, *before):
    shapes = [
        jax.ShapeDtypeStruct((blocks * capacity,) + queries.shape[1:], BF) for _, blocks in pieces
    ]
    whole = lambda array: pl.BlockSpec(array.shape, lambda i, s: (0, 0, 0, 0))
    packed = pl.pallas_call(
        functools.partial(pack_kernel, pieces, capacity),
        out_shape=shapes,
        grid_spec=pltpu.PrefetchScalarGridSpec(
            num_scalar_prefetch=1,
            grid=(1,),
            in_specs=[whole(queries)] + [pl.BlockSpec(memory_space=pl.ANY)] * len(before),
            out_specs=[whole(shape) for shape in shapes],
        ),
        compiler_params=params(16),
        cost_estimate=SMALL,
        name="pack_queries",
    )(slot_row, queries, *before)
    return [x.reshape(-1, x.shape[-1]) for x in packed]


def split_kernel(heads, steps, k_hbm, v_hbm, kt_ref, vs_ref, buffer, wide, sems):
    step = pl.program_id(0)
    each = buffer.shape[2]
    count = each // heads

    def copy(source, which, part):
        rows = source.at[pl.ds(part * each, each), :]
        return pltpu.make_async_copy(rows, buffer.at[which, part], sems.at[which, part])

    @pl.when(step == 0)
    def _():
        for part in range(steps):
            copy(k_hbm, 0, part).start()
            copy(v_hbm, 1, part).start()

    for which, source in ((0, k_hbm), (1, v_hbm)):
        copy(source, which, step).wait()
        wide[...] = buffer[which, step].astype(F32)
        for a in range(heads):
            part = wide[pl.ds(a, count, stride=heads), :]
            if which == 0:
                kt_ref[a] = part.T.astype(BF)
            else:
                vs_ref[a] = part.astype(BF)


def split_heads(keys, values):
    count, heads, dim = keys.shape
    steps = 4
    each = count // steps
    return pl.pallas_call(
        functools.partial(split_kernel, heads, steps),
        out_shape=[
            jax.ShapeDtypeStruct((heads, dim, count), BF),
            jax.ShapeDtypeStruct((heads, count, dim), BF),
        ],
        grid=(steps,),
        in_specs=[pl.BlockSpec(memory_space=pl.ANY)] * 2,
        out_specs=[
            pl.BlockSpec((heads, dim, each), lambda i: (0, 0, i)),
            pl.BlockSpec((heads, each, dim), lambda i: (0, i, 0)),
        ],
        scratch_shapes=[
            pltpu.VMEM((2, steps, each * heads, dim), BF),
            pltpu.VMEM((each * heads, dim), F32),
            pltpu.SemaphoreType.DMA((2, steps)),
        ],
        compiler_params=params(48),
        cost_estimate=SMALL,
        name="split_heads",
    )(keys.reshape(count * heads, dim), values.reshape(count * heads, dim))


def attend_kernel(capacity, per, group, block, chunk, count, outs, at_ref, *refs):
    del at_ref
    q_refs, (k_ref, v_ref) = refs[:count], refs[count : count + 2]
    o_refs, (acc_ref, weight_ref) = refs[-2 - outs : -2], refs[-2:]
    heads, dim, keys = k_ref.shape
    total = rows = capacity * per
    each = rows // heads
    scale = dim**-0.5 * math.log2(math.e)
    ones = jnp.ones((block, dim), BF)
    turn = pl.program_id(0)
    grid = q_refs[0][...].astype(F32)
    for t in range(1, count):
        grid = jnp.where(turn == t, q_refs[t][...].astype(F32), grid)
    grid = grid.reshape(total // (heads * group), heads, group, dim)
    queries = [grid[:, a].reshape(each, dim).astype(BF) for a in range(heads)]

    def scores(a, j):
        part = k_ref[a, :, pl.ds(j * block, block)]
        return jnp.dot(queries[a], part, preferred_element_type=F32)

    def values(a, j):
        return jnp.concatenate([v_ref[a, pl.ds(j * block, block), :], ones], axis=1)

    def natural(parts):
        split = [x.reshape(each // group, 1, group, dim) for x in parts]
        return jnp.concatenate(split, axis=1).reshape(total, dim)

    def finish(shifts):
        sums = [acc_ref[a, :, dim:] for a in range(heads)]
        out = natural([acc_ref[a, :, :dim] / sums[a] for a in range(heads)]).astype(BF)
        log_sum = natural([shifts[a] + jnp.log2(sums[a]) for a in range(heads)])
        high = log_sum.astype(BF).astype(F32)
        lane = lax.broadcasted_iota(jnp.int32, (total, dim), 1)
        row = lax.broadcasted_iota(jnp.int32, (total, dim), 0)
        term = jnp.where(lane < per, high, log_sum - high)
        term = jnp.where((lane % per == row % per) & (lane < 2 * per), term, 0.0).astype(BF)
        slot = lax.broadcasted_iota(jnp.int32, (EXTRA, rows), 0)
        source = lax.broadcasted_iota(jnp.int32, (EXTRA, rows), 1) // per
        pick = jnp.where(source == slot, 1.0, 0.0).astype(BF)
        logs = jnp.dot(pick, term, preferred_element_type=F32).astype(BF)
        for t, o_ref in enumerate(o_refs):

            @pl.when(turn == t)
            def _():
                o_ref[:rows, :] = out
                o_ref[rows:, :] = logs

    turns = keys // block
    steps = block // chunk

    def middle(part):
        weights = jnp.exp2(part - jnp.max(part, axis=1, keepdims=True))
        total = jnp.sum(weights, axis=1, keepdims=True)
        return jnp.sum(weights * part, axis=1, keepdims=True) / total

    def accumulate(a, j):
        slot = (a * turns + j) % 2
        part = jnp.dot(weight_ref[slot], values(a, j), preferred_element_type=F32)
        if j == 0:
            acc_ref[a] = part
        else:
            acc_ref[a] += part

    shifts = []
    before = None
    for a in range(heads):
        for j in range(turns):
            slot = (a * turns + j) % 2
            for c in range(steps):
                first = j * block + c * chunk
                part = jnp.dot(
                    queries[a], k_ref[a, :, first : first + chunk], preferred_element_type=F32
                )
                if first == 0:
                    shifts.append(middle(part * scale))
                weights = jnp.exp2((part * scale - shifts[a]).astype(BF))
                weight_ref[slot, :, c * chunk : (c + 1) * chunk] = weights
            if before is not None:
                accumulate(*before)
            before = (a, j)
    accumulate(*before)
    finish(shifts)
    fits = jnp.max(acc_ref[:, :, dim:]) < LIMIT

    @pl.when(jnp.logical_not(fits))
    def _():
        acc_ref[...] = jnp.zeros_like(acc_ref)
        tops = []
        for a in range(heads):

            def step(j, top):
                part = scores(a, j) * scale
                new = jnp.maximum(top, jnp.max(part, axis=1, keepdims=True))
                weights = jnp.exp2(part - new).astype(BF)
                acc_ref[a] = acc_ref[a] * jnp.exp2(top - new) + jnp.dot(
                    weights, values(a, j), preferred_element_type=F32
                )
                return new

            tops.append(lax.fori_loop(0, turns, step, jnp.full((each, 1), -1e30, F32)))
        finish(tops)


def attend(queries, keys_t, values, at, capacity, per, group, *before):
    dim = queries[0].shape[1]
    heads, keys, _ = values.shape
    rows = capacity * per
    count = len(queries)
    blocks = count if count > 1 else queries[0].shape[0] // rows
    block = min(1024, keys)
    chunk = min(256, block)
    once = lambda array: pl.BlockSpec(
        array.shape, lambda i, s: (0,) * array.ndim, pipeline_mode=pl.Buffered(1)
    )
    place = (lambda i, s: (0, 0)) if count > 1 else (lambda i, s: (s[0] ^ i, 0))
    out = jax.ShapeDtypeStruct((rows + EXTRA, dim), BF)
    return pl.pallas_call(
        functools.partial(attend_kernel, capacity, per, group, block, chunk, count, blocks),
        out_shape=[out] * blocks,
        grid_spec=pltpu.PrefetchScalarGridSpec(
            num_scalar_prefetch=1,
            grid=(blocks,),
            in_specs=[pl.BlockSpec((rows, dim), place)] * count
            + [once(keys_t), once(values)]
            + [pl.BlockSpec(memory_space=pl.ANY)] * len(before),
            out_specs=[pl.BlockSpec(out.shape, lambda i, s: (0, 0))] * blocks,
            scratch_shapes=[
                pltpu.VMEM((heads, rows // heads, 2 * dim), F32),
                pltpu.VMEM((2, rows // heads, block), BF),
            ],
        ),
        compiler_params=params(24),
        cost_estimate=SMALL,
        name="attend_prefix",
    )(at, *queries, keys_t, values, *before)


def visibility(lengths, draft_count, suffix_count):
    position = jnp.arange(suffix_count + draft_count, dtype=jnp.int32)
    draft_pos = jnp.arange(draft_count, dtype=jnp.int32)
    earlier = position[None, None, :] < lengths[:, None, None]
    earlier = earlier & (position[None, None, :] < suffix_count)
    fresh = (position[None, :] >= suffix_count) & (
        position[None, :] - suffix_count <= draft_pos[:, None]
    )
    return earlier | fresh[None, :, :]


def local_attention(query_grid, key_rows, value_rows, visible):
    scale = query_grid.shape[-1] ** (-0.5)
    scores = (
        jnp.einsum("rtagd,rjad->rtagj", query_grid, key_rows, preferred_element_type=F32) * scale
    )
    visible_mask = visible[:, :, None, None, :]
    scores = jnp.where(visible_mask, scores, F32(-1e30))
    top = jnp.max(scores, axis=-1)
    exponent = jnp.where(visible_mask, jnp.exp(scores - top[..., None]), F32(0.0))
    denominator = jnp.sum(exponent, axis=-1)
    summed = jnp.einsum(
        "rtagj,rjad->rtagd", exponent.astype(BF), value_rows, preferred_element_type=F32
    )
    return summed / denominator[..., None], (top + jnp.log(denominator)) * F32(math.log2(math.e))


def fetch(weight, shards, buffer, sems, width):
    count, _, block = buffer.shape
    each = width // block
    copies = []
    for n in range(count):
        column = pl.multiple_of(shards[n // each] * width + (n % each) * block, block)
        source = weight.at[:, pl.ds(column, block)]
        copies.append(pltpu.make_async_copy(source, buffer.at[n], sems.at[n]))
        copies[-1].start()
    return copies


def multiply(att, copies, buffer, outs):
    block = buffer.shape[2]
    each = len(copies) // len(outs)
    rows = att[...]
    for n, copy in enumerate(copies):
        copy.wait()
        product = jnp.dot(rows, buffer[n], preferred_element_type=F32).astype(BF)
        outs[n // each][:, n % each * block : (n % each + 1) * block] = product


def join_kernel(capacity, count, base, shares, order, target, shards, *refs):
    received, (local, local_log, weight) = refs[:count], refs[count : count + 3]
    att, *outs = refs[-8 - shares - 1 : -8]
    blocks, block_logs, part, mine, logs, spread, buffer, sems = refs[-8:]
    copies = fetch(weight, shards, buffer, sems, outs[0].shape[1])
    rows, per, dim = part.shape
    held = capacity * per
    heads = att.shape[1] // dim
    draft = per // heads
    done = 0
    for array in received:
        for first in range(0, array.shape[0], held + EXTRA):
            values = array[first : first + held, :].astype(F32)
            blocks[done * capacity : (done + 1) * capacity] = values.reshape(capacity, per, dim)
            last = array[first + held : first + held + EXTRA, :].astype(F32)
            block_logs[done * EXTRA : (done + 1) * EXTRA] = last
            done += 1

    def gather(i, _):
        at = order[base + i]
        slot = target[base + i]
        part[i] = blocks[slot]
        mine[i] = local[at].astype(F32)
        place = (slot // capacity) * EXTRA + slot % capacity
        logs[0, pl.ds(i, 1), :] = block_logs[pl.ds(place, 1), :]
        logs[1, pl.ds(i, 1), :] = local_log[pl.ds(at, 1), :]
        return 0

    lax.fori_loop(0, rows, gather, 0)
    lane = lax.broadcasted_iota(jnp.int32, (rows, dim), 1)
    first = logs[0] + pltpu.roll(logs[0], dim - per, axis=1)
    share = 1.0 / (1.0 + jnp.exp2(logs[1] - first))
    high = share.astype(BF).astype(F32)
    low = pltpu.roll(share - high, per, axis=1)
    logs[0] = jnp.where(lane < per, high, jnp.where(lane < 2 * per, low, 0.0))
    diagonal = lax.broadcasted_iota(jnp.int32, (per, dim), 1) % per
    diagonal = diagonal == lax.broadcasted_iota(jnp.int32, (per, dim), 0)

    def widen(i, _):
        row = logs[0, pl.ds(i, 1), :]
        spread[i] = jnp.where(diagonal, row, 0.0).astype(BF)
        return 0

    lax.fori_loop(0, rows, widen, 0)
    ones = jnp.ones((dim, dim), BF)
    shares = jnp.dot(
        spread[...].reshape(rows * per, dim), ones, preferred_element_type=F32
    ).reshape(rows, per, dim)
    part[...] = mine[...] + shares * (part[...] - mine[...])
    flat = part.reshape(rows * per, dim)
    for h in range(heads):
        head = flat[pl.ds(h, rows * draft, stride=heads), :]
        att[:, h * dim : (h + 1) * dim] = head.astype(BF)


    multiply(att, copies, buffer, outs)


def join(
    received, local, local_log, order, target, heads, base, rows, capacity, weight, shards, width, *before
):
    count = len(received)
    per, dim = local.shape[1:]
    blocks = sum(array.shape[0] for array in received) // (capacity * per + EXTRA)
    shares = shards.shape[0]
    lines = rows * per // heads
    block = min(256, width)
    whole = lambda array: pl.BlockSpec(array.shape, lambda n, *_: (0,) * array.ndim)
    att = jax.ShapeDtypeStruct((lines, heads * dim), BF)
    out = jax.ShapeDtypeStruct((lines, width), BF)
    return pl.pallas_call(
        functools.partial(join_kernel, capacity, count, base, shares),
        out_shape=[att] + [out] * shares,
        grid_spec=pltpu.PrefetchScalarGridSpec(
            num_scalar_prefetch=3,
            grid=(1,),
            in_specs=[whole(array) for array in received]
            + [whole(local), whole(local_log)]
            + [pl.BlockSpec(memory_space=pl.ANY)] * (1 + len(before)),
            out_specs=[whole(att)] + [whole(out)] * shares,
            scratch_shapes=[
                pltpu.VMEM((blocks * capacity, per, dim), F32),
                pltpu.VMEM((blocks * EXTRA, dim), F32),
                pltpu.VMEM((rows, per, dim), F32),
                pltpu.VMEM((rows, per, dim), F32),
                pltpu.VMEM((2, rows, dim), F32),
                pltpu.VMEM((rows, per, dim), BF),
                pltpu.VMEM((shares * width // block, heads * dim, block), BF),
                pltpu.SemaphoreType.DMA((shares * width // block,)),
            ],
        ),
        compiler_params=params(48),
        cost_estimate=SMALL,
        name="join_project",
    )(order, target, shards, *received, local, local_log, weight, *before)


def project_kernel(shares, shards, att, weight, *refs):
    outs, (buffer, sems) = refs[-2 - shares : -2], refs[-2:]
    multiply(att, fetch(weight, shards, buffer, sems, outs[0].shape[1]), buffer, outs)


def project(att, weight, shards, width, *before):
    rows, depth = att.shape
    shares = shards.shape[0]
    block = min(256, width)
    out = jax.ShapeDtypeStruct((rows, width), BF)
    whole = lambda array: pl.BlockSpec(array.shape, lambda n, *_: (0,) * array.ndim)
    return pl.pallas_call(
        functools.partial(project_kernel, shares),
        out_shape=[out] * shares,
        grid_spec=pltpu.PrefetchScalarGridSpec(
            num_scalar_prefetch=1,
            grid=(1,),
            in_specs=[whole(att)] + [pl.BlockSpec(memory_space=pl.ANY)] * (1 + len(before)),
            out_specs=[whole(out)] * shares,
            scratch_shapes=[
                pltpu.VMEM((shares * width // block, depth, block), BF),
                pltpu.SemaphoreType.DMA((shares * width // block,)),
            ],
        ),
        compiler_params=params(48),
        cost_estimate=SMALL,
        name="project",
    )(shards, att, weight, *before)


def project_sum(join_with, weight, shards, split, before):
    size = lax.axis_size("tensor")
    chips = size // 2
    width = weight.shape[1] // size
    order = list(range(1, chips)) + [0]
    with_join = 1 if split else len(shards)
    att, *products = join_with(jnp.concatenate(shards[:with_join]), width)
    got = []
    for k, d in enumerate(order):
        while len(products) < 2 * k + 2:
            waits = before if d == 0 else []
            wanted = shards[len(products) :] if d == 0 else shards[len(products) : len(products) + 1]
            products += project(att, weight, jnp.concatenate(wanted), width, *waits)
        send, keep = products[2 * k : 2 * k + 2]
        there = lax.ppermute(send, "tensor", [(i, i ^ 1) for i in range(size)])
        if d:
            total = (keep.astype(F32) + there.astype(F32)).astype(BF)
            before = list(before) + [total]
            got.append(lax.ppermute(total, "tensor", [(i, i ^ (2 * d)) for i in range(size)]))
    total = keep.astype(F32)
    for term in got:
        total = total + term.astype(F32)
    return [total, there], [total], keep


def arrange_kernel(counts, place_ref, *refs):
    out_ref = refs[-1]
    rows, draft, _ = out_ref.shape
    halves, start = [], 0
    for count in counts:
        total = refs[start][...]
        for term in refs[start + 1 : start + count]:
            total = total + term[...].astype(F32)
        halves.append(total.astype(BF))
        start += count
    values = jnp.concatenate(halves, axis=0)
    size = rows * draft
    pick = lax.broadcasted_iota(jnp.int32, (size, size), 1) == place_ref[...]
    result = jnp.dot(
        jnp.where(pick, 1.0, 0.0).astype(BF), values, preferred_element_type=F32
    )
    for r in range(rows):
        out_ref[r] = result[r * draft : (r + 1) * draft].astype(BF)


def arrange(halves, place, rows, draft):
    width = halves[0][0].shape[1]
    index = (place[:, None] * draft + jnp.arange(draft, dtype=jnp.int32)[None, :]).reshape(-1, 1)
    return pl.pallas_call(
        functools.partial(arrange_kernel, [len(half) for half in halves]),
        out_shape=jax.ShapeDtypeStruct((rows, draft, width), BF),
        compiler_params=params(20),
        cost_estimate=SMALL,
        name="arrange_rows",
    )(index, *[term for half in halves for term in half])


def exchange(x):
    size = lax.axis_size("dp")
    groups = [list(range(size // 2)), list(range(size // 2, size))]
    return lax.all_to_all(
        x, "dp", split_axis=0, concat_axis=0, axis_index_groups=groups, tiled=True
    )


def hop(x, shift):
    size = lax.axis_size("dp")
    return lax.ppermute(x, "dp", [(i, i ^ shift) for i in range(size)])


def body(
    queries,
    draft_keys,
    draft_values,
    suffix_keys,
    suffix_values,
    suffix_len,
    prefix_keys,
    prefix_values,
    row_prefix,
    prefix_slot,
    out_weight,
):
    row_count, draft, query_heads, dim = queries.shape
    heads = draft_keys.shape[2]
    group = query_heads // heads
    per = draft * query_heads
    suffix_count = suffix_keys.shape[1]
    peers = lax.axis_size("dp")
    capacity = 2 * row_count // peers
    own = lax.axis_index("tensor").astype(jnp.int32)
    me = lax.axis_index("dp").astype(jnp.int32)

    size = lax.axis_size("tensor")
    half = peers // 2
    here = (me % half).reshape(1)
    distances = list(range(1, size // 2)) + [0]
    shards = [(own ^ (2 * d + other)).reshape(1) for d in distances for other in (1, 0)]

    slot_row, place, order, target = route(row_prefix, prefix_slot, me, peers, capacity)
    lead = half // 2
    first = pack(queries, slot_row, [(half + d, 1) for d in range(lead)], capacity, here, *shards)
    near, *late = pack(
        queries,
        slot_row,
        [(0, half)] + [(half + d, 1) for d in range(lead, half)],
        capacity,
        first[0],
    )
    far = [hop(x, half + d) for d, x in enumerate(first + late)]
    near = exchange(near)

    keys_t, values = split_heads(prefix_keys[0], prefix_values[0])
    zero = jnp.zeros((1,), jnp.int32)
    back, before = [None] * peers, []
    for batch in [range(half, half + lead), range(half)] + [[d] for d in range(half + lead, peers)]:
        arrays = [near] if batch[0] == 0 else [far[d - half] for d in batch]
        if batch[-1] == peers - 1:
            before = list(before) + back[half : half + lead]
        at = here if batch[0] == 0 else zero
        results = attend(arrays, keys_t, values, at, capacity, per, group, *before)
        before = results[:1]
        for d, result in zip(batch, results):
            back[d] = hop(result, d) if d else result

    query_grid = queries.reshape(row_count, draft, heads, group, dim)
    all_keys = jnp.concatenate([suffix_keys, draft_keys], axis=1)
    all_values = jnp.concatenate([suffix_values, draft_values], axis=1)
    visible = visibility(suffix_len, draft, suffix_count)
    local, local_log = local_attention(query_grid, all_keys, all_values, visible)
    local = local.reshape(row_count, per, dim).astype(BF)
    local_log = jnp.pad(local_log.reshape(row_count, per), ((0, 0), (0, dim - per)))

    rows = row_count // 2
    early = peers - rows // capacity
    outs, waits = [], []
    for base in (0, rows):
        received = back if base else back[:early]

        def join_with(shards, width):
            return join(
                received,
                local,
                local_log,
                order,
                target,
                query_heads,
                base,
                rows,
                capacity,
                out_weight,
                shards,
                width,
                *before,
            )

        terms, waits, product = project_sum(join_with, out_weight, shards, base > 0, waits)
        before = [product]
        outs.append(terms)
    return arrange(outs, place, row_count, draft)


def solution(mesh):
    placed = (
        P("dp", None, "tensor", None),
        P("dp", None, "tensor", None),
        P("dp", None, "tensor", None),
        P("dp", None, "tensor", None),
        P("dp", None, "tensor", None),
        P("dp"),
        P("dp", None, "tensor", None),
        P("dp", None, "tensor", None),
        P("dp", None),
        P(),
        P("tensor", None),
    )
    return jax.shard_map(
        body, mesh=mesh, in_specs=placed, out_specs=P("dp", None, "tensor"), check_vma=False
    )
```

```python
import functools
import math

import jax
import jax.numpy as jnp
from jax import lax
from jax.experimental import pallas as pl
from jax.experimental.pallas import tpu as pltpu
from jax.sharding import PartitionSpec as P

BF = jnp.bfloat16
F32 = jnp.float32
EXTRA = 16
LIMIT = 1e30
SMALL = pl.CostEstimate(flops=1 << 20, bytes_accessed=1 << 10, transcendentals=0)


def params(mebibytes):
    return pltpu.CompilerParams(vmem_limit_bytes=mebibytes * 1024 * 1024)


def route(row_prefix, prefix_slot, me, peers, capacity):
    rows = row_prefix.shape[0]
    prefixes = prefix_slot.shape[0]
    name = row_prefix[:, 0]
    row = jnp.arange(rows, dtype=jnp.int32)
    owner = jnp.sum(
        jnp.where(
            row_prefix == jnp.arange(prefixes, dtype=jnp.int32)[None, :], prefix_slot[None, :], 0
        ),
        axis=1,
    )
    same = (name[:, None] == name[None, :]) & (row[None, :] < row[:, None])
    rank = jnp.sum(same.astype(jnp.int32), axis=1)
    half = peers // 2
    shift = owner ^ me
    sent = jnp.where(shift < half, owner % half, shift) * capacity + rank
    target = shift * capacity + rank
    slots = jnp.arange(peers * capacity, dtype=jnp.int32)
    slot_row = jnp.sum(jnp.where(sent[None, :] == slots[:, None], row[None, :], 0), axis=1)
    place = jnp.sum((target[None, :] < target[:, None]).astype(jnp.int32), axis=1)
    at = place[None, :] == row[:, None]
    order = jnp.sum(jnp.where(at, row[None, :], 0), axis=1)
    order_target = jnp.sum(jnp.where(at, target[None, :], 0), axis=1)
    return slot_row, place, order, order_target


def pack_kernel(pieces, capacity, slot_row, q_ref, *refs):
    outs = refs[-len(pieces) :]

    def one(k, _):
        for (first, blocks), out in zip(pieces, outs):
            for b in range(blocks):
                out[b * capacity + k] = q_ref[slot_row[(first + b) * capacity + k]]
        return 0

    lax.fori_loop(0, capacity, one, 0)


def pack(queries, slot_row, pieces, capacity, *before):
    shapes = [
        jax.ShapeDtypeStruct((blocks * capacity,) + queries.shape[1:], BF) for _, blocks in pieces
    ]
    whole = lambda array: pl.BlockSpec(array.shape, lambda i, s: (0, 0, 0, 0))
    packed = pl.pallas_call(
        functools.partial(pack_kernel, pieces, capacity),
        out_shape=shapes,
        grid_spec=pltpu.PrefetchScalarGridSpec(
            num_scalar_prefetch=1,
            grid=(1,),
            in_specs=[whole(queries)] + [pl.BlockSpec(memory_space=pl.ANY)] * len(before),
            out_specs=[whole(shape) for shape in shapes],
        ),
        compiler_params=params(16),
        cost_estimate=SMALL,
        name="pack_queries",
    )(slot_row, queries, *before)
    return [x.reshape(-1, x.shape[-1]) for x in packed]


def split_kernel(heads, steps, k_hbm, v_hbm, kt_ref, vs_ref, buffer, wide, sems):
    step = pl.program_id(0)
    each = buffer.shape[2]
    count = each // heads

    def copy(source, which, part):
        rows = source.at[pl.ds(part * each, each), :]
        return pltpu.make_async_copy(rows, buffer.at[which, part], sems.at[which, part])

    @pl.when(step == 0)
    def _():
        for part in range(steps):
            copy(k_hbm, 0, part).start()
            copy(v_hbm, 1, part).start()

    for which, source in ((0, k_hbm), (1, v_hbm)):
        copy(source, which, step).wait()
        wide[...] = buffer[which, step].astype(F32)
        for a in range(heads):
            part = wide[pl.ds(a, count, stride=heads), :]
            if which == 0:
                kt_ref[a] = part.T.astype(BF)
            else:
                vs_ref[a] = part.astype(BF)


def split_heads(keys, values):
    count, heads, dim = keys.shape
    steps = 4
    each = count // steps
    return pl.pallas_call(
        functools.partial(split_kernel, heads, steps),
        out_shape=[
            jax.ShapeDtypeStruct((heads, dim, count), BF),
            jax.ShapeDtypeStruct((heads, count, dim), BF),
        ],
        grid=(steps,),
        in_specs=[pl.BlockSpec(memory_space=pl.ANY)] * 2,
        out_specs=[
            pl.BlockSpec((heads, dim, each), lambda i: (0, 0, i)),
            pl.BlockSpec((heads, each, dim), lambda i: (0, i, 0)),
        ],
        scratch_shapes=[
            pltpu.VMEM((2, steps, each * heads, dim), BF),
            pltpu.VMEM((each * heads, dim), F32),
            pltpu.SemaphoreType.DMA((2, steps)),
        ],
        compiler_params=params(48),
        cost_estimate=SMALL,
        name="split_heads",
    )(keys.reshape(count * heads, dim), values.reshape(count * heads, dim))


def attend_kernel(capacity, per, group, block, chunk, count, outs, at_ref, *refs):
    del at_ref
    q_refs, (k_ref, v_ref) = refs[:count], refs[count : count + 2]
    o_refs, (acc_ref, weight_ref) = refs[-2 - outs : -2], refs[-2:]
    heads, dim, keys = k_ref.shape
    total = rows = capacity * per
    each = rows // heads
    scale = dim**-0.5 * math.log2(math.e)
    ones = jnp.ones((block, dim), BF)
    turn = pl.program_id(0)
    grid = q_refs[0][...].astype(F32)
    for t in range(1, count):
        grid = jnp.where(turn == t, q_refs[t][...].astype(F32), grid)
    grid = grid.reshape(total // (heads * group), heads, group, dim)
    queries = [grid[:, a].reshape(each, dim).astype(BF) for a in range(heads)]

    def scores(a, j):
        part = k_ref[a, :, pl.ds(j * block, block)]
        return jnp.dot(queries[a], part, preferred_element_type=F32)

    def values(a, j):
        return jnp.concatenate([v_ref[a, pl.ds(j * block, block), :], ones], axis=1)

    def natural(parts):
        split = [x.reshape(each // group, 1, group, dim) for x in parts]
        return jnp.concatenate(split, axis=1).reshape(total, dim)

    def finish(shifts):
        sums = [acc_ref[a, :, dim:] for a in range(heads)]
        out = natural([acc_ref[a, :, :dim] / sums[a] for a in range(heads)]).astype(BF)
        log_sum = natural([shifts[a] + jnp.log2(sums[a]) for a in range(heads)])
        high = log_sum.astype(BF).astype(F32)
        lane = lax.broadcasted_iota(jnp.int32, (total, dim), 1)
        row = lax.broadcasted_iota(jnp.int32, (total, dim), 0)
        term = jnp.where(lane < per, high, log_sum - high)
        term = jnp.where((lane % per == row % per) & (lane < 2 * per), term, 0.0).astype(BF)
        slot = lax.broadcasted_iota(jnp.int32, (EXTRA, rows), 0)
        source = lax.broadcasted_iota(jnp.int32, (EXTRA, rows), 1) // per
        pick = jnp.where(source == slot, 1.0, 0.0).astype(BF)
        logs = jnp.dot(pick, term, preferred_element_type=F32).astype(BF)
        for t, o_ref in enumerate(o_refs):

            @pl.when(turn == t)
            def _():
                o_ref[:rows, :] = out
                o_ref[rows:, :] = logs

    turns = keys // block
    steps = block // chunk

    def middle(part):
        weights = jnp.exp2(part - jnp.max(part, axis=1, keepdims=True))
        total = jnp.sum(weights, axis=1, keepdims=True)
        return jnp.sum(weights * part, axis=1, keepdims=True) / total

    def accumulate(a, j):
        slot = (a * turns + j) % 2
        part = jnp.dot(weight_ref[slot], values(a, j), preferred_element_type=F32)
        if j == 0:
            acc_ref[a] = part
        else:
            acc_ref[a] += part

    shifts = []
    before = None
    for a in range(heads):
        for j in range(turns):
            slot = (a * turns + j) % 2
            for c in range(steps):
                first = j * block + c * chunk
                part = jnp.dot(
                    queries[a], k_ref[a, :, first : first + chunk], preferred_element_type=F32
                )
                if first == 0:
                    shifts.append(middle(part[:, :256] * scale))
                weights = jnp.exp2((part * scale - shifts[a]).astype(BF))
                weight_ref[slot, :, c * chunk : (c + 1) * chunk] = weights
            if before is not None:
                accumulate(*before)
            before = (a, j)
    accumulate(*before)
    finish(shifts)
    fits = jnp.max(acc_ref[:, :, dim:]) < LIMIT

    @pl.when(jnp.logical_not(fits))
    def _():
        acc_ref[...] = jnp.zeros_like(acc_ref)
        tops = []
        for a in range(heads):

            def step(j, top):
                part = scores(a, j) * scale
                new = jnp.maximum(top, jnp.max(part, axis=1, keepdims=True))
                weights = jnp.exp2(part - new).astype(BF)
                acc_ref[a] = acc_ref[a] * jnp.exp2(top - new) + jnp.dot(
                    weights, values(a, j), preferred_element_type=F32
                )
                return new

            tops.append(lax.fori_loop(0, turns, step, jnp.full((each, 1), -1e30, F32)))
        finish(tops)


def attend(queries, keys_t, values, at, capacity, per, group, *before):
    dim = queries[0].shape[1]
    heads, keys, _ = values.shape
    rows = capacity * per
    count = len(queries)
    blocks = count if count > 1 else queries[0].shape[0] // rows
    block = min(1024, keys)
    chunk = min(512, block)
    once = lambda array: pl.BlockSpec(
        array.shape, lambda i, s: (0,) * array.ndim, pipeline_mode=pl.Buffered(1)
    )
    place = (lambda i, s: (0, 0)) if count > 1 else (lambda i, s: (s[0] ^ i, 0))
    out = jax.ShapeDtypeStruct((rows + EXTRA, dim), BF)
    return pl.pallas_call(
        functools.partial(attend_kernel, capacity, per, group, block, chunk, count, blocks),
        out_shape=[out] * blocks,
        grid_spec=pltpu.PrefetchScalarGridSpec(
            num_scalar_prefetch=1,
            grid=(blocks,),
            in_specs=[pl.BlockSpec((rows, dim), place)] * count
            + [once(keys_t), once(values)]
            + [pl.BlockSpec(memory_space=pl.ANY)] * len(before),
            out_specs=[pl.BlockSpec(out.shape, lambda i, s: (0, 0))] * blocks,
            scratch_shapes=[
                pltpu.VMEM((heads, rows // heads, 2 * dim), F32),
                pltpu.VMEM((2, rows // heads, block), BF),
            ],
        ),
        compiler_params=params(24),
        cost_estimate=SMALL,
        name="attend_prefix",
    )(at, *queries, keys_t, values, *before)


def visibility(lengths, draft_count, suffix_count):
    position = jnp.arange(suffix_count + draft_count, dtype=jnp.int32)
    draft_pos = jnp.arange(draft_count, dtype=jnp.int32)
    earlier = position[None, None, :] < lengths[:, None, None]
    earlier = earlier & (position[None, None, :] < suffix_count)
    fresh = (position[None, :] >= suffix_count) & (
        position[None, :] - suffix_count <= draft_pos[:, None]
    )
    return earlier | fresh[None, :, :]


def local_attention(query_grid, key_rows, value_rows, visible):
    scale = query_grid.shape[-1] ** (-0.5)
    scores = (
        jnp.einsum("rtagd,rjad->rtagj", query_grid, key_rows, preferred_element_type=F32) * scale
    )
    visible_mask = visible[:, :, None, None, :]
    scores = jnp.where(visible_mask, scores, F32(-1e30))
    top = jnp.max(scores, axis=-1)
    exponent = jnp.where(visible_mask, jnp.exp(scores - top[..., None]), F32(0.0))
    denominator = jnp.sum(exponent, axis=-1)
    summed = jnp.einsum(
        "rtagj,rjad->rtagd", exponent.astype(BF), value_rows, preferred_element_type=F32
    )
    return summed / denominator[..., None], (top + jnp.log(denominator)) * F32(math.log2(math.e))


def fetch(weight, shards, buffer, sems, width):
    count, _, block = buffer.shape
    each = width // block
    copies = []
    for n in range(count):
        column = pl.multiple_of(shards[n // each] * width + (n % each) * block, block)
        source = weight.at[:, pl.ds(column, block)]
        copies.append(pltpu.make_async_copy(source, buffer.at[n], sems.at[n]))
        copies[-1].start()
    return copies


def multiply(att, copies, buffer, outs):
    block = buffer.shape[2]
    each = len(copies) // len(outs)
    rows = att[...]
    for n, copy in enumerate(copies):
        copy.wait()
        product = jnp.dot(rows, buffer[n], preferred_element_type=F32).astype(BF)
        outs[n // each][:, n % each * block : (n % each + 1) * block] = product


def join_kernel(capacity, count, base, shares, order, target, shards, *refs):
    received, (local, local_log, weight) = refs[:count], refs[count : count + 3]
    att, *outs = refs[-8 - shares - 1 : -8]
    blocks, block_logs, part, mine, logs, spread, buffer, sems = refs[-8:]
    copies = fetch(weight, shards, buffer, sems, outs[0].shape[1])
    rows, per, dim = part.shape
    held = capacity * per
    heads = att.shape[1] // dim
    draft = per // heads
    done = 0
    for array in received:
        for first in range(0, array.shape[0], held + EXTRA):
            values = array[first : first + held, :].astype(F32)
            blocks[done * capacity : (done + 1) * capacity] = values.reshape(capacity, per, dim)
            last = array[first + held : first + held + EXTRA, :].astype(F32)
            block_logs[done * EXTRA : (done + 1) * EXTRA] = last
            done += 1

    def gather(i, _):
        at = order[base + i]
        slot = target[base + i]
        part[i] = blocks[slot]
        mine[i] = local[at].astype(F32)
        place = (slot // capacity) * EXTRA + slot % capacity
        logs[0, pl.ds(i, 1), :] = block_logs[pl.ds(place, 1), :]
        logs[1, pl.ds(i, 1), :] = local_log[pl.ds(at, 1), :]
        return 0

    lax.fori_loop(0, rows, gather, 0)
    lane = lax.broadcasted_iota(jnp.int32, (rows, dim), 1)
    first = logs[0] + pltpu.roll(logs[0], dim - per, axis=1)
    share = 1.0 / (1.0 + jnp.exp2(logs[1] - first))
    high = share.astype(BF).astype(F32)
    low = pltpu.roll(share - high, per, axis=1)
    logs[0] = jnp.where(lane < per, high, jnp.where(lane < 2 * per, low, 0.0))
    diagonal = lax.broadcasted_iota(jnp.int32, (per, dim), 1) % per
    diagonal = diagonal == lax.broadcasted_iota(jnp.int32, (per, dim), 0)

    def widen(i, _):
        row = logs[0, pl.ds(i, 1), :]
        spread[i] = jnp.where(diagonal, row, 0.0).astype(BF)
        return 0

    lax.fori_loop(0, rows, widen, 0)
    ones = jnp.ones((dim, dim), BF)
    shares = jnp.dot(
        spread[...].reshape(rows * per, dim), ones, preferred_element_type=F32
    ).reshape(rows, per, dim)
    part[...] = mine[...] + shares * (part[...] - mine[...])
    flat = part.reshape(rows * per, dim)
    for h in range(heads):
        head = flat[pl.ds(h, rows * draft, stride=heads), :]
        att[:, h * dim : (h + 1) * dim] = head.astype(BF)


    multiply(att, copies, buffer, outs)


def join(
    received, local, local_log, order, target, heads, base, rows, capacity, weight, shards, width, *before
):
    count = len(received)
    per, dim = local.shape[1:]
    blocks = sum(array.shape[0] for array in received) // (capacity * per + EXTRA)
    shares = shards.shape[0]
    lines = rows * per // heads
    block = min(256, width)
    whole = lambda array: pl.BlockSpec(array.shape, lambda n, *_: (0,) * array.ndim)
    att = jax.ShapeDtypeStruct((lines, heads * dim), BF)
    out = jax.ShapeDtypeStruct((lines, width), BF)
    return pl.pallas_call(
        functools.partial(join_kernel, capacity, count, base, shares),
        out_shape=[att] + [out] * shares,
        grid_spec=pltpu.PrefetchScalarGridSpec(
            num_scalar_prefetch=3,
            grid=(1,),
            in_specs=[whole(array) for array in received]
            + [whole(local), whole(local_log)]
            + [pl.BlockSpec(memory_space=pl.ANY)] * (1 + len(before)),
            out_specs=[whole(att)] + [whole(out)] * shares,
            scratch_shapes=[
                pltpu.VMEM((blocks * capacity, per, dim), F32),
                pltpu.VMEM((blocks * EXTRA, dim), F32),
                pltpu.VMEM((rows, per, dim), F32),
                pltpu.VMEM((rows, per, dim), F32),
                pltpu.VMEM((2, rows, dim), F32),
                pltpu.VMEM((rows, per, dim), BF),
                pltpu.VMEM((shares * width // block, heads * dim, block), BF),
                pltpu.SemaphoreType.DMA((shares * width // block,)),
            ],
        ),
        compiler_params=params(48),
        cost_estimate=SMALL,
        name="join_project",
    )(order, target, shards, *received, local, local_log, weight, *before)


def project_kernel(shares, shards, att, weight, *refs):
    outs, (buffer, sems) = refs[-2 - shares : -2], refs[-2:]
    multiply(att, fetch(weight, shards, buffer, sems, outs[0].shape[1]), buffer, outs)


def project(att, weight, shards, width, *before):
    rows, depth = att.shape
    shares = shards.shape[0]
    block = min(256, width)
    out = jax.ShapeDtypeStruct((rows, width), BF)
    whole = lambda array: pl.BlockSpec(array.shape, lambda n, *_: (0,) * array.ndim)
    return pl.pallas_call(
        functools.partial(project_kernel, shares),
        out_shape=[out] * shares,
        grid_spec=pltpu.PrefetchScalarGridSpec(
            num_scalar_prefetch=1,
            grid=(1,),
            in_specs=[whole(att)] + [pl.BlockSpec(memory_space=pl.ANY)] * (1 + len(before)),
            out_specs=[whole(out)] * shares,
            scratch_shapes=[
                pltpu.VMEM((shares * width // block, depth, block), BF),
                pltpu.SemaphoreType.DMA((shares * width // block,)),
            ],
        ),
        compiler_params=params(48),
        cost_estimate=SMALL,
        name="project",
    )(shards, att, weight, *before)


def project_sum(join_with, weight, shards, split, before):
    size = lax.axis_size("tensor")
    chips = size // 2
    width = weight.shape[1] // size
    order = list(range(1, chips)) + [0]
    with_join = 1 if split else len(shards)
    att, *products = join_with(jnp.concatenate(shards[:with_join]), width)
    got = []
    for k, d in enumerate(order):
        while len(products) < 2 * k + 2:
            waits = before if d == 0 else []
            wanted = shards[len(products) :] if d == 0 else shards[len(products) : len(products) + 1]
            products += project(att, weight, jnp.concatenate(wanted), width, *waits)
        send, keep = products[2 * k : 2 * k + 2]
        there = lax.ppermute(send, "tensor", [(i, i ^ 1) for i in range(size)])
        if d:
            total = (keep.astype(F32) + there.astype(F32)).astype(BF)
            before = list(before) + [total]
            got.append(lax.ppermute(total, "tensor", [(i, i ^ (2 * d)) for i in range(size)]))
    total = keep.astype(F32)
    for term in got:
        total = total + term.astype(F32)
    return [total, there], [total], keep


def arrange_kernel(counts, place_ref, *refs):
    out_ref = refs[-1]
    rows, draft, _ = out_ref.shape
    halves, start = [], 0
    for count in counts:
        total = refs[start][...]
        for term in refs[start + 1 : start + count]:
            total = total + term[...].astype(F32)
        halves.append(total.astype(BF))
        start += count
    values = jnp.concatenate(halves, axis=0)
    size = rows * draft
    pick = lax.broadcasted_iota(jnp.int32, (size, size), 1) == place_ref[...]
    result = jnp.dot(
        jnp.where(pick, 1.0, 0.0).astype(BF), values, preferred_element_type=F32
    )
    for r in range(rows):
        out_ref[r] = result[r * draft : (r + 1) * draft].astype(BF)


def arrange(halves, place, rows, draft):
    width = halves[0][0].shape[1]
    index = (place[:, None] * draft + jnp.arange(draft, dtype=jnp.int32)[None, :]).reshape(-1, 1)
    return pl.pallas_call(
        functools.partial(arrange_kernel, [len(half) for half in halves]),
        out_shape=jax.ShapeDtypeStruct((rows, draft, width), BF),
        compiler_params=params(20),
        cost_estimate=SMALL,
        name="arrange_rows",
    )(index, *[term for half in halves for term in half])


def exchange(x):
    size = lax.axis_size("dp")
    groups = [list(range(size // 2)), list(range(size // 2, size))]
    return lax.all_to_all(
        x, "dp", split_axis=0, concat_axis=0, axis_index_groups=groups, tiled=True
    )


def hop(x, shift):
    size = lax.axis_size("dp")
    return lax.ppermute(x, "dp", [(i, i ^ shift) for i in range(size)])


def body(
    queries,
    draft_keys,
    draft_values,
    suffix_keys,
    suffix_values,
    suffix_len,
    prefix_keys,
    prefix_values,
    row_prefix,
    prefix_slot,
    out_weight,
):
    row_count, draft, query_heads, dim = queries.shape
    heads = draft_keys.shape[2]
    group = query_heads // heads
    per = draft * query_heads
    suffix_count = suffix_keys.shape[1]
    peers = lax.axis_size("dp")
    capacity = 2 * row_count // peers
    own = lax.axis_index("tensor").astype(jnp.int32)
    me = lax.axis_index("dp").astype(jnp.int32)

    size = lax.axis_size("tensor")
    half = peers // 2
    here = (me % half).reshape(1)
    distances = list(range(1, size // 2)) + [0]
    shards = [(own ^ (2 * d + other)).reshape(1) for d in distances for other in (1, 0)]

    slot_row, place, order, target = route(row_prefix, prefix_slot, me, peers, capacity)
    lead = half // 2
    first = pack(queries, slot_row, [(half + d, 1) for d in range(lead)], capacity, here, *shards)
    near, *late = pack(
        queries,
        slot_row,
        [(0, half)] + [(half + d, 1) for d in range(lead, half)],
        capacity,
        first[0],
    )
    far = [hop(x, half + d) for d, x in enumerate(first + late)]
    near = exchange(near)

    keys_t, values = split_heads(prefix_keys[0], prefix_values[0])
    zero = jnp.zeros((1,), jnp.int32)
    back, before = [None] * peers, []
    for batch in [range(half, half + lead), range(half)] + [[d] for d in range(half + lead, peers)]:
        arrays = [near] if batch[0] == 0 else [far[d - half] for d in batch]
        if batch[-1] == peers - 1:
            before = list(before) + back[half : half + lead]
        at = here if batch[0] == 0 else zero
        results = attend(arrays, keys_t, values, at, capacity, per, group, *before)
        before = results[:1]
        for d, result in zip(batch, results):
            back[d] = hop(result, d) if d else result

    query_grid = queries.reshape(row_count, draft, heads, group, dim)
    all_keys = jnp.concatenate([suffix_keys, draft_keys], axis=1)
    all_values = jnp.concatenate([suffix_values, draft_values], axis=1)
    visible = visibility(suffix_len, draft, suffix_count)
    local, local_log = local_attention(query_grid, all_keys, all_values, visible)
    local = local.reshape(row_count, per, dim).astype(BF)
    local_log = jnp.pad(local_log.reshape(row_count, per), ((0, 0), (0, dim - per)))

    rows = row_count // 2
    early = peers - rows // capacity
    outs, waits = [], []
    for base in (0, rows):
        received = back if base else back[:early]

        def join_with(shards, width):
            return join(
                received,
                local,
                local_log,
                order,
                target,
                query_heads,
                base,
                rows,
                capacity,
                out_weight,
                shards,
                width,
                *before,
            )

        terms, waits, product = project_sum(join_with, out_weight, shards, base > 0, waits)
        before = [product]
        outs.append(terms)
    return arrange(outs, place, row_count, draft)


def solution(mesh):
    placed = (
        P("dp", None, "tensor", None),
        P("dp", None, "tensor", None),
        P("dp", None, "tensor", None),
        P("dp", None, "tensor", None),
        P("dp", None, "tensor", None),
        P("dp"),
        P("dp", None, "tensor", None),
        P("dp", None, "tensor", None),
        P("dp", None),
        P(),
        P("tensor", None),
    )
    return jax.shard_map(
        body, mesh=mesh, in_specs=placed, out_specs=P("dp", None, "tensor"), check_vma=False
    )
```
